32 devices in a mesh: stream: 8 (over y, x, core), blk: 4 (over z).
Axes of the slice: x: 2, y: 2, z: 4, core: 2. Of those that a mesh axis runs over, the one named last changes fastest.
Arguments:
- segment: bfloat16 [8, 512, 1024], P('stream', 'blk'), may hold values from -6 to 6
- memory: bfloat16 [8, 512, 1024], P('stream', 'blk'), may hold values from -6 to 6
- compressed: bfloat16 [8, 512, 1024], P('stream', 'blk'), may hold values from -6 to 6
- document_labels: int32 [8, 3, 512], P('stream'), may hold values from 0 to 3, as said below
- memory_filled_count: int32 [8], P('stream'), may hold values from 0 to 1024, as said below
- norm_gain: float32 [1024], replicated, may hold values from 0.1 to 1.9
- w_query: bfloat16 [1024, 1024], replicated, may hold values from -0.1875 to 0.1875
- w_key: bfloat16 [1024, 1024], replicated, may hold values from -0.1875 to 0.1875
- w_value: bfloat16 [1024, 1024], replicated, may hold values from -0.1875 to 0.1875
- w_output: bfloat16 [1024, 1024], replicated, may hold values from -0.75 to 0.75
- ffn_gain: float32 [1024], replicated, may hold values from 0.1 to 1.9
- w_expand: bfloat16 [1024, 4096], replicated, may hold values from -0.1875 to 0.1875
- w_reduce: bfloat16 [4096, 1024], replicated, may hold values from -0.1875 to 0.1875
- w_compress: bfloat16 [2048, 1024], replicated, may hold values from -0.125 to 0.125
- result_cotangent: bfloat16 [8, 512, 1024], P('stream', 'blk'), may hold values from -6 to 6
- compressed_cotangent: bfloat16 [8, 256, 1024], P('stream', 'blk'), may hold values from -6 to 6
Outputs:
- result: bfloat16 [8, 512, 1024], P('stream', 'blk')
- new_compressed: bfloat16 [8, 256, 1024], P('stream', 'blk')
- grad_segment: bfloat16 [8, 512, 1024], P('stream', 'blk')
- grad_norm_gain: float32 [1024], P(('stream', 'blk'))
- grad_query: float32 [1024, 1024], P(('stream', 'blk'))
- grad_key: float32 [1024, 1024], P(('stream', 'blk'))
- grad_value: float32 [1024, 1024], P(('stream', 'blk'))
- grad_output: float32 [1024, 1024], P(('stream', 'blk'))
- grad_ffn_gain: float32 [1024], P(('stream', 'blk'))
- grad_expand: float32 [1024, 4096], P(('stream', 'blk'))
- grad_reduce: float32 [4096, 1024], P(None, ('stream', 'blk'))
- grad_compress: float32 [2048, 1024], P(('stream', 'blk'))
The draws below stay inside these ranges and needn't reach their ends.
Inputs may be any that keep to these rules, and one draw needn't show every extreme that they name: `document_labels`: per stream the ids never fall along the compressed slots, then the memory slots, then the segment positions. `memory_filled_count`: counts the most recent slots of compressed memory and memory taken together.
All inputs are finite; a program needn't handle non-finite values.
Results may differ from the reference program's by a relative error of at most 0.014.
Values may be sent and summed in bfloat16 or wider, within the bound.
No kernel may reach another device: no remote copies, remote signals or barrier semaphores. Data moves between devices by JAX's collectives and lax.ppermute only.
A program may use at most 256 MiB of HBM per device.

```python
import jax
import jax.numpy as jnp
from jax import lax

D = 1024
H = 8
HD = 128
FF = 4096
SEG = 512
MEM = 512
CMEM = 512
RATE = 2
STREAMS = 8
N_BLK = 4


def chosen_stream(key):
    return jax.random.randint(jax.random.fold_in(key, 7), (), 0, STREAMS)


def draw_document_labels(key, part):
    picked = chosen_stream(key)
    key = jax.random.fold_in(key, 11)
    cuts = jax.random.randint(key, (STREAMS, 3), 1, 3 * SEG)
    single = jnp.arange(STREAMS, dtype=jnp.int32) == picked
    cuts = jnp.where(single[:, None], 3 * SEG, cuts)
    places = jnp.arange(3 * SEG, dtype=jnp.int32)
    counted = jnp.sum((places[None, :, None] >= cuts[:, None, :]).astype(jnp.int32), axis=2)
    return counted.reshape(STREAMS, 3, SEG).astype(jnp.int32)


def draw_memory_filled_count(key, part):
    picked = chosen_stream(key)
    key = jax.random.fold_in(key, 13)
    counts = jax.random.randint(key, (STREAMS,), 0, MEM + CMEM + 1)
    single = jnp.arange(STREAMS, dtype=jnp.int32) == picked
    return jnp.where(single, MEM + CMEM, counts).astype(jnp.int32)


def block_scale(stream_key, dims, split, smallest, high):
    def one(axis_at, parts):
        heights = jax.random.uniform(jax.random.fold_in(jax.random.fold_in(stream_key, 6), axis_at), (parts,), jnp.float32, smallest / len(split), high / len(split))
        return jnp.repeat(jnp.exp(heights), dims[axis_at] // parts).reshape((-1,) + (1,) * (len(dims) - axis_at - 1))

    factor_of = one(*split[0])
    for cut in split[1:]:
        factor_of = factor_of * one(*cut)
    return factor_of


def noise(own_key, extent, width, bound, cuts=(), kind=jnp.bfloat16):
    factor_of = block_scale(own_key, extent, cuts, -0.22, 0.18) if cuts else 1.0
    values = jax.random.normal(own_key, extent, jnp.float32) * width * factor_of
    return jnp.minimum(jnp.maximum(values, -bound), bound).astype(kind)


def setup_inputs(seed: int = 0) -> dict:
    streams_of = jax.random.split(jax.random.key(seed), 17)
    segment = noise(streams_of[0], (STREAMS, SEG, D), 1.0, 6.0, ((0, 8), (1, 4)))
    memory = noise(streams_of[1], (STREAMS, MEM, D), 1.0, 6.0, ((0, 8), (1, 4)))
    compressed = noise(streams_of[2], (STREAMS, CMEM, D), 1.0, 6.0, ((0, 8), (1, 4)))
    document_labels = draw_document_labels(jax.random.fold_in(streams_of[16], 71), 0)
    memory_filled_count = draw_memory_filled_count(jax.random.fold_in(streams_of[16], 71), 0)
    norm_gain = jnp.clip(1.0 + 0.18 * jax.random.normal(streams_of[5], (D,), jnp.float32), 0.1, 1.9)
    w_query = noise(streams_of[6], (D, D), D ** -0.5, 0.1875)
    w_key = noise(streams_of[7], (D, D), D ** -0.5, 0.1875)
    w_value = noise(streams_of[8], (D, D), D ** -0.5, 0.1875)
    w_output = noise(streams_of[9], (D, D), (D // 16) ** -0.5, 0.75)
    ffn_gain = jnp.clip(1.0 + 0.18 * jax.random.normal(streams_of[10], (D,), jnp.float32), 0.1, 1.9)
    w_expand = noise(streams_of[11], (D, FF), D ** -0.5, 0.1875)
    w_reduce = noise(streams_of[12], (FF, D), (FF // 4) ** -0.5, 0.1875)
    w_compress = noise(streams_of[13], (RATE * D, D), (RATE * D) ** -0.5, 0.125)
    result_cotangent = noise(streams_of[14], (STREAMS, SEG, D), 1.0, 6.0, ((0, 8), (1, 4)))
    compressed_cotangent = noise(streams_of[15], (STREAMS, MEM // RATE, D), 1.0, 6.0, ((0, 8), (1, 4)))
    return {"segment": segment, "memory": memory, "compressed": compressed, "document_labels": document_labels, "memory_filled_count": memory_filled_count, "norm_gain": norm_gain, "w_query": w_query, "w_key": w_key, "w_value": w_value, "w_output": w_output, "ffn_gain": ffn_gain, "w_expand": w_expand, "w_reduce": w_reduce, "w_compress": w_compress, "result_cotangent": result_cotangent, "compressed_cotangent": compressed_cotangent}


@jax.custom_vjp
def low(v):
    return lax.optimization_barrier(v.astype(jnp.bfloat16)).astype(jnp.float32)

@jax.custom_vjp
def low_back(v):
    return v

def low_keep(v):
    return (low(v), None)

def low_pass(kept, grad):
    return (grad,)

def back_keep(v):
    return (v, None)

def back_low(kept, grad):
    return (low(grad),)
low.defvjp(low_keep, low_pass)
low_back.defvjp(back_keep, back_low)
epsilon = 1e-05
masked_score = -1e+30

def layer_norm(rows_in, gain):
    center = lax.optimization_barrier(jnp.mean(rows_in, axis=-1, keepdims=True))
    offset = rows_in - center
    spread = lax.optimization_barrier(jnp.mean(offset * offset, axis=-1, keepdims=True))
    return offset * lax.rsqrt(spread + epsilon) * gain

def highest(left, right):
    return jnp.dot(left, right, precision=lax.Precision.HIGHEST)

def stream_forward(params, segment, memory, compressed, document_labels, memory_filled_count):
    norm_gain, w_query, w_key, w_value, w_output, ffn_gain, w_expand, w_reduce, w_compress = params
    stacked = jnp.concatenate([compressed, memory, segment], axis=0)
    normed = low(layer_norm(stacked, norm_gain))
    queries = low(low_back(highest(normed[2 * SEG:], w_query))).reshape(SEG, H, HD)
    keys = low(low_back(highest(normed, w_key))).reshape(3 * SEG, H, HD)
    values = low(low_back(highest(normed, w_value))).reshape(3 * SEG, H, HD)
    key_slot = jnp.arange(3 * SEG, dtype=jnp.int32)
    key_kind = key_slot // SEG
    key_pos = key_slot % SEG
    query_pos = jnp.arange(SEG, dtype=jnp.int32)
    in_memory = (key_slot >= CMEM + MEM - memory_filled_count)[None, :]
    causal = key_pos[None, :] <= query_pos[:, None]
    visible = jnp.where((key_kind < 2)[None, :], in_memory, causal)
    flat_docs = document_labels.reshape(3 * SEG)
    allowed = visible & (flat_docs[None, :] == document_labels[2][:, None])
    query_block = SEG // N_BLK
    pieces = []
    for block in range(N_BLK):
        block_keys = low_back(keys)
        block_values = low_back(values)
        lower = block * query_block
        upper = lower + query_block
        raw_scores = jnp.einsum('qhd,khd->hqk', queries[lower:upper], block_keys, precision=lax.Precision.HIGHEST) * HD ** (-0.5)
        scores = jnp.where(allowed[lower:upper][None], low_back(raw_scores), masked_score)
        row_top = lax.optimization_barrier(jnp.max(scores, axis=-1, keepdims=True))
        weights = jnp.exp(scores - row_top)
        probs = low(weights / lax.optimization_barrier(jnp.sum(weights, axis=-1, keepdims=True)))
        pieces.append(jnp.einsum('hqk,khd->qhd', probs, block_values, precision=lax.Precision.HIGHEST))
    attended = jnp.concatenate(pieces, axis=0).reshape(SEG, D)
    attended = low(low_back(attended))
    middle = segment + low_back(highest(attended, w_output))
    normed_ffn = low(layer_norm(middle, ffn_gain))
    hidden = low_back(highest(normed_ffn, w_expand))
    activated = low(jax.nn.gelu(hidden, approximate=False))
    result = middle + low_back(highest(activated, w_reduce))
    compact = highest(memory.reshape(MEM // RATE, RATE * D), w_compress)
    return (result, compact)

def reference(segment, memory, compressed, document_labels, memory_filled_count, norm_gain, w_query, w_key, w_value, w_output, ffn_gain, w_expand, w_reduce, w_compress, result_cotangent, compressed_cotangent):
    params = tuple((weight.astype(jnp.float32) for weight in (norm_gain, w_query, w_key, w_value, w_output, ffn_gain, w_expand, w_reduce, w_compress)))

    def carry_update(totals, item):
        seg_in, mem_in, comp_in, docs_in, valid_in, out_grad, comp_grad = item

        def forward(param_in, seg_value):
            return stream_forward(param_in, seg_value, mem_in.astype(jnp.float32), comp_in.astype(jnp.float32), docs_in, valid_in)
        outputs, pullback = jax.vjp(forward, params, seg_in.astype(jnp.float32))
        param_grads, seg_grad = pullback((out_grad.astype(jnp.float32), comp_grad.astype(jnp.float32)))
        totals = jax.tree.map(jnp.add, totals, param_grads)
        return (totals, (outputs[0].astype(jnp.bfloat16), outputs[1].astype(jnp.bfloat16), seg_grad.astype(jnp.bfloat16)))
    initial_carry = tuple((jnp.zeros_like(weight) for weight in params))
    running_totals, (step_results, compacted_slots, segment_gradients) = lax.scan(carry_update, initial_carry, (segment, memory, compressed, document_labels, memory_filled_count, result_cotangent, compressed_cotangent))
    return (step_results, compacted_slots, segment_gradients, running_totals[0], running_totals[1], running_totals[2], running_totals[3], running_totals[4], running_totals[5], running_totals[6], running_totals[7], running_totals[8])
```

```python
import functools

import jax
import jax.numpy as jnp
from jax import lax
from jax.experimental import pallas as pl
from jax.experimental.pallas import tpu as pltpu
from jax.sharding import PartitionSpec as P

HD = 128
RATE = 2
PLANE = 8

epsilon = 1e-05
masked_score = -1e30
hidden_slot = 1 << 30

f32 = jnp.float32
bf16 = jnp.bfloat16
MIB = 1 << 20


def dot(left, right, contract=((1,), (0,))):
    return lax.dot_general(left, right, (contract, ((), ())), preferred_element_type=f32)


def standardized(rows):
    offset = rows - jnp.mean(rows, axis=-1, keepdims=True)
    scale = lax.rsqrt(jnp.mean(offset * offset, axis=-1, keepdims=True) + epsilon)
    return offset * scale, scale


def norm_input_gradient(e, gain, unit, scale):
    eg = e * gain
    return scale * (
        eg
        - jnp.mean(eg, axis=-1, keepdims=True)
        - unit * jnp.mean(eg * unit, axis=-1, keepdims=True)
    )


def project_kernel(rows_ref, gain_ref, wq_ref, wk_ref, wv_ref, normed_ref, q_ref, k_ref, v_ref):
    @pl.when(pl.program_id(0) == 0)
    def _():
        unit, _ = standardized(rows_ref[...].astype(f32))
        normed_ref[...] = (unit * gain_ref[...]).astype(bf16)

    normed = normed_ref[...]
    first_query = normed.shape[0] - q_ref.shape[0]
    q_ref[...] = dot(normed[first_query:], wq_ref[...]).astype(bf16)
    k_ref[...] = dot(normed, wk_ref[...]).astype(bf16)
    v_ref[...] = dot(normed, wv_ref[...]).astype(bf16)


def project(rows, gain, w_query, w_key, w_value):
    count, width = rows.shape
    out_width = w_key.shape[1]
    tile = 256
    whole = lambda i: (0, 0)
    column = lambda i: (0, i)
    return pl.pallas_call(
        project_kernel,
        grid=(out_width // tile,),
        in_specs=[
            pl.BlockSpec((count, width), whole),
            pl.BlockSpec((1, width), whole),
            pl.BlockSpec((width, tile), column),
            pl.BlockSpec((width, tile), column),
            pl.BlockSpec((width, tile), column),
        ],
        out_specs=[
            pl.BlockSpec((count, width), whole),
            pl.BlockSpec((count // 3, tile), column),
            pl.BlockSpec((count, tile), column),
            pl.BlockSpec((count, tile), column),
        ],
        out_shape=[
            jax.ShapeDtypeStruct((count, width), bf16),
            jax.ShapeDtypeStruct((count // 3, out_width), bf16),
            jax.ShapeDtypeStruct((count, out_width), bf16),
            jax.ShapeDtypeStruct((count, out_width), bf16),
        ],
        compiler_params=pltpu.CompilerParams(vmem_limit_bytes=20 * MIB),
        cost_estimate=pl.CostEstimate(
            flops=2 * count * width * out_width * 7 // 3,
            bytes_accessed=6 * width * out_width + 8 * count * width,
            transcendentals=0,
        ),
        name="project",
    )(rows, gain, w_query, w_key, w_value)


def attend_kernel(slots, *refs):
    q_ref = refs[0]
    k_refs = refs[1 : 1 + slots]
    v_refs = refs[1 + slots : 1 + 2 * slots]
    qdoc_ref, qpos_ref, kdoc_ref, kpos_ref, out_ref = refs[1 + 2 * slots :]
    scale = HD ** (-0.5)
    q = q_ref[...]
    scores = []
    for slot in range(slots):
        raw = dot(q, k_refs[slot][...], ((1,), (1,))) * scale
        allowed = (kdoc_ref[slot : slot + 1, :] == qdoc_ref[...]) & (
            kpos_ref[slot : slot + 1, :] <= qpos_ref[...]
        )
        scores.append(jnp.where(allowed, raw, masked_score))
    top = functools.reduce(jnp.maximum, [jnp.max(s, axis=-1, keepdims=True) for s in scores])
    weights = [jnp.exp(s - top) for s in scores]
    total = sum(jnp.sum(w, axis=-1, keepdims=True) for w in weights)
    inverse = 1.0 / total
    out = sum(
        dot((weights[slot] * inverse).astype(bf16), v_refs[slot][...]) for slot in range(slots)
    )
    out_ref[...] = out.astype(bf16)


def attend(query, keys, values, qdoc, qpos, kdoc, kpos):
    slots = len(keys)
    rows, width = query.shape
    key_rows = keys[0].shape[0]
    column = lambda h: (0, h)
    whole = lambda h: (0, 0)
    return pl.pallas_call(
        functools.partial(attend_kernel, slots),
        grid=(width // HD,),
        in_specs=[pl.BlockSpec((rows, HD), column)]
        + [pl.BlockSpec((key_rows, HD), column)] * (2 * slots)
        + [pl.BlockSpec((rows, 1), whole)] * 2
        + [pl.BlockSpec((slots, key_rows), whole)] * 2,
        out_specs=pl.BlockSpec((rows, HD), column),
        out_shape=jax.ShapeDtypeStruct((rows, width), bf16),
        compiler_params=pltpu.CompilerParams(vmem_limit_bytes=24 * MIB),
        cost_estimate=pl.CostEstimate(
            flops=4 * rows * slots * key_rows * width,
            bytes_accessed=4 * slots * key_rows * width,
            transcendentals=rows * slots * key_rows * (width // HD),
        ),
        name="attend",
    )(query, *keys, *values, qdoc, qpos, kdoc, kpos)


def middle_kernel(
    place_ref,
    att_ref,
    seg_ref,
    wo_ref,
    gain_ref,
    we_ref,
    wr_ref,
    cot_ref,
    result_ref,
    normed_ref,
    act_ref,
    dh_ref,
    dmid_ref,
    branch_ref,
    datt_ref,
    unit_ref,
    scale_ref,
    res_acc,
    dn_acc,
):
    step = pl.program_id(0)

    @pl.when(step == 0)
    def _():
        middle = seg_ref[...].astype(f32) + dot(att_ref[...], wo_ref[...])
        unit, scale = standardized(middle)
        unit_ref[...] = unit
        scale_ref[...] = scale
        normed_ref[...] = (unit * gain_ref[...]).astype(bf16)
        res_acc[...] = middle
        dn_acc[...] = jnp.zeros_like(dn_acc)

    hidden = dot(normed_ref[...], we_ref[...])
    d_act = dot(cot_ref[...], wr_ref[...], ((1,), (1,)))
    cdf = 0.5 + 0.5 * lax.erf(hidden * (0.5**0.5))
    density = jnp.exp(hidden * hidden * -0.5) * 0.3989422804014327
    act = (hidden * cdf).astype(bf16)
    dh = (d_act * (cdf + hidden * density)).astype(bf16)
    act_ref[0] = act
    dh_ref[0] = dh
    res_acc[...] += dot(act, wr_ref[...])
    dn_acc[...] += dot(dh, we_ref[...], ((1,), (1,)))

    @pl.when(step == pl.num_programs(0) - 1)
    def _():
        result_ref[...] = res_acc[...].astype(bf16)
        d_mid = cot_ref[...].astype(f32) + norm_input_gradient(
            dn_acc[...], gain_ref[...], unit_ref[...], scale_ref[...]
        )
        dmid_ref[...] = d_mid
        branch = d_mid.astype(bf16)
        branch_ref[...] = branch
        datt_ref[...] = dot(branch, wo_ref[...], ((1,), (1,))).astype(bf16)


def middle_part(place, attended, segment, w_output, gain, w_expand, w_reduce, cotangent):
    rows, width = segment.shape
    hidden = w_expand.shape[1]
    tile = hidden // PLANE
    whole = lambda f, s: (0, 0)
    row_spec = pl.BlockSpec((rows, width), whole)
    slice_spec = pl.BlockSpec((1, rows, tile), lambda f, s: (f ^ s[0], 0, 0))
    return pl.pallas_call(
        middle_kernel,
        grid_spec=pltpu.PrefetchScalarGridSpec(
            num_scalar_prefetch=1,
            grid=(PLANE,),
            in_specs=[
                row_spec,
                row_spec,
                pl.BlockSpec((width, width), whole),
                pl.BlockSpec((1, width), whole),
                pl.BlockSpec((width, tile), lambda f, s: (0, f)),
                pl.BlockSpec((tile, width), lambda f, s: (f, 0)),
                row_spec,
            ],
            out_specs=[row_spec, row_spec, slice_spec, slice_spec, row_spec, row_spec, row_spec],
            scratch_shapes=[
                pltpu.VMEM((rows, width), f32),
                pltpu.VMEM((rows, 1), f32),
                pltpu.VMEM((rows, width), f32),
                pltpu.VMEM((rows, width), f32),
            ],
        ),
        out_shape=[
            jax.ShapeDtypeStruct((rows, width), bf16),
            jax.ShapeDtypeStruct((rows, width), bf16),
            jax.ShapeDtypeStruct((PLANE, rows, tile), bf16),
            jax.ShapeDtypeStruct((PLANE, rows, tile), bf16),
            jax.ShapeDtypeStruct((rows, width), f32),
            jax.ShapeDtypeStruct((rows, width), bf16),
            jax.ShapeDtypeStruct((rows, width), bf16),
        ],
        compiler_params=pltpu.CompilerParams(vmem_limit_bytes=28 * MIB),
        cost_estimate=pl.CostEstimate(
            flops=2 * rows * width * (4 * hidden + 2 * width),
            bytes_accessed=4 * width * hidden + 2 * width * width,
            transcendentals=2 * rows * hidden,
        ),
        name="middle",
    )(place, attended, segment, w_output, gain, w_expand, w_reduce, cotangent)


def attend_back_kernel(slots, *refs):
    take = iter(refs[1:])
    q_refs = [next(take) for _ in range(slots)]
    g_refs = [next(take) for _ in range(slots)]
    k_refs = [next(take) for _ in range(slots)]
    v_refs = [next(take) for _ in range(slots)]
    qdoc_ref, qpos_ref, kdoc_ref, kpos_ref = (next(take) for _ in range(4))
    dq_ref, dk_ref, dv_ref = (next(take) for _ in range(3))
    scale = HD ** (-0.5)
    rows = q_refs[0].shape[0]
    dk = [None] * slots
    dv = [None] * slots
    for one in range(slots):
        q = q_refs[one][...]
        grad = g_refs[one][...]
        qdoc = qdoc_ref[one * rows : (one + 1) * rows, :]
        qpos = qpos_ref[one * rows : (one + 1) * rows, :]
        scores = []
        for slot in range(slots):
            raw = dot(q, k_refs[slot][...], ((1,), (1,))) * scale
            allowed = (kdoc_ref[slot : slot + 1, :] == qdoc) & (
                kpos_ref[slot : slot + 1, :] <= qpos
            )
            scores.append(jnp.where(allowed, raw, masked_score))
        top = functools.reduce(jnp.maximum, [jnp.max(s, axis=-1, keepdims=True) for s in scores])
        weights = [jnp.exp(s - top) for s in scores]
        inverse = 1.0 / sum(jnp.sum(w, axis=-1, keepdims=True) for w in weights)
        probs = [w * inverse for w in weights]
        d_probs = [dot(grad, v_refs[slot][...], ((1,), (1,))) for slot in range(slots)]
        delta = sum(jnp.sum(p * d, axis=-1, keepdims=True) for p, d in zip(probs, d_probs))
        dq = None
        for slot in range(slots):
            d_score = (probs[slot] * (d_probs[slot] - delta)).astype(bf16)
            part = dot(d_score, k_refs[slot][...])
            dq = part if dq is None else dq + part
            dk_part = dot(d_score, q, ((0,), (0,)))
            dv_part = dot(probs[slot].astype(bf16), grad, ((0,), (0,)))
            dk[slot] = dk_part if dk[slot] is None else dk[slot] + dk_part
            dv[slot] = dv_part if dv[slot] is None else dv[slot] + dv_part
        dq_ref[one] = (dq * scale).astype(bf16)
    for slot in range(slots):
        dk_ref[slot] = (dk[slot] * scale).astype(bf16)
        dv_ref[slot] = dv[slot].astype(bf16)


def attend_back(block, queries, grads, keys, values, qdoc, qpos, kdoc, kpos):
    slots = len(keys)
    rows, width = queries[0].shape
    key_rows = keys[0].shape[0]
    own = grads[0].shape[1]
    heads = own // HD
    owned = lambda h, b: (0, b[0] * heads + h)
    local = lambda h, b: (0, h)
    whole = lambda h, b: (0, 0)
    return pl.pallas_call(
        functools.partial(attend_back_kernel, slots),
        grid_spec=pltpu.PrefetchScalarGridSpec(
            num_scalar_prefetch=1,
            grid=(heads,),
            in_specs=[pl.BlockSpec((rows, HD), owned)] * slots
            + [pl.BlockSpec((rows, HD), local)] * slots
            + [pl.BlockSpec((key_rows, HD), owned)] * (2 * slots)
            + [pl.BlockSpec((slots * rows, 1), whole)] * 2
            + [pl.BlockSpec((slots, key_rows), whole)] * 2,
            out_specs=[
                pl.BlockSpec((slots, rows, HD), lambda h, b: (0, 0, h)),
                pl.BlockSpec((slots, key_rows, HD), lambda h, b: (0, 0, h)),
                pl.BlockSpec((slots, key_rows, HD), lambda h, b: (0, 0, h)),
            ],
        ),
        out_shape=[
            jax.ShapeDtypeStruct((slots, rows, own), bf16),
            jax.ShapeDtypeStruct((slots, key_rows, own), bf16),
            jax.ShapeDtypeStruct((slots, key_rows, own), bf16),
        ],
        compiler_params=pltpu.CompilerParams(vmem_limit_bytes=40 * MIB),
        cost_estimate=pl.CostEstimate(
            flops=10 * slots * rows * slots * key_rows * own,
            bytes_accessed=12 * slots * key_rows * own,
            transcendentals=slots * rows * slots * key_rows * heads,
        ),
        name="attend_back",
    )(block, *queries, *grads, *keys, *values, qdoc, qpos, kdoc, kpos)


def segment_kernel(slots, own, *refs):
    pieces = refs[1 : 1 + slots]
    wq_ref, wk_ref, wv_ref, seg_ref, gain_ref, dmid_ref, out_ref, acc = refs[1 + slots :]
    step = pl.program_id(0)

    @pl.when(step == 0)
    def _():
        acc[...] = jnp.zeros_like(acc)

    for slot in range(slots):

        @pl.when(step == slot)
        def _(slot=slot):
            piece = pieces[slot][...]
            last = ((1,), (1,))
            acc[...] += (
                dot(piece[:, :own], wq_ref[...], last)
                + dot(piece[:, own : 2 * own], wk_ref[...], last)
                + dot(piece[:, 2 * own :], wv_ref[...], last)
            )

    @pl.when(step == slots - 1)
    def _():
        unit, scale = standardized(seg_ref[...].astype(f32))
        out_ref[...] = (
            dmid_ref[...] + norm_input_gradient(acc[...], gain_ref[...], unit, scale)
        ).astype(bf16)


def segment_gradient(block, pieces, w_query, w_key, w_value, segment, gain, d_middle):
    slots = len(pieces)
    rows, width = segment.shape
    own = w_query.shape[1] // slots
    whole = lambda k, b: (0, 0)
    weight = pl.BlockSpec((width, own), lambda k, b: (0, lax.rem(b[0] + k, slots)))
    row_spec = pl.BlockSpec((rows, width), whole)
    return pl.pallas_call(
        functools.partial(segment_kernel, slots, own),
        grid_spec=pltpu.PrefetchScalarGridSpec(
            num_scalar_prefetch=1,
            grid=(slots,),
            in_specs=[pl.BlockSpec((rows, 3 * own), whole)] * slots
            + [weight] * 3
            + [row_spec, pl.BlockSpec((1, width), whole), row_spec],
            out_specs=row_spec,
            scratch_shapes=[pltpu.VMEM((rows, width), f32)],
        ),
        out_shape=jax.ShapeDtypeStruct((rows, width), bf16),
        compiler_params=pltpu.CompilerParams(vmem_limit_bytes=20 * MIB),
        cost_estimate=pl.CostEstimate(
            flops=6 * rows * width * width, bytes_accessed=6 * width * width, transcendentals=0
        ),
        name="segment_gradient",
    )(block, *pieces, w_query, w_key, w_value, segment, gain, d_middle)


def on_device(
    segment,
    memory,
    compressed,
    document_labels,
    memory_filled_count,
    norm_gain,
    w_query,
    w_key,
    w_value,
    w_output,
    ffn_gain,
    w_expand,
    w_reduce,
    w_compress,
    result_cotangent,
    compressed_cotangent,
):
    _, rows, width = segment.shape
    blocks = lax.axis_size("blk")
    planes = lax.axis_size("stream")
    groups = planes // PLANE
    block = lax.axis_index("blk")
    stream = lax.axis_index("stream")
    place = lax.rem(stream, PLANE)
    core = lax.rem(stream, 2)
    hidden = w_expand.shape[1]
    ff_tile = hidden // PLANE
    half = width // 2
    own = width // blocks
    seg_len = rows * blocks
    part_rows = width // (planes * blocks)
    part_pairs = RATE * part_rows
    segment, memory, compressed = segment[0], memory[0], compressed[0]
    cotangent, comp_cotangent = result_cotangent[0], compressed_cotangent[0]
    labels, filled = document_labels[0], memory_filled_count[0]
    gain = norm_gain.reshape(1, width)
    gain_ffn = ffn_gain.reshape(1, width)
    block_ref = block.astype(jnp.int32).reshape(1)
    place_ref = place.astype(jnp.int32).reshape(1)

    def along_blk(x, shift):
        return lax.ppermute(x, "blk", [(i, (i + shift) % blocks) for i in range(blocks)])

    def in_plane(x, flip):
        return lax.ppermute(x, "stream", [(i, i ^ flip) for i in range(planes)])

    def columns(x, index, size):
        return lax.dynamic_slice_in_dim(x, index * size, size, 1)

    def by_core(mine, other, axis):
        return jnp.where(
            core == 0,
            jnp.concatenate([mine, other], axis=axis),
            jnp.concatenate([other, mine], axis=axis),
        )

    def spread(same, sliced):
        count = sliced[0].shape[0] if sliced else same.shape[0]
        wide = 0
        if same is not None:
            wide = same.shape[1] // 2
            keep, give = columns(same, core, wide), columns(same, 1 - core, wide)
        lead = [give] if wide else []
        tail = [sliced[j] for j in (1, 3, 5, 7)] if sliced else []
        got = in_plane(jnp.concatenate(lead + tail, axis=1), 1)
        each = sliced[0].shape[1] if sliced else 0
        out = []
        for j in (0, 2, 4, 6):
            mine = ([keep] if wide else []) + ([sliced[j]] if sliced else [])
            other = ([got[:, :wide]] if wide else []) + (
                [got[:, wide + j // 2 * each : wide + (j // 2 + 1) * each]] if sliced else []
            )
            both = by_core(jnp.concatenate(mine, 1), jnp.concatenate(other, 1), 0)
            out.append(both if j == 0 else in_plane(both, j))
        out = jnp.concatenate(out, axis=0)
        whole = None
        if wide:
            mine = out[:, :wide]
            whole = by_core(mine, in_plane(mine, 1), 1)
        return whole, out[:, wide:]

    def plane_slices(x, group_size):
        if groups > 1:
            split = x.reshape(x.shape[0], groups, PLANE, -1)
            x = split.transpose(0, 2, 1, 3).reshape(x.shape[0], -1)
        size = x.shape[1] // PLANE
        return [columns(x, place ^ j, size) for j in range(PLANE)]

    def over_groups(x):
        total = lax.dynamic_index_in_dim(x, stream // PLANE, 0, False).astype(f32)
        for k in range(1, groups):
            piece = lax.dynamic_index_in_dim(x, (stream // PLANE) ^ k, 0, False)
            total = total + in_plane(piece.astype(bf16), k * PLANE).astype(f32)
        return total

    def blk_sum(x):
        total = lax.dynamic_index_in_dim(x, block, 0, False).astype(f32)
        for k in range(1, blocks):
            piece = lax.dynamic_index_in_dim(x, lax.rem(block + k, blocks), 0, False)
            total = total + along_blk(piece, k).astype(f32)
        return total

    def blk_ring(entry):
        total = entry(lax.rem(block + blocks - 1, blocks))
        for k in range(blocks - 1):
            moved = along_blk(total, 1)
            total = moved.astype(f32) + entry(
                lax.rem(block + 2 * blocks - 2 - k, blocks)
            ).astype(f32)
            if k < blocks - 2:
                total = total.astype(bf16)
        return total

    rings = [[jnp.concatenate([compressed, memory], axis=0)], [segment]]
    for k in range(blocks - 1):
        for ring in rings:
            ring.append(along_blk(ring[-1], 1))

    pairs = memory.reshape(rows // RATE, RATE * width)
    pair_rows = rows // RATE
    cot_low, cot_high = cotangent[:pair_rows], cotangent[pair_rows:]
    same = jnp.concatenate(
        [
            x[:, h * half : (h + 1) * half]
            for h in range(2)
            for x in (cot_low, cot_high, comp_cotangent)
        ],
        axis=1,
    )
    same_all, pairs_all = spread(same, plane_slices(pairs, part_pairs))
    same_all = same_all.reshape(-1, 2, 3, half)
    cot_all = same_all[:, :, :2].reshape(PLANE, pair_rows, 2, 2, half)
    cot_all = cot_all.transpose(0, 3, 1, 2, 4).reshape(PLANE * rows, width)
    comp_cot_all = same_all[:, :, 2].reshape(-1, width)

    compress_part = dot(pairs_all, comp_cot_all, ((0,), (0,))).astype(bf16)
    compress_part = compress_part.reshape(groups, blocks, part_pairs, width)
    compress_sum = blk_sum(compress_part.transpose(1, 0, 2, 3))
    grad_compress = over_groups(compress_sum)
    new_compressed = dot(pairs, w_compress).astype(bf16)

    projected = []
    for k in range(blocks):
        projected.append(
            project(
                jnp.concatenate([rings[0][k], rings[1][k]], axis=0),
                gain,
                w_query,
                w_key,
                w_value,
            )
        )
    normed = [p[0] for p in projected]
    queries = [p[1] for p in projected]
    keys = [p[2] for p in projected]
    values = [p[3] for p in projected]

    owners = lax.rem(block - jnp.arange(blocks, dtype=jnp.int32) + blocks, blocks)
    by_owner = labels.reshape(3, blocks, rows).transpose(1, 0, 2)
    kdoc = by_owner[owners].reshape(blocks, 3 * rows)
    position = owners[:, None] * rows + jnp.arange(rows, dtype=jnp.int32)[None]
    first_filled = 2 * seg_len - filled
    kpos = jnp.concatenate(
        [
            jnp.where(position >= first_filled, -1, hidden_slot),
            jnp.where(position + seg_len >= first_filled, -1, hidden_slot),
            position,
        ],
        axis=1,
    ).astype(jnp.int32)
    qdoc = kdoc[:, 2 * rows :].reshape(blocks * rows, 1)
    qpos = position.reshape(blocks * rows, 1).astype(jnp.int32)

    attended = attend(queries[0], keys, values, qdoc[:rows], qpos[:rows], kdoc, kpos)
    result, normed_ffn, act, d_hidden, d_middle, d_branch, d_attended = middle_part(
        place_ref, attended, segment, w_output, gain_ffn, w_expand, w_reduce, cotangent
    )

    grads = [columns(d_attended, block, own)]
    for k in range(1, blocks):
        grads.append(along_blk(columns(d_attended, lax.rem(block + k, blocks), own), k))

    attended_slices = plane_slices(attended, part_rows)
    _, act_all = spread(
        None, [jnp.concatenate([act[j], attended_slices[j]], axis=1) for j in range(PLANE)]
    )
    act_all, attended_all = act_all[:, :ff_tile], act_all[:, ff_tile:]
    reduce_part = dot(cot_all, act_all, ((0,), (0,))).astype(bf16)

    dq, dk, dv = attend_back(
        block_ref, queries, grads, keys, values, qdoc, qpos, kdoc, kpos
    )
    pieces = [
        jnp.concatenate([dq[k], dk[k, 2 * rows :], dv[k, 2 * rows :]], axis=1)
        for k in range(blocks)
    ]
    arrived = [pieces[0]] + [along_blk(pieces[k], -k) for k in range(1, blocks)]

    both, d_hidden_all = spread(
        jnp.concatenate(
            [x[:, h * half : (h + 1) * half] for h in range(2) for x in (normed_ffn, d_branch)],
            axis=1,
        ),
        [d_hidden[j] for j in range(PLANE)],
    )
    both = both.reshape(-1, 2, 2, half)
    normed_ffn_all = both[:, :, 0].reshape(-1, width)
    d_branch_all = both[:, :, 1].reshape(-1, width)
    expand_part = dot(normed_ffn_all, d_hidden_all, ((0,), (0,))).astype(bf16)
    output_part = dot(attended_all, d_branch_all, ((0,), (0,))).astype(bf16)

    def ring_of(part):
        cut = part.reshape(groups * PLANE, blocks, part_rows, ff_tile)
        return blk_ring(lambda i: lax.dynamic_index_in_dim(cut, i, 1, False))

    wide = jnp.concatenate([ring_of(expand_part), ring_of(reduce_part)], axis=2).astype(bf16)
    wide = wide.reshape(groups, PLANE, part_rows, 2 * ff_tile)

    def to_place(j):
        cut = lax.dynamic_index_in_dim(wide, place ^ j, 1, False)
        return cut.reshape(groups * part_rows, 2 * ff_tile)

    outgoing = [to_place(j) for j in range(PLANE)]
    count = groups * part_rows
    got = in_plane(jnp.concatenate([outgoing[j] for j in (1, 3, 5, 7)], axis=0), 1)
    slices = []
    for j in (0, 2, 4, 6):
        other = got[j // 2 * count : (j // 2 + 1) * count]
        if j == 0:
            slices += [outgoing[0], other]
        else:
            moved = in_plane(jnp.concatenate([outgoing[j], other], axis=0), j)
            slices += [moved[:count], moved[count:]]
    for bit in range(3):
        flipped = (place >> bit) & 1 == 1
        slices = [jnp.where(flipped, slices[m ^ (1 << bit)], slices[m]) for m in range(PLANE)]
    summed = [
        over_groups(
            jnp.concatenate([x[:, at : at + ff_tile] for x in slices], axis=1).reshape(
                groups, part_rows, hidden
            )
        )
        for at in (0, ff_tile)
    ]
    grad_expand, reduce_turned = summed

    output_part = output_part.reshape(groups, blocks, part_rows, width).transpose(1, 0, 2, 3)
    grad_output = over_groups(blk_sum(output_part))

    def over_slots(pick, grad, first):
        return sum(dot(normed[k][first:], grad[k], ((0,), (0,))) for k in range(blocks))

    qkv = jnp.concatenate(
        [over_slots(0, dq, 2 * rows), over_slots(0, dk, 0), over_slots(0, dv, 0)], axis=1
    ).astype(bf16)
    qkv = qkv.reshape(groups, PLANE // 2, 2, blocks * part_rows, 3 * own)
    qkv = lax.dynamic_index_in_dim(qkv, core, 2, False).astype(f32) + in_plane(
        lax.dynamic_index_in_dim(qkv, 1 - core, 2, False), 1
    ).astype(f32)
    qkv = qkv.astype(bf16)
    chip = place // 2
    total = lax.dynamic_index_in_dim(qkv, chip, 1, False).astype(f32)
    for j in (2, 4, 6):
        piece = lax.dynamic_index_in_dim(qkv, chip ^ (j // 2), 1, False)
        total = total + in_plane(piece, j).astype(f32)
    total = total.astype(bf16).reshape(groups, blocks, part_rows, 3 * own)
    parts = [lax.dynamic_index_in_dim(total, block, 1, False)]
    for k in range(1, blocks):
        piece = lax.dynamic_index_in_dim(total, lax.rem(block + k, blocks), 1, False)
        parts.append(along_blk(piece, k))
    stacked = jnp.stack(parts)[owners]
    stacked = stacked.reshape(blocks, groups, part_rows, 3, own).transpose(1, 2, 3, 0, 4)
    stacked = over_groups(stacked.reshape(groups, part_rows, 3 * width))
    grad_query, grad_key, grad_value = (
        stacked[:, :width],
        stacked[:, width : 2 * width],
        stacked[:, 2 * width :],
    )

    start = (stream * blocks + block) * part_rows

    def mine(x):
        return lax.dynamic_slice_in_dim(x, start, part_rows, 0)

    def weighted(weight, grad):
        return jnp.sum(mine(weight).astype(f32) * grad, axis=1)

    grad_norm_gain = (
        weighted(w_query, grad_query) + weighted(w_key, grad_key) + weighted(w_value, grad_value)
    ) / mine(norm_gain)
    grad_ffn_gain = weighted(w_expand, grad_expand) / mine(ffn_gain)

    grad_segment = segment_gradient(
        block_ref, arrived, w_query, w_key, w_value, segment, gain, d_middle
    )
    return (
        result[None],
        new_compressed[None],
        grad_segment[None],
        grad_norm_gain,
        grad_query,
        grad_key,
        grad_value,
        grad_output,
        grad_ffn_gain,
        grad_expand,
        reduce_turned.T,
        grad_compress,
    )


def solution(mesh):
    tokens = P("stream", "blk", None)
    both = ("stream", "blk")
    in_specs = (
        (tokens,) * 3
        + (P("stream", None, None), P("stream"))
        + (P(),) * 9
        + (tokens,) * 2
    )
    out_specs = (
        (tokens,) * 3
        + (P(both),)
        + (P(both, None),) * 4
        + (P(both), P(both, None), P(None, both), P(both, None))
    )
    return jax.shard_map(
        on_device, mesh=mesh, in_specs=in_specs, out_specs=out_specs, check_vma=False
    )
```

```python
import functools

import jax
import jax.numpy as jnp
from jax import lax
from jax.experimental import pallas as pl
from jax.experimental.pallas import tpu as pltpu
from jax.sharding import PartitionSpec as P

HD = 128
RATE = 2
PLANE = 8

epsilon = 1e-05
masked_score = -1e30
hidden_slot = 1 << 30

f32 = jnp.float32
bf16 = jnp.bfloat16
MIB = 1 << 20
FLOPS_PER_US = 0.5e9
VM = pl.BlockSpec(memory_space=pltpu.VMEM)
SM = pl.BlockSpec(memory_space=pltpu.SMEM)
ANY = pl.BlockSpec(memory_space=pl.ANY)


def dot(left, right, contract=((1,), (0,))):
    return lax.dot_general(left, right, (contract, ((), ())), preferred_element_type=f32)


def standardized(rows):
    offset = rows - jnp.mean(rows, axis=-1, keepdims=True)
    scale = lax.rsqrt(jnp.mean(offset * offset, axis=-1, keepdims=True) + epsilon)
    return offset * scale, scale


def norm_input_gradient(e, gain, unit, scale):
    eg = e * gain
    return scale * (
        eg
        - jnp.mean(eg, axis=-1, keepdims=True)
        - unit * jnp.mean(eg * unit, axis=-1, keepdims=True)
    )


LOG2E = 1.4426950408889634
SCORE_SCALE = HD ** (-0.5) * LOG2E
LAST = ((1,), (1,))
FIRST = ((0,), (0,))
TILE = 256


def block_of(shape):
    return pl.BlockSpec(shape, lambda i: (0,) * len(shape))


def call(
    kernel, name, ins, outs, scratch=(), copies=0, grant=24, after=(), cost_us=1.0
):
    in_specs, operands = [], []
    inputs = len(ins)

    def body(*refs):
        kernel(*refs[:inputs], *refs[inputs + len(after) :])

    for x in ins:
        far = isinstance(x, tuple)
        x = x[0] if far else x
        operands.append(pltpu.with_memory_space_constraint(x, pltpu.HBM) if far else x)
        in_specs.append(ANY if far else SM if x.size == 1 else block_of(x.shape))
    operands += after
    in_specs += [ANY] * len(after)
    scratch = list(scratch)
    if copies:
        scratch.append(pltpu.SemaphoreType.DMA((copies,)))
    return pl.pallas_call(
        body,
        grid=(1,),
        in_specs=in_specs,
        out_specs=[ANY if isinstance(o, tuple) else block_of(o.shape) for o in outs],
        out_shape=[
            pltpu.HBM(o[0].shape, o[0].dtype) if isinstance(o, tuple) else o for o in outs
        ],
        scratch_shapes=scratch,
        compiler_params=pltpu.CompilerParams(vmem_limit_bytes=grant * MIB),
        cost_estimate=pl.CostEstimate(
            flops=int(cost_us * FLOPS_PER_US), bytes_accessed=0, transcendentals=0
        ),
        name=name,
    )(*operands)


def gate(arrays, after):
    count = len(arrays)
    return pl.pallas_call(
        lambda *refs: None,
        in_specs=[ANY] * (count + len(after)),
        out_specs=[ANY] * count,
        out_shape=[pltpu.HBM(x.shape, x.dtype) for x in arrays],
        input_output_aliases={i: i for i in range(count)},
        compiler_params=pltpu.CompilerParams(vmem_limit_bytes=MIB),
        cost_estimate=pl.CostEstimate(flops=0, bytes_accessed=0, transcendentals=0),
        name="gate",
    )(*arrays, *after)


class Copies:
    def __init__(self, sems):
        self.sems, self.count = sems, 0

    def __call__(self, source, target):
        copy = pltpu.make_async_copy(source, target, self.sems.at[self.count])
        copy.start()
        self.count += 1
        return copy


def lanes(start, size):
    return pl.ds(pl.multiple_of(start, size), size)


def shape_of(shape, dtype=bf16):
    return jax.ShapeDtypeStruct(shape, dtype)


def norm_rows(raw, gain_ref, normed_ref):
    rows = raw.shape[1]
    for i in range(raw.shape[0]):
        unit, _ = standardized(raw[i].astype(f32))
        normed_ref[i * rows : (i + 1) * rows, :] = (unit * gain_ref[...]).astype(bf16)


ROW_CUTS = 4


def bring_rows(bring, source, target):
    step = source.shape[0] // ROW_CUTS
    return [
        bring(source.at[pl.ds(i * step, step)], target.at[pl.ds(i * step, step)])
        for i in range(ROW_CUTS)
    ]


def wait_all(copies):
    for copy in copies:
        copy.wait()


def project_kernel(all_queries, *refs):
    block_ref, *raw_refs = refs[:4]
    gain_ref, wq_ref, wk_ref, wv_ref = refs[4:8]
    outs = refs[8:12]
    wq, wk, wv, normed_ref, q_ref, k_ref, v_ref, raw, sems = refs[12:]
    bring = Copies(sems)
    width = k_ref.shape[1]
    raws = [bring(ref, raw.at[i]) for i, ref in enumerate(raw_refs)]
    coming = [bring_rows(bring, wk_ref, wk), bring_rows(bring, wv_ref, wv)]
    if all_queries:
        query_weight = bring(wq_ref, wq)
    else:
        own = q_ref.shape[1]
        query_weight = bring(wq_ref.at[:, lanes(block_ref[0] * own, own)], wq)
    wait_all(raws)
    norm_rows(raw, gain_ref, normed_ref)
    leaving = [bring(normed_ref, outs[0])]
    normed = normed_ref[...]
    for copies, weight, target, out in zip(coming, (wk, wv), (k_ref, v_ref), outs[2:]):
        wait_all(copies)
        for at in range(0, width, TILE):
            target[:, at : at + TILE] = dot(normed, weight[:, at : at + TILE]).astype(bf16)
        leaving.append(bring(target, out))
    query_weight.wait()
    q_ref[...] = dot(normed[2 * raw.shape[1] :], wq[...]).astype(bf16)
    leaving.append(bring(q_ref, outs[1]))
    wait_all(leaving)


def projected_shapes(rows, width, own):
    return [
        shape_of((3 * rows, width)),
        shape_of((rows, own)),
        shape_of((3 * rows, width)),
        shape_of((3 * rows, width)),
    ]


def project(block, raw_rows, gain, w_query, w_key, w_value, own, after):
    rows, width = raw_rows[0].shape
    shapes = projected_shapes(rows, width, own)
    weights = [(width, own), (width, width), (width, width)]
    return call(
        functools.partial(project_kernel, own == width),
        "project",
        [block] + [(x,) for x in raw_rows] + [gain, (w_query,), (w_key,), (w_value,)],
        [(x,) for x in shapes],
        scratch=[pltpu.VMEM(x, bf16) for x in weights]
        + [pltpu.VMEM(x.shape, x.dtype) for x in shapes]
        + [pltpu.VMEM((3, rows, width), bf16)],
        copies=2 * ROW_CUTS + 8,
        after=after,
        cost_us=0.1,
    )


def compress_kernel(pairs_ref, w_far, out_ref, w_ref, sems):
    bring = Copies(sems)
    count = w_ref.shape[0]
    coming = [bring(w_far.at[pl.ds(i * w_ref.shape[1], w_ref.shape[1])], w_ref.at[i]) for i in range(count)]
    total = None
    for i in range(count):
        coming[i].wait()
        part = dot(pairs_ref[:, i * w_ref.shape[1] : (i + 1) * w_ref.shape[1]], w_ref[i])
        total = part if total is None else total + part
    out_ref[...] = total.astype(bf16)


def compress(pairs, w_compress, after):
    depth, width = w_compress.shape
    count = 4
    return call(
        compress_kernel,
        "compress",
        [pairs, (w_compress,)],
        [shape_of((pairs.shape[0], width))],
        scratch=[pltpu.VMEM((count, depth // count, width), bf16)],
        copies=count,
        after=after,
        cost_us=3.2,
    )[0]


def score_bias(qdoc, qpos, kdoc_ref, kpos_ref, slot):
    allowed = (kdoc_ref[slot : slot + 1, :] == qdoc) & (kpos_ref[slot : slot + 1, :] <= qpos)
    return jnp.where(allowed, 0.0, masked_score)


def attend_kernel(slots, *refs):
    qdoc_ref, qpos_ref, kdoc_ref, kpos_ref, q_far = refs[:5]
    k_far = refs[5 : 5 + slots]
    v_far = refs[5 + slots : 5 + 2 * slots]
    out_ref, stat_ref, bias_ref, q_ref, k_ref, v_ref, sems = refs[5 + 2 * slots :]
    rows, width = q_ref.shape
    bring = Copies(sems)
    query = bring(q_far, q_ref)
    tiles = [slice(at, at + TILE) for at in range(0, width, TILE)]
    coming = [
        [
            bring(far[slot].at[:, at], near.at[slot, :, at])
            for slot in range(slots)
            for far, near in ((k_far, k_ref), (v_far, v_ref))
        ]
        for at in tiles
    ]
    qdoc, qpos = qdoc_ref[:rows, :], qpos_ref[:rows, :]
    for slot in range(slots):
        bias_ref[slot] = score_bias(qdoc, qpos, kdoc_ref, kpos_ref, slot)
    query.wait()
    lane = lax.broadcasted_iota(jnp.int32, (rows, HD), 1)
    stats = jnp.zeros((rows, HD), f32)
    heads = width // HD
    for head in range(heads):
        if head * HD % TILE == 0:
            for copy in coming[head * HD // TILE]:
                copy.wait()
        at = slice(head * HD, (head + 1) * HD)
        q = q_ref[:, at]
        scores = [
            dot(q, k_ref[slot, :, at], LAST) * SCORE_SCALE + bias_ref[slot]
            for slot in range(slots)
        ]
        top = functools.reduce(jnp.maximum, scores)
        top = jnp.max(top, axis=-1, keepdims=True)
        weights = [jnp.exp2(s - top) for s in scores]
        total = jnp.sum(functools.reduce(jnp.add, weights), axis=-1, keepdims=True)
        out_ref[:, at] = functools.reduce(
            jnp.add,
            [dot(weights[slot].astype(bf16), v_ref[slot, :, at]) for slot in range(slots)],
        )
        stats = jnp.where(lane == head, top, stats)
        stats = jnp.where(lane == heads + head, total, stats)
    stat_ref[...] = stats


def attend(query, keys, values, marks, after):
    slots = len(keys)
    rows, width = query.shape
    key_rows = keys[0].shape[0]
    return call(
        functools.partial(attend_kernel, slots),
        "attend",
        [*marks, (query,)] + [(x,) for x in (*keys, *values)],
        [shape_of((rows, width), f32), shape_of((rows, HD), f32)],
        scratch=[
            pltpu.VMEM((slots, rows, key_rows), f32),
            pltpu.VMEM((rows, width), bf16),
            pltpu.VMEM((slots, key_rows, width), bf16),
            pltpu.VMEM((slots, key_rows, width), bf16),
        ],
        copies=1 + 2 * slots * (width // TILE),
        after=after,
        cost_us=0.1,
    )


def finish_kernel(slot, *refs):
    block_ref, *raw_refs = refs[:4]
    gain_ref, wq_far, wk_far, wv_far = refs[4:8]
    query_far, sum_ref, stat_ref, qdoc_ref, qpos_ref, kdoc_ref, kpos_ref = refs[8:15]
    seg_ref, wo_far, gain_ffn_ref = refs[15:18]
    outs = refs[18:23]
    middle_ref, nf_ref = refs[23:25]
    wq, wk, wv, normed_ref, q_ref, k_ref, v_ref, wo, query_ref, att_ref, raw, sems = refs[25:]
    rows, width = query_ref.shape
    bring = Copies(sems)
    raws = [bring(ref, raw.at[i]) for i, ref in enumerate(raw_refs)]
    coming = [bring_rows(bring, wk_far, wk), bring_rows(bring, wv_far, wv)]
    query = bring(query_far, query_ref)
    output_weight = bring(wo_far, wo)
    own = q_ref.shape[1]
    query_weight = bring(wq_far.at[:, lanes(block_ref[0] * own, own)], wq)
    bias = score_bias(qdoc_ref[:rows, :], qpos_ref[:rows, :], kdoc_ref, kpos_ref, slot)
    wait_all(raws)
    norm_rows(raw, gain_ref, normed_ref)
    leaving = [bring(normed_ref, outs[0])]
    normed = normed_ref[...]
    query.wait()
    heads = width // HD
    for copies, weight, target, out in zip(coming, (wk, wv), (k_ref, v_ref), outs[2:4]):
        wait_all(copies)
        for at in range(0, width, TILE):
            target[:, at : at + TILE] = dot(normed, weight[:, at : at + TILE]).astype(bf16)
        leaving.append(bring(target, out))
    group = 4
    for start in range(0, heads, group):
        some = range(start, start + group)
        at = {h: slice(h * HD, (h + 1) * HD) for h in some}
        scores = {
            h: dot(query_ref[:, at[h]], k_ref[:, at[h]], LAST) * SCORE_SCALE + bias for h in some
        }
        before = {h: stat_ref[:, h : h + 1] for h in some}
        top = {
            h: jnp.maximum(before[h], jnp.max(scores[h], axis=-1, keepdims=True)) for h in some
        }
        weights = {h: jnp.exp2(scores[h] - top[h]) for h in some}
        shrink = {h: jnp.exp2(before[h] - top[h]) for h in some}
        total = {
            h: stat_ref[:, heads + h : heads + h + 1] * shrink[h]
            + jnp.sum(weights[h], axis=-1, keepdims=True)
            for h in some
        }
        out = {
            h: sum_ref[:, at[h]] * shrink[h] + dot(weights[h].astype(bf16), v_ref[:, at[h]])
            for h in some
        }
        for h in some:
            att_ref[:, at[h]] = (out[h] * (1.0 / total[h])).astype(bf16)
    query_weight.wait()
    q_ref[...] = dot(normed[2 * raw.shape[1] :], wq[...]).astype(bf16)
    leaving.append(bring(q_ref, outs[1]))
    leaving.append(bring(att_ref, outs[4]))
    output_weight.wait()
    middle = seg_ref[...].astype(f32) + dot(att_ref[...], wo[...])
    middle_ref[...] = middle
    unit, _ = standardized(middle)
    nf_ref[...] = (unit * gain_ffn_ref[...]).astype(bf16)
    wait_all(leaving)


def finish(
    slot, block, raw_rows, gain, w_query, w_key, w_value, own, query, partial, marks, segment, w_output, gain_ffn, after
):
    rows, width = segment.shape
    shapes = projected_shapes(rows, width, own)
    weights = [(width, own), (width, width), (width, width)]
    return call(
        functools.partial(finish_kernel, slot),
        "finish",
        [block] + [(x,) for x in raw_rows] + [gain, (w_query,), (w_key,), (w_value,), (query,), *partial, *marks]
        + [segment, (w_output,), gain_ffn],
        [(x,) for x in shapes]
        + [(shape_of((rows, width)),), shape_of((rows, width), f32), shape_of((rows, width))],
        scratch=[pltpu.VMEM(x, bf16) for x in weights]
        + [pltpu.VMEM(x.shape, x.dtype) for x in shapes]
        + [
            pltpu.VMEM((width, width), bf16),
            pltpu.VMEM((rows, width), bf16),
            pltpu.VMEM((rows, width), bf16),
            pltpu.VMEM((3, rows, width), bf16),
        ],
        copies=2 * ROW_CUTS + 11,
        after=after,
        cost_us=9.0,
    )


def feed_kernel(chips, place_ref, nf_own, nf_got, cot_own, cot_got, we_far, wr_far, *refs):
    both_far = refs[:chips]
    res_ref, dn_ref, send_ref, nf_ref, cot_ref, both, we, wr, sems = refs[chips:]
    rows = nf_own.shape[0]
    tile = wr.shape[1]
    bring = Copies(sems)
    coming = []

    def ahead(chip):
        if chip < chips:
            at = lanes((place_ref[0] ^ (2 * chip)) * tile, tile)
            coming.append(
                (
                    bring(we_far.at[:, at], we.at[chip]),
                    bring(wr_far.at[at, :], wr.at[chip]),
                )
            )

    ahead(0)
    ahead(1)
    nf_ref[:rows] = nf_own[...]
    nf_ref[rows:] = nf_got[...]
    cot_ref[:rows] = cot_own[...]
    cot_ref[rows:] = cot_got[...]
    part = tile // 2
    leaving = []
    res = dn = None
    for chip in range(chips):
        wait_all(coming[chip])
        ahead(chip + 2)
        for at in range(0, tile, part):
            here = slice(at, at + part)
            hidden = dot(nf_ref[...], we[chip, :, here])
            d_act = dot(cot_ref[...], wr[chip, here, :], LAST)
            cdf = 0.5 + 0.5 * lax.erf(hidden * (0.5**0.5))
            density = jnp.exp2(hidden * hidden * (-0.5 * LOG2E)) * 0.3989422804014327
            both[chip, 0, :, here] = (hidden * cdf).astype(bf16)
            both[chip, 1, :, here] = (
                d_act * (cdf + hidden * density)
            ).astype(bf16)
        leaving.append(bring(both.at[chip], both_far[chip]))
        res_part = dot(both[chip, 0], wr[chip])
        dn_part = dot(both[chip, 1], we[chip], LAST)
        res = res_part if chip == 0 else res + res_part
        dn = dn_part if chip == 0 else dn + dn_part
    res_ref[...] = res[:rows]
    dn_ref[...] = dn[:rows]
    send_ref[0] = res[rows:].astype(bf16)
    send_ref[1] = dn[rows:].astype(bf16)
    wait_all(leaving)


def feed(place, nf_own, nf_got, cot_own, cot_got, w_expand, w_reduce, after):
    rows, width = nf_own.shape
    chips = PLANE // 2
    tile = w_expand.shape[1] // PLANE
    return call(
        functools.partial(feed_kernel, chips),
        "feed",
        [place, nf_own, nf_got, cot_own, cot_got, (w_expand,), (w_reduce,)],
        [(shape_of((2, 2 * rows, tile)),)] * chips
        + [shape_of((rows, width), f32)] * 2
        + [shape_of((2, rows, width))],
        scratch=[
            pltpu.VMEM((2 * rows, width), bf16),
            pltpu.VMEM((2 * rows, width), bf16),
            pltpu.VMEM((chips, 2, 2 * rows, tile), bf16),
            pltpu.VMEM((chips, width, tile), bf16),
            pltpu.VMEM((chips, tile, width), bf16),
        ],
        copies=3 * chips,
        grant=28,
        after=after,
        cost_us=8.0,
    )


def leave_kernel(slots, block_ref, *refs):
    res_ref, dn_ref, got_ref, middle_ref, cot_ref, gain_ref, wo_far = refs[:7]
    result_ref, dmid_far, branch_far = refs[7:10]
    datt_refs = refs[10 : 10 + slots]
    wo, dmid_ref, branch_ref, sems = refs[10 + slots :]
    own = wo.shape[1]
    bring = Copies(sems)
    coming = [
        bring(wo_far.at[lanes(lax.rem(block_ref[0] + slot, slots) * own, own), :], wo.at[slot])
        for slot in range(slots)
    ]
    middle = middle_ref[...]
    result_ref[...] = (middle + (res_ref[...] + got_ref[0].astype(f32))).astype(bf16)
    unit, scale = standardized(middle)
    d_normed = dn_ref[...] + got_ref[1].astype(f32)
    d_mid = cot_ref[...].astype(f32) + norm_input_gradient(d_normed, gain_ref[...], unit, scale)
    dmid_ref[...] = d_mid
    branch = d_mid.astype(bf16)
    branch_ref[...] = branch
    leaving = [bring(dmid_ref, dmid_far), bring(branch_ref, branch_far)]
    for slot in range(slots):
        coming[slot].wait()
        datt_refs[slot][...] = dot(branch, wo[slot], LAST).astype(bf16)
    wait_all(leaving)


def leave(block, slots, res, dn, got, middle, cotangent, gain, w_output, after):
    rows, width = middle.shape
    own = width // slots
    return call(
        functools.partial(leave_kernel, slots),
        "leave",
        [block, res, dn, got, middle, cotangent, gain, (w_output,)],
        [shape_of((rows, width)), (shape_of((rows, width), f32),), (shape_of((rows, width)),)]
        + [shape_of((rows, own))] * slots,
        scratch=[
            pltpu.VMEM((slots, own, width), bf16),
            pltpu.VMEM((rows, width), f32),
            pltpu.VMEM((rows, width), bf16),
        ],
        copies=slots + 2,
        after=after,
        cost_us=3.8,
    )


def attend_back_kernel(slots, heads, block_ref, *refs):
    take = iter(refs)
    marks = [next(take) for _ in range(4)]
    g_refs = [next(take) for _ in range(slots)]
    q_far = [next(take) for _ in range(slots)]
    k_far = [next(take) for _ in range(slots)]
    v_far = [next(take) for _ in range(slots)]
    piece_far = [next(take) for _ in range(slots)]
    dk_far, dv_far, q_ref, k_ref, v_ref, piece_refs, dk_ref, dv_ref, sems = take
    qdoc_ref, qpos_ref, kdoc_ref, kpos_ref = marks
    scale = HD ** (-0.5)
    rows = g_refs[0].shape[0]
    own = heads * HD
    bring = Copies(sems)
    owned = lanes(block_ref[0] * own, own)
    coming = []
    for slot in range(slots):
        coming.append(bring(q_far[slot].at[:, owned] if slot == 0 else q_far[slot], q_ref.at[slot]))
        coming.append(bring(k_far[slot].at[:, owned], k_ref.at[slot]))
        coming.append(bring(v_far[slot].at[:, owned], v_ref.at[slot]))
    for copy in coming:
        copy.wait()
    dk = [[None] * slots for _ in range(heads)]
    dv = [[None] * slots for _ in range(heads)]
    for one in range(slots):
        here = slice(one * rows, (one + 1) * rows)
        qdoc, qpos = qdoc_ref[here, :], qpos_ref[here, :]
        bias = [score_bias(qdoc, qpos, kdoc_ref, kpos_ref, slot) for slot in range(slots)]
        for head in range(heads):
            at = slice(head * HD, (head + 1) * HD)
            q = q_ref[one, :, at]
            grad = g_refs[one][:, at]
            scores = [
                dot(q, k_ref[slot, :, at], LAST) * SCORE_SCALE + bias[slot]
                for slot in range(slots)
            ]
            top = jnp.max(functools.reduce(jnp.maximum, scores), axis=-1, keepdims=True)
            weights = [jnp.exp2(s - top) for s in scores]
            total = jnp.sum(functools.reduce(jnp.add, weights), axis=-1, keepdims=True)
            inverse = 1.0 / total
            probs = [w * inverse for w in weights]
            d_probs = [dot(grad, v_ref[slot, :, at], LAST) for slot in range(slots)]
            delta = jnp.sum(
                functools.reduce(jnp.add, [p * d for p, d in zip(probs, d_probs)]),
                axis=-1,
                keepdims=True,
            )
            dq = None
            for slot in range(slots):
                d_score = (probs[slot] * (d_probs[slot] - delta)).astype(bf16)
                part = dot(d_score, k_ref[slot, :, at])
                dq = part if dq is None else dq + part
                dk_part = dot(d_score, q, FIRST)
                dv_part = dot(probs[slot].astype(bf16), grad, FIRST)
                dk[head][slot] = dk_part if one == 0 else dk[head][slot] + dk_part
                dv[head][slot] = dv_part if one == 0 else dv[head][slot] + dv_part
            piece_refs[one, :, at] = (dq * scale).astype(bf16)
    leaving = []
    for slot in range(slots):
        for head in range(heads):
            at = slice(head * HD, (head + 1) * HD)
            d_key = (dk[head][slot] * scale).astype(bf16)
            d_value = dv[head][slot].astype(bf16)
            dk_ref[slot, :, at] = d_key
            dv_ref[slot, :, at] = d_value
            for i, value in enumerate((d_key, d_value)):
                first = (i + 1) * own + head * HD
                piece_refs[slot, :, first : first + HD] = value[2 * rows :]
        leaving.append(bring(piece_refs.at[slot], piece_far[slot]))
    leaving += [bring(dk_ref, dk_far), bring(dv_ref, dv_far)]
    wait_all(leaving)


def attend_back(block, queries, grads, keys, values, marks, after):
    slots = len(keys)
    key_rows = keys[0].shape[0]
    rows, own = grads[0].shape
    heads = own // HD
    return call(
        functools.partial(attend_back_kernel, slots, heads),
        "attend_back",
        [block, *marks, *grads] + [(x,) for x in (*queries, *keys, *values)],
        [(shape_of((rows, 3 * own)),)] * slots + [(shape_of((slots, key_rows, own)),)] * 2,
        scratch=[
            pltpu.VMEM((slots, rows, own), bf16),
            pltpu.VMEM((slots, key_rows, own), bf16),
            pltpu.VMEM((slots, key_rows, own), bf16),
            pltpu.VMEM((slots, rows, 3 * own), bf16),
            pltpu.VMEM((slots, key_rows, own), bf16),
            pltpu.VMEM((slots, key_rows, own), bf16),
        ],
        copies=4 * slots + 2,
        after=after,
        cost_us=4.0,
    )


def heads_kernel(slots, place_ref, *refs):
    piece_far = refs[:slots]
    normed_far = refs[slots : 2 * slots]
    dk_far, dv_far = refs[2 * slots : 2 * slots + 2]
    keep_far, give_far, out_ref, pieces, normed, dk, dv, sems = refs[2 * slots + 2 :]
    own = dk.shape[2]
    rows = pieces.shape[1]
    cut = out_ref.shape[2]
    core = lax.rem(place_ref[0], 2)
    bring = Copies(sems)
    second = [bring(normed_far[0], normed.at[0]), bring(dv_far, dv)]
    second += [bring(normed_far[slot], normed.at[slot]) for slot in range(1, slots)]
    third = [bring(dk_far, dk)]
    fourth = [bring(piece_far[slot], pieces.at[slot]) for slot in range(slots)]
    leaving = []

    def store(value, at):
        value = value.astype(bf16)
        here = slice(at, at + value.shape[1])
        for j in range(value.shape[0] // cut):
            out_ref[j % 2, j // 2, :, here] = value[j * cut : (j + 1) * cut]
        here = pl.ds(at, value.shape[1])
        leaving.append(bring(out_ref.at[1 - core, :, :, here], give_far.at[:, :, here]))
        leaving.append(bring(out_ref.at[core, :, :, here], keep_far.at[:, :, here]))

    def over_slots(part):
        total = part(0)
        for slot in range(1, slots):
            total = total + part(slot)
        return total

    wait_all(second)
    store(over_slots(lambda slot: dot(normed[slot], dv[slot], FIRST)), 2 * own)
    wait_all(third)
    store(over_slots(lambda slot: dot(normed[slot], dk[slot], FIRST)), own)
    wait_all(fourth)
    store(over_slots(lambda slot: dot(normed[slot, 2 * rows :], pieces[slot, :, :own], FIRST)), 0)
    wait_all(leaving)


def heads_gradient(place, normed, pieces, dk, dv, cut, after):
    slots, key_rows, own = dk.shape
    rows = pieces[0].shape[0]
    width = normed[0].shape[1]
    half = (width // cut // 2, cut, 3 * own)
    return call(
        functools.partial(heads_kernel, slots),
        "heads_gradient",
        [place] + [(x,) for x in (*pieces, *normed, dk, dv)],
        [(shape_of(half),)] * 2,
        scratch=[
            pltpu.VMEM((2, *half), bf16),
            pltpu.VMEM((slots, rows, 3 * own), bf16),
            pltpu.VMEM((slots, key_rows, width), bf16),
            pltpu.VMEM((slots, key_rows, own), bf16),
            pltpu.VMEM((slots, key_rows, own), bf16),
        ],
        copies=2 * slots + 8,
        after=after,
        grant=36,
        cost_us=0.1,
    )


def output_kernel(place_ref, att_far, branch_far, keep_far, give_far, out_ref, att, branch, sems):
    core = lax.rem(place_ref[0], 2)
    cut = out_ref.shape[2]
    bring = Copies(sems)
    wait_all([bring(att_far, att), bring(branch_far, branch)])
    step = 2 * cut
    leaving = []
    for i in range(out_ref.shape[1]):
        at = slice(i * step, (i + 1) * step)
        value = dot(att[:, at], branch[...], FIRST).astype(bf16)
        for j in range(2):
            out_ref[j, i] = value[j * cut : (j + 1) * cut]
        leaving.append(bring(out_ref.at[1 - core, i], give_far.at[i]))
        leaving.append(bring(out_ref.at[core, i], keep_far.at[i]))
    wait_all(leaving)


def output_gradient(place, attended, branch, cut, after):
    rows, width = attended.shape
    half = (width // cut // 2, cut, width)
    return call(
        output_kernel,
        "output_gradient",
        [place, (attended,), (branch,)],
        [(shape_of(half),)] * 2,
        scratch=[
            pltpu.VMEM((2, *half), bf16),
            pltpu.VMEM((rows, width), bf16),
            pltpu.VMEM((rows, width), bf16),
        ],
        copies=2 + 2 * half[0],
        after=after,
        cost_us=2.8,
    )


def pair_add_kernel(place_ref, *refs):
    keep_far = refs[:2]
    got = refs[2:4]
    outs = refs[4:8]
    near = refs[8:10]
    total, sems = refs[10:]
    bring = Copies(sems)
    chip = place_ref[0] // 2
    order = [1, 2, 3, 0]
    coming = {j: [bring(f.at[chip ^ j], n.at[j]) for f, n in zip(keep_far, near)] for j in order}
    leaving = []
    width = near[0].shape[2]
    for j in order:
        wait_all(coming[j])
        for at, a, b in zip((slice(0, width), slice(width, None)), near, got):
            total[j, :, at] = (a[j].astype(f32) + b[chip ^ j].astype(f32)).astype(bf16)
        leaving.append(bring(total.at[j], outs[j]))
    wait_all(leaving)


def pair_add(place, qkv_keep, qkv_got, output_keep, output_got, after):
    chips, rows, width = qkv_keep.shape
    wide = output_keep.shape[2]
    return call(
        pair_add_kernel,
        "pair_add",
        [place, (qkv_keep,), (output_keep,), qkv_got, output_got],
        [(shape_of((rows, width + wide)),)] * chips,
        scratch=[
            pltpu.VMEM(qkv_keep.shape, bf16),
            pltpu.VMEM(output_keep.shape, bf16),
            pltpu.VMEM((chips, rows, width + wide), bf16),
        ],
        copies=3 * chips,
        after=after,
        cost_us=3.0,
    )


def chip_add_kernel(chips, block_ref, *refs):
    pieces = refs[:chips]
    outs = refs[chips:-1]
    total = refs[-1]
    total[...] = sum(p[...].astype(f32) for p in pieces)
    blocks = len(outs)
    rows = total.shape[0] // blocks
    for k in range(blocks):
        outs[k][...] = total[lanes((block_ref[0] ^ k) * rows, rows), :].astype(bf16)


def chip_add(block, blocks, pieces, after):
    rows, width = pieces[0].shape
    return call(
        functools.partial(chip_add_kernel, len(pieces)),
        "chip_add",
        [block, *pieces],
        [shape_of((rows // blocks, width))] * blocks,
        scratch=[pltpu.VMEM((rows, width), f32)],
        after=after,
        cost_us=0.1,
    )


def last_heads_kernel(blocks, block_ref, *refs):
    parts = refs[:blocks]
    gain_ref = refs[blocks]
    weights_far = refs[blocks + 1 : blocks + 4]
    at_ref = refs[blocks + 4]
    outs = refs[blocks + 5 : blocks + 8]
    output_ref, norm_ref, weights, sems = refs[blocks + 8 :]
    rows, width = output_ref.shape
    own = width // blocks
    bring = Copies(sems)
    here = pl.ds(pl.multiple_of(at_ref[0] * rows, rows), rows)
    coming = [bring(far.at[here, :], weights.at[i]) for i, far in enumerate(weights_far)]
    for k in range(blocks):
        at = lanes((block_ref[0] ^ k) * own, own)
        for i in range(3):
            outs[i][:, at] = parts[k][:, i * own : (i + 1) * own].astype(f32)
    first = 3 * own
    output_ref[...] = sum(p[:, first : first + width].astype(f32) for p in parts)
    wait_all(coming)
    total = sum(weights[i].astype(f32) * outs[i][...] for i in range(3))
    norm_ref[...] = jnp.sum(total, axis=1, keepdims=True) / gain_ref[...]


def last_heads(block, index, parts, gain, w_query, w_key, w_value, after):
    blocks = len(parts)
    rows = parts[0].shape[0]
    width = w_query.shape[0]
    return call(
        functools.partial(last_heads_kernel, blocks),
        "last_heads",
        [block, *parts, gain, (w_query,), (w_key,), (w_value,), index],
        [shape_of((rows, width), f32)] * 4 + [shape_of((rows, 1), f32)],
        scratch=[pltpu.VMEM((3, rows, width), bf16)],
        copies=3,
        after=after,
        cost_us=1.8,
    )


def segment_kernel(slots, block_ref, *refs):
    pieces_far = refs[:slots]
    seg_ref, gain_ref, dmid_far = refs[slots : slots + 3]
    far = refs[slots + 3 : slots + 6]
    out_ref, weight, pieces, dmid_ref, sems = refs[slots + 6 :]
    own = pieces.shape[2] // 3
    bring = Copies(sems)
    coming = []
    for slot in range(slots):
        at = lanes(lax.rem(block_ref[0] + slot, slots) * own, own)
        bring_piece = bring(pieces_far[slot], pieces.at[slot])
        coming.append([bring(far[i].at[:, at], weight.at[slot, i]) for i in range(3)])
        coming[-1].append(bring_piece)
    middle = bring(dmid_far, dmid_ref)
    total = None
    for slot in range(slots):
        wait_all(coming[slot])
        for i in range(3):
            part = dot(pieces[slot, :, i * own : (i + 1) * own], weight[slot, i], LAST)
            total = part if total is None else total + part
    unit, scale = standardized(seg_ref[...].astype(f32))
    middle.wait()
    out_ref[...] = (
        dmid_ref[...] + norm_input_gradient(total, gain_ref[...], unit, scale)
    ).astype(bf16)


def segment_gradient(block, pieces, w_query, w_key, w_value, segment, gain, d_middle, after):
    slots = len(pieces)
    rows, width = segment.shape
    return call(
        functools.partial(segment_kernel, slots),
        "segment_gradient",
        [block]
        + [(x,) for x in pieces]
        + [segment, gain, (d_middle,), (w_query,), (w_key,), (w_value,)],
        [shape_of((rows, width))],
        scratch=[
            pltpu.VMEM((slots, 3, width, width // slots), bf16),
            pltpu.VMEM((slots, *pieces[0].shape), bf16),
            pltpu.VMEM((rows, width), f32),
        ],
        copies=4 * slots + 1,
        after=after,
        cost_us=4.8,
    )[0]


def plane_kernel(blocks, block_ref, *refs):
    chips = PLANE // 2
    left_far = refs[: 2 * PLANE]
    right_far = refs[2 * PLANE : 2 * PLANE + chips]
    out_far, first_r, first_e, out_ref, left, right, sems = refs[2 * PLANE + chips :]
    rows = left_far[0].shape[0]
    bring = Copies(sems)
    coming = [[], []]
    for i in range(2):
        for chip in range(chips):
            at = pl.ds(2 * chip * rows, 2 * rows)
            coming[i].append(bring(right_far[chip].at[i], right.at[i, at]))
        for j in range(PLANE):
            at = pl.ds(j * rows, rows)
            coming[i].append(bring(left_far[i * PLANE + j], left.at[i, at]))
    cut = out_ref.shape[3]
    width = left.shape[2]
    step = width // 4
    leaving = []
    for i in range(2):
        wait_all(coming[i])
        for at in range(0, width, step):
            value = dot(left[i, :, at : at + step], right[i], FIRST).astype(bf16)
            for part in range(step // cut):
                j = at // cut + part
                out_ref[j % blocks, i, j // blocks] = value[part * cut : (part + 1) * cut]
    leaving.append(bring(out_ref, out_far))
    start = lax.rem(block_ref[0] + blocks - 1, blocks)
    first_r[...] = out_ref[start, 0]
    first_e[...] = out_ref[start, 1]
    wait_all(leaving)


def plane_gradients(block, cots, nfs, both, blocks, cut, after):
    rows, width = cots[0].shape
    _, _, tile = both[0].shape
    out = (blocks, 2, width // (blocks * cut), cut, tile)
    return call(
        functools.partial(plane_kernel, blocks),
        "plane_gradients",
        [block] + [(x,) for x in (*cots, *nfs, *both)],
        [(shape_of(out),), shape_of(out[2:]), shape_of(out[2:])],
        scratch=[
            pltpu.VMEM(out, bf16),
            pltpu.VMEM((2, PLANE * rows, width), bf16),
            pltpu.VMEM((2, PLANE * rows, tile), bf16),
        ],
        copies=2 * PLANE + PLANE + 1,
        after=after,
        cost_us=0.1,
    )


def ring_kernel(which, k, blocks, block_ref, moved_ref, part_far, out_ref, part_ref, sems):
    bring = Copies(sems)
    piece = lax.rem(block_ref[0] + 2 * blocks - k, blocks)
    bring(part_far.at[piece, which], part_ref).wait()
    out_ref[...] = (moved_ref[...].astype(f32) + part_ref[...].astype(f32)).astype(bf16)


def ring_add(block, which, k, moved, part, after):
    blocks = part.shape[0]
    return call(
        functools.partial(ring_kernel, which, k, blocks),
        "ring_add",
        [block, moved, (part,)],
        [shape_of(moved.shape)],
        scratch=[pltpu.VMEM(moved.shape, bf16)],
        copies=1,
        after=after,
    )[0]


def compress_gradient_kernel(place_ref, pairs_own, pairs_got, comp_own, comp_got, *refs):
    outs = refs[:-2]
    left, right = refs[-2:]
    rows = pairs_own.shape[0]
    cut = left.shape[2]
    right[:rows] = comp_own[...]
    right[rows:] = comp_got[...]
    for chip in range(len(outs)):
        at = lanes((place_ref[0] ^ (2 * chip)) * cut, cut)
        left[chip, :rows] = pairs_own[:, at]
        left[chip, rows:] = pairs_got[:, at]
        outs[chip][...] = dot(left[chip], right[...], FIRST).astype(bf16)


def compress_gradient(place, pairs_own, pairs_got, comp_own, comp_got, after):
    rows, depth = pairs_own.shape
    width = comp_own.shape[1]
    chips = PLANE // 2
    cut = depth // PLANE
    return call(
        compress_gradient_kernel,
        "compress_gradient",
        [place, pairs_own, pairs_got, comp_own, comp_got],
        [shape_of((cut, width))] * chips,
        scratch=[pltpu.VMEM((chips, 2 * rows, cut), bf16), pltpu.VMEM((2 * rows, width), bf16)],
        after=after,
        cost_us=1.5,
    )


def spread_kernel(place_ref, block_ref, r_moved, e_moved, part_far, *refs):
    outs = refs[:PLANE]
    part_ref, sems = refs[PLANE:]
    bring = Copies(sems)
    bring(part_far.at[block_ref[0]], part_ref).wait()
    for j in range(PLANE):
        at = place_ref[0] ^ j
        for i, moved in enumerate((r_moved, e_moved)):
            outs[j][i] = (part_ref[i, at].astype(f32) + moved[at].astype(f32)).astype(bf16)


def spread(place, block, moved, part, after):
    count, rows, tile = moved[0].shape
    return call(
        spread_kernel,
        "spread",
        [place, block, *moved, (part,)],
        [shape_of((2, rows, tile))] * count,
        scratch=[pltpu.VMEM((2, count, rows, tile), bf16)],
        copies=1,
        after=after,
        cost_us=1.2,
    )


def last_wide_kernel(place_ref, index_ref, *refs):
    parts = refs[:PLANE]
    gain_ref, weight_far, expand_ref, reduce_ref, gain_out, weight, sems = refs[PLANE:]
    rows = weight.shape[0]
    tile = parts[0].shape[2]
    bring = Copies(sems)
    coming = bring(
        weight_far.at[pl.ds(pl.multiple_of(index_ref[0] * rows, rows), rows), :], weight
    )
    for j in range(PLANE):
        at = lanes((place_ref[0] ^ j) * tile, tile)
        reduce_ref[:, at] = parts[j][0].astype(f32)
        expand_ref[:, at] = parts[j][1].astype(f32)
    coming.wait()
    total = jnp.sum(weight[...].astype(f32) * expand_ref[...], axis=1, keepdims=True)
    gain_out[...] = total / gain_ref[...]


def last_wide(place, index, parts, gain, w_expand, after):
    _, rows, tile = parts[0].shape
    hidden = PLANE * tile
    return call(
        last_wide_kernel,
        "last_wide",
        [place, index, *parts, gain, (w_expand,)],
        [shape_of((rows, hidden), f32)] * 2 + [shape_of((rows, 1), f32)],
        scratch=[pltpu.VMEM((rows, hidden), bf16)],
        copies=1,
        after=after,
        cost_us=2.0,
    )


def on_plane(
    segment,
    memory,
    compressed,
    document_labels,
    memory_filled_count,
    norm_gain,
    w_query,
    w_key,
    w_value,
    w_output,
    ffn_gain,
    w_expand,
    w_reduce,
    w_compress,
    result_cotangent,
    compressed_cotangent,
):
    _, rows, width = segment.shape
    blocks = lax.axis_size("blk")
    block = lax.axis_index("blk")
    place = lax.axis_index("stream")
    own = width // blocks
    seg_len = rows * blocks
    part_rows = width // (PLANE * blocks)
    chips = PLANE // 2
    segment, memory, compressed = segment[0], memory[0], compressed[0]
    cotangent, comp_cotangent = result_cotangent[0], compressed_cotangent[0]
    labels, filled = document_labels[0], memory_filled_count[0]
    gain = norm_gain.reshape(1, width)
    gain_ffn = ffn_gain.reshape(1, width)
    block_ref = block.astype(jnp.int32).reshape(1)
    place_ref = place.astype(jnp.int32).reshape(1)
    index = place * blocks + block
    index_ref = index.astype(jnp.int32).reshape(1)

    def along_blk(x, shift):
        return lax.ppermute(x, "blk", [(i, (i + shift) % blocks) for i in range(blocks)])

    def along_blk_flip(x, flip):
        return lax.ppermute(x, "blk", [(i, i ^ flip) for i in range(blocks)])

    def in_plane(x, flip):
        return lax.ppermute(x, "stream", [(i, i ^ flip) for i in range(PLANE)])

    owners = lax.rem(block - jnp.arange(blocks, dtype=jnp.int32) + blocks, blocks)
    by_owner = labels.reshape(3, blocks, rows).transpose(1, 0, 2)
    kdoc = by_owner[owners].reshape(blocks, 3 * rows)
    position = owners[:, None] * rows + jnp.arange(rows, dtype=jnp.int32)[None]
    first_filled = 2 * seg_len - filled
    kpos = jnp.concatenate(
        [
            jnp.where(position >= first_filled, -1, hidden_slot),
            jnp.where(position + seg_len >= first_filled, -1, hidden_slot),
            position,
        ],
        axis=1,
    ).astype(jnp.int32)
    qdoc = kdoc[:, 2 * rows :].reshape(blocks * rows, 1)
    qpos = position.reshape(blocks * rows, 1).astype(jnp.int32)
    marks = (qdoc, qpos, kdoc, kpos)

    def hop(arrays, after):
        arrays = [gate([x], after)[0] for x in arrays]
        return arrays, [along_blk(x, 1) for x in arrays]

    weights = (w_query, w_key, w_value)
    raw = [compressed, memory, segment]
    arriving = [along_blk(x, 1) for x in raw]
    pairs = memory.reshape(rows // RATE, RATE * width)
    projected = [project(block_ref, raw, gain, *weights, width, [])]
    query = projected[0][1]
    compress_parts = compress_gradient(
        place_ref, pairs, in_plane(pairs, 1), comp_cotangent, in_plane(comp_cotangent, 1), [query]
    )
    raw, arriving = hop(arriving, [compress_parts[0]])
    projected.append(raw)
    cots = [cotangent, in_plane(cotangent, 1)]
    for j in range(1, chips):
        cots.append(in_plane(cotangent, 2 * j))
        cots.append(in_plane(cots[-1], 1))
    later = []
    for k in range(2, blocks - 1):
        raw, arriving = hop(arriving, [query])
        later.append(raw)
    compress_parts = [compress_parts[0], *gate(compress_parts[1:], raw)]
    compress_parts = [compress_parts[0]] + [
        in_plane(compress_parts[j], 2 * j) for j in range(1, chips)
    ]
    projected[1:] = [
        project(block_ref, rows3, gain, *weights, own, raw) for rows3 in projected[1:] + later
    ]
    keys, values = ([p[i] for p in projected] for i in (2, 3))
    partial = attend(query, keys, values, marks, [])
    *last, attended, middle, normed_ffn = finish(
        blocks - 1,
        block_ref,
        arriving,
        gain,
        *weights,
        own,
        query,
        partial,
        marks,
        segment,
        w_output,
        gain_ffn,
        cots[2:],
    )
    projected.append(last)
    normed, queries, keys, values = ([p[i] for p in projected] for i in range(4))

    nfs = [normed_ffn, in_plane(normed_ffn, 1)]
    for j in range(1, chips - 1):
        nfs.append(in_plane(normed_ffn, 2 * j))
        nfs.append(in_plane(nfs[-1], 1))
    new_compressed = compress(pairs, w_compress, [normed_ffn, *compress_parts[1:]])
    compress_parts = chip_add(block_ref, blocks, compress_parts, [new_compressed])
    compress_parts = [compress_parts[0]] + [
        along_blk_flip(compress_parts[k], k) for k in range(1, blocks)
    ]
    *both, res, dn, send = feed(
        place_ref,
        normed_ffn,
        nfs[1],
        cotangent,
        cots[1],
        w_expand,
        w_reduce,
        [new_compressed] + nfs[2:5:2],
    )
    sent = in_plane(send, 1)
    both = [both[0], in_plane(both[1], 2), in_plane(both[2], 4), both[3]]
    result, d_middle, d_branch, *d_attended = leave(
        block_ref,
        blocks,
        res,
        dn,
        sent,
        middle,
        cotangent,
        gain_ffn,
        w_output,
        nfs[3:6],
    )
    grads = [d_attended[0]] + [along_blk(d_attended[k], k) for k in range(1, blocks)]
    output_keep, output_give = output_gradient(
        place_ref, attended, d_branch, blocks * part_rows, both[1:3] + grads[1:3]
    )
    both[3], diagonal = gate([both[3], normed_ffn], grads[1:])
    both[3] = in_plane(both[3], 6)
    nfs.append(in_plane(diagonal, 6))
    nfs.append(in_plane(nfs[-1], 1))
    *pieces, dk, dv = attend_back(
        block_ref, queries, grads, keys, values, marks, [output_keep]
    )
    arrived = [pieces[0]] + [along_blk(pieces[k], -k) for k in range(1, blocks)]
    qkv_keep, qkv_give = heads_gradient(
        place_ref, normed, pieces, dk, dv, blocks * part_rows, [nfs[6], *compress_parts[1:]]
    )
    (output_give,) = gate([output_give], [qkv_keep])
    part, *moved = plane_gradients(block_ref, cots, nfs, both, blocks, part_rows, [qkv_keep])
    four = pair_add(
        place_ref,
        qkv_keep,
        in_plane(qkv_give, 1),
        output_keep,
        in_plane(output_give, 1),
        [*moved, *arrived[1:]],
    )
    before = four[0]
    for k in range(2, blocks):
        for i in range(2):
            moved[i] = ring_add(block_ref, i, k, along_blk(moved[i], 1), part, [before])
            before = moved[i]
    four = [four[0]] + [in_plane(four[j], 2 * j) for j in range(1, chips)]
    grad_segment = segment_gradient(
        block_ref, arrived, *weights, segment, gain, d_middle, [before]
    )
    parts = chip_add(block_ref, blocks, four, [grad_segment])
    parts = [parts[0]] + [along_blk_flip(parts[k], k) for k in range(1, blocks)]
    wide = spread(
        place_ref, block_ref, [along_blk(x, 1) for x in moved], part, [parts[0]]
    )
    wide = [wide[0]] + [in_plane(wide[j], j) for j in range(1, PLANE)]

    def mine(x):
        return lax.dynamic_slice_in_dim(x, index * part_rows, part_rows, 0).reshape(-1, 1)

    grad_compress = sum(x.astype(f32) for x in compress_parts)
    grad_query, grad_key, grad_value, grad_output, grad_norm_gain = last_heads(
        block_ref, index_ref, parts, mine(norm_gain), *weights, [grad_segment]
    )
    grad_expand, reduce_turned, grad_ffn_gain = last_wide(
        place_ref, index_ref, wide, mine(ffn_gain), w_expand, [grad_query]
    )
    return (
        result[None],
        new_compressed[None],
        grad_segment[None],
        grad_norm_gain.reshape(-1),
        grad_query,
        grad_key,
        grad_value,
        grad_output,
        grad_ffn_gain.reshape(-1),
        grad_expand,
        reduce_turned.T,
        grad_compress,
    )


def layer_norm(rows_in, gain):
    center = jnp.mean(rows_in, axis=-1, keepdims=True)
    offset = rows_in - center
    spread = jnp.mean(offset * offset, axis=-1, keepdims=True)
    return offset * lax.rsqrt(spread + epsilon) * gain


def exact_gelu(values_in):
    return jax.nn.gelu(values_in, approximate=False)


def on_any(
    segment,
    memory,
    compressed,
    document_labels,
    memory_filled_count,
    norm_gain,
    w_query,
    w_key,
    w_value,
    w_output,
    ffn_gain,
    w_expand,
    w_reduce,
    w_compress,
    result_cotangent,
    compressed_cotangent,
):
    streams, block_rows, model_width = segment.shape
    head_count = model_width // HD
    blocks = lax.axis_size("blk")
    my_block = lax.axis_index("blk")
    seg_len = block_rows * blocks
    key_count = 3 * seg_len
    score_scale = HD ** (-0.5)
    stacked = jnp.concatenate([compressed, memory, segment], axis=1).astype(jnp.float32)
    normed_full, norm_pull = jax.vjp(layer_norm, stacked, norm_gain)
    normed = normed_full.astype(jnp.bfloat16)
    seg_normed = normed[:, 2 * block_rows :]
    queries = jnp.einsum(
        "srd,de->sre", seg_normed, w_query, preferred_element_type=jnp.float32
    ).astype(jnp.bfloat16)
    query_heads = queries.reshape(streams, block_rows, head_count, HD)
    keys = jnp.einsum("srd,de->rse", normed, w_key, preferred_element_type=jnp.float32).astype(
        jnp.bfloat16
    )
    values = jnp.einsum("srd,de->rse", normed, w_value, preferred_element_type=jnp.float32).astype(
        jnp.bfloat16
    )
    all_keys, all_values = (
        lax.all_gather(keys, "blk", axis=0, tiled=True),
        lax.all_gather(values, "blk", axis=0, tiled=True),
    )
    key_index = jnp.arange(key_count, dtype=jnp.int32)
    key_owner = key_index // (3 * block_rows)
    within = key_index % (3 * block_rows)
    key_kind = within // block_rows
    key_pos = key_owner * block_rows + within % block_rows
    key_slot = key_kind * seg_len + key_pos
    key_docs = (
        document_labels.reshape(streams, 3, blocks, block_rows)
        .transpose(0, 2, 1, 3)
        .reshape(streams, key_count)
    )
    query_pos = my_block * block_rows + jnp.arange(block_rows, dtype=jnp.int32)
    query_docs = lax.dynamic_slice_in_dim(
        document_labels[:, 2], my_block * block_rows, block_rows, 1
    )
    in_memory = key_slot[None, :] >= 2 * seg_len - memory_filled_count[:, None]
    causal = key_pos[None, :] <= query_pos[:, None]
    visible = jnp.where((key_kind < 2)[None, None, :], in_memory[:, None, :], causal[None, :, :])
    allowed = visible & (key_docs[:, None, :] == query_docs[:, :, None])

    def scores_of(key_set):
        key_view = key_set.reshape(key_count, streams, head_count, HD)
        raw_scores = (
            jnp.einsum("sqhd,kshd->shqk", query_heads, key_view, preferred_element_type=jnp.float32)
            * score_scale
        )
        return jnp.where(allowed[:, None], raw_scores, masked_score)

    scores = scores_of(all_keys)
    row_top = jnp.max(scores, axis=-1, keepdims=True)
    weights = jnp.exp(scores - row_top)
    row_total = jnp.sum(weights, axis=-1, keepdims=True)
    probs = (weights / row_total).astype(jnp.bfloat16)
    log_total = row_top + jnp.log(row_total)
    value_heads = all_values.reshape(key_count, streams, head_count, HD)
    attended = jnp.einsum("shqk,kshd->sqhd", probs, value_heads, preferred_element_type=jnp.float32)
    attended = attended.reshape(streams, block_rows, model_width).astype(jnp.bfloat16)
    middle = segment.astype(jnp.float32) + jnp.einsum(
        "sre,ed->srd", attended, w_output, preferred_element_type=jnp.float32
    )
    normed_ffn_full, ffn_pull = jax.vjp(layer_norm, middle, ffn_gain)
    normed_ffn = normed_ffn_full.astype(jnp.bfloat16)
    hidden = jnp.einsum("srd,df->srf", normed_ffn, w_expand, preferred_element_type=jnp.float32)
    activated_full, gelu_pull = jax.vjp(exact_gelu, hidden)
    activated = activated_full.astype(jnp.bfloat16)
    result = (
        middle + jnp.einsum("srf,fd->srd", activated, w_reduce, preferred_element_type=jnp.float32)
    ).astype(jnp.bfloat16)
    mem_pairs = memory.reshape(streams, block_rows // RATE, RATE * model_width)
    new_compressed = jnp.einsum(
        "srp,pd->srd", mem_pairs, w_compress, preferred_element_type=jnp.float32
    ).astype(jnp.bfloat16)
    reduce_turned = jnp.einsum(
        "srd,srf->df", result_cotangent, activated, preferred_element_type=jnp.float32
    )
    d_activated = jnp.einsum(
        "srd,fd->srf", result_cotangent, w_reduce, preferred_element_type=jnp.float32
    )
    d_hidden = gelu_pull(d_activated)[0].astype(jnp.bfloat16)
    grad_expand = jnp.einsum(
        "srd,srf->df", normed_ffn, d_hidden, preferred_element_type=jnp.float32
    )
    d_normed_ffn = jnp.einsum("srf,df->srd", d_hidden, w_expand, preferred_element_type=jnp.float32)
    d_middle_norm, grad_ffn_gain = ffn_pull(d_normed_ffn)
    d_middle = result_cotangent.astype(jnp.float32) + d_middle_norm
    d_branch = d_middle.astype(jnp.bfloat16)
    grad_output = jnp.einsum("sre,srd->ed", attended, d_branch, preferred_element_type=jnp.float32)
    d_attended = jnp.einsum(
        "srd,ed->sre", d_branch, w_output, preferred_element_type=jnp.float32
    ).astype(jnp.bfloat16)
    d_attended = d_attended.reshape(streams, block_rows, head_count, HD)
    key_heads = all_keys.reshape(key_count, streams, head_count, HD)
    probs_full = jnp.exp(scores_of(all_keys) - log_total)
    probs_low = probs_full.astype(jnp.bfloat16)
    d_probs = jnp.einsum(
        "sqhd,kshd->shqk", d_attended, value_heads, preferred_element_type=jnp.float32
    )
    row_delta = jnp.sum(probs_full * d_probs, axis=-1, keepdims=True)
    d_scores = (probs_full * (d_probs - row_delta)).astype(jnp.bfloat16)
    d_queries = (
        jnp.einsum("shqk,kshd->sqhd", d_scores, key_heads, preferred_element_type=jnp.float32)
        * score_scale
    )
    d_queries = d_queries.astype(jnp.bfloat16).reshape(streams, block_rows, model_width)
    count = 3 * block_rows * lax.axis_size("blk")
    key_part = (
        jnp.einsum("shqk,sqhd->kshd", d_scores, query_heads, preferred_element_type=jnp.float32)
        * score_scale
    )
    value_part = jnp.einsum(
        "shqk,sqhd->kshd", probs_low, d_attended, preferred_element_type=jnp.float32
    )
    key_grads = lax.psum_scatter(
        jnp.stack(
            [
                key_part.reshape(count, streams, model_width),
                value_part.reshape(count, streams, model_width),
            ],
            axis=1,
        ).astype(jnp.bfloat16),
        "blk",
        scatter_dimension=0,
        tiled=True,
    ).astype(jnp.float32)
    d_keys = key_grads[:, 0].astype(jnp.bfloat16)
    d_values = key_grads[:, 1].astype(jnp.bfloat16)
    grad_query = jnp.einsum(
        "srd,sre->de", seg_normed, d_queries, preferred_element_type=jnp.float32
    )
    grad_key = jnp.einsum("srd,rse->de", normed, d_keys, preferred_element_type=jnp.float32)
    grad_value = jnp.einsum("srd,rse->de", normed, d_values, preferred_element_type=jnp.float32)
    d_normed = jnp.einsum("rse,de->srd", d_keys, w_key, preferred_element_type=jnp.float32)
    d_normed = d_normed + jnp.einsum(
        "rse,de->srd", d_values, w_value, preferred_element_type=jnp.float32
    )
    d_seg_normed = jnp.einsum("sre,de->srd", d_queries, w_query, preferred_element_type=jnp.float32)
    d_normed = d_normed + jnp.pad(d_seg_normed, ((0, 0), (2 * block_rows, 0), (0, 0)))
    d_stacked, grad_norm_gain = norm_pull(d_normed)
    grad_segment = (d_middle + d_stacked[:, 2 * block_rows :]).astype(jnp.bfloat16)
    grad_compress = jnp.einsum(
        "srp,srd->pd", mem_pairs, compressed_cotangent, preferred_element_type=jnp.float32
    )
    weight_grads = (
        grad_norm_gain,
        grad_query,
        grad_key,
        grad_value,
        grad_output,
        grad_ffn_gain,
        grad_expand,
        reduce_turned,
        grad_compress,
    )
    summed = (
        lax.psum_scatter(weight_grads[0], ("stream", "blk"), scatter_dimension=0, tiled=True),
        lax.psum_scatter(weight_grads[1], ("stream", "blk"), scatter_dimension=0, tiled=True),
        lax.psum_scatter(weight_grads[2], ("stream", "blk"), scatter_dimension=0, tiled=True),
        lax.psum_scatter(weight_grads[3], ("stream", "blk"), scatter_dimension=0, tiled=True),
        lax.psum_scatter(weight_grads[4], ("stream", "blk"), scatter_dimension=0, tiled=True),
        lax.psum_scatter(weight_grads[5], ("stream", "blk"), scatter_dimension=0, tiled=True),
        lax.psum_scatter(weight_grads[6], ("stream", "blk"), scatter_dimension=0, tiled=True),
        lax.psum_scatter(weight_grads[7], ("stream", "blk"), scatter_dimension=0, tiled=True),
        lax.psum_scatter(weight_grads[8], ("stream", "blk"), scatter_dimension=0, tiled=True),
    )
    grad_reduce = summed[7].T
    return (
        result,
        new_compressed,
        grad_segment,
        summed[0],
        summed[1],
        summed[2],
        summed[3],
        summed[4],
        summed[5],
        summed[6],
        grad_reduce,
        summed[8],
    )


def solution(mesh):
    tokens = P("stream", "blk", None)
    both = ("stream", "blk")
    in_specs = (
        (tokens,) * 3
        + (P("stream", None, None), P("stream"))
        + (P(),) * 9
        + (tokens,) * 2
    )
    out_specs = (
        (tokens,) * 3
        + (P(both),)
        + (P(both, None),) * 4
        + (P(both), P(both, None), P(None, both), P(both, None))
    )
    one_plane = mesh.shape["stream"] == PLANE
    return jax.shard_map(
        on_plane if one_plane else on_any, mesh=mesh, in_specs=in_specs, out_specs=out_specs, check_vma=False
    )
```

```python
import functools

import jax
import jax.numpy as jnp
from jax import lax
from jax.experimental import pallas as pl
from jax.experimental.pallas import tpu as pltpu
from jax.sharding import PartitionSpec as P

HD = 128
RATE = 2
PLANE = 8

epsilon = 1e-05
masked_score = -1e30
hidden_slot = 1 << 30

f32 = jnp.float32
bf16 = jnp.bfloat16
MIB = 1 << 20
FLOPS_PER_US = 0.5e9
VM = pl.BlockSpec(memory_space=pltpu.VMEM)
SM = pl.BlockSpec(memory_space=pltpu.SMEM)
ANY = pl.BlockSpec(memory_space=pl.ANY)


def dot(left, right, contract=((1,), (0,))):
    return lax.dot_general(left, right, (contract, ((), ())), preferred_element_type=f32)


def standardized(rows):
    offset = rows - jnp.mean(rows, axis=-1, keepdims=True)
    scale = lax.rsqrt(jnp.mean(offset * offset, axis=-1, keepdims=True) + epsilon)
    return offset * scale, scale


def norm_input_gradient(e, gain, unit, scale):
    eg = e * gain
    return scale * (
        eg
        - jnp.mean(eg, axis=-1, keepdims=True)
        - unit * jnp.mean(eg * unit, axis=-1, keepdims=True)
    )


LOG2E = 1.4426950408889634
SCORE_SCALE = HD ** (-0.5) * LOG2E
LAST = ((1,), (1,))
FIRST = ((0,), (0,))
TILE = 256


def block_of(shape):
    return pl.BlockSpec(shape, lambda i: (0,) * len(shape))


def call(
    kernel, name, ins, outs, scratch=(), copies=0, grant=24, after=(), cost_us=1.0
):
    in_specs, operands = [], []
    inputs = len(ins)

    def body(*refs):
        kernel(*refs[:inputs], *refs[inputs + len(after) :])

    for x in ins:
        far = isinstance(x, tuple)
        x = x[0] if far else x
        operands.append(pltpu.with_memory_space_constraint(x, pltpu.HBM) if far else x)
        in_specs.append(ANY if far else SM if x.size == 1 else block_of(x.shape))
    operands += after
    in_specs += [ANY] * len(after)
    scratch = list(scratch)
    if copies:
        scratch.append(pltpu.SemaphoreType.DMA((copies,)))
    return pl.pallas_call(
        body,
        grid=(1,),
        in_specs=in_specs,
        out_specs=[ANY if isinstance(o, tuple) else block_of(o.shape) for o in outs],
        out_shape=[
            pltpu.HBM(o[0].shape, o[0].dtype) if isinstance(o, tuple) else o for o in outs
        ],
        scratch_shapes=scratch,
        compiler_params=pltpu.CompilerParams(vmem_limit_bytes=grant * MIB),
        cost_estimate=pl.CostEstimate(
            flops=int(cost_us * FLOPS_PER_US), bytes_accessed=0, transcendentals=0
        ),
        name=name,
    )(*operands)


def gate(arrays, after):
    count = len(arrays)
    return pl.pallas_call(
        lambda *refs: None,
        in_specs=[ANY] * (count + len(after)),
        out_specs=[ANY] * count,
        out_shape=[pltpu.HBM(x.shape, x.dtype) for x in arrays],
        input_output_aliases={i: i for i in range(count)},
        compiler_params=pltpu.CompilerParams(vmem_limit_bytes=MIB),
        cost_estimate=pl.CostEstimate(flops=0, bytes_accessed=0, transcendentals=0),
        name="gate",
    )(*arrays, *after)


class Copies:
    def __init__(self, sems):
        self.sems, self.count = sems, 0

    def __call__(self, source, target):
        copy = pltpu.make_async_copy(source, target, self.sems.at[self.count])
        copy.start()
        self.count += 1
        return copy


def lanes(start, size):
    return pl.ds(pl.multiple_of(start, size), size)


def shape_of(shape, dtype=bf16):
    return jax.ShapeDtypeStruct(shape, dtype)


def norm_rows(raw, gain_ref, normed_ref):
    rows = raw.shape[1]
    for i in range(raw.shape[0]):
        unit, _ = standardized(raw[i].astype(f32))
        normed_ref[i * rows : (i + 1) * rows, :] = (unit * gain_ref[...]).astype(bf16)


ROW_CUTS = 4


def bring_rows(bring, source, target):
    step = source.shape[0] // ROW_CUTS
    return [
        bring(source.at[pl.ds(i * step, step)], target.at[pl.ds(i * step, step)])
        for i in range(ROW_CUTS)
    ]


def wait_all(copies):
    for copy in copies:
        copy.wait()


def project_kernel(all_queries, *refs):
    block_ref, *raw_refs = refs[:4]
    gain_ref, wq_ref, wk_ref, wv_ref = refs[4:8]
    outs = refs[8:12]
    wq, wk, wv, normed_ref, q_ref, k_ref, v_ref, raw, sems = refs[12:]
    bring = Copies(sems)
    width = k_ref.shape[1]
    raws = [bring(ref, raw.at[i]) for i, ref in enumerate(raw_refs)]
    coming = [bring_rows(bring, wk_ref, wk), bring_rows(bring, wv_ref, wv)]
    if all_queries:
        query_weight = bring(wq_ref, wq)
    else:
        own = q_ref.shape[1]
        query_weight = bring(wq_ref.at[:, lanes(block_ref[0] * own, own)], wq)
    wait_all(raws)
    norm_rows(raw, gain_ref, normed_ref)
    leaving = [bring(normed_ref, outs[0])]
    normed = normed_ref[...]
    for copies, weight, target, out in zip(coming, (wk, wv), (k_ref, v_ref), outs[2:]):
        wait_all(copies)
        for at in range(0, width, TILE):
            target[:, at : at + TILE] = dot(normed, weight[:, at : at + TILE]).astype(bf16)
        leaving.append(bring(target, out))
    query_weight.wait()
    q_ref[...] = dot(normed[2 * raw.shape[1] :], wq[...]).astype(bf16)
    leaving.append(bring(q_ref, outs[1]))
    wait_all(leaving)


def projected_shapes(rows, width, own):
    return [
        shape_of((3 * rows, width)),
        shape_of((rows, own)),
        shape_of((3 * rows, width)),
        shape_of((3 * rows, width)),
    ]


def project(block, raw_rows, gain, w_query, w_key, w_value, own, after):
    rows, width = raw_rows[0].shape
    shapes = projected_shapes(rows, width, own)
    weights = [(width, own), (width, width), (width, width)]
    return call(
        functools.partial(project_kernel, own == width),
        "project",
        [block] + [(x,) for x in raw_rows] + [gain, (w_query,), (w_key,), (w_value,)],
        [(x,) for x in shapes],
        scratch=[pltpu.VMEM(x, bf16) for x in weights]
        + [pltpu.VMEM(x.shape, x.dtype) for x in shapes]
        + [pltpu.VMEM((3, rows, width), bf16)],
        copies=2 * ROW_CUTS + 8,
        after=after,
        cost_us=0.1,
    )


def compress_kernel(pairs_ref, w_far, out_ref, w_ref, sems):
    bring = Copies(sems)
    count = w_ref.shape[0]
    coming = [bring(w_far.at[pl.ds(i * w_ref.shape[1], w_ref.shape[1])], w_ref.at[i]) for i in range(count)]
    total = None
    for i in range(count):
        coming[i].wait()
        part = dot(pairs_ref[:, i * w_ref.shape[1] : (i + 1) * w_ref.shape[1]], w_ref[i])
        total = part if total is None else total + part
    out_ref[...] = total.astype(bf16)


def compress(pairs, w_compress, after):
    depth, width = w_compress.shape
    count = 4
    return call(
        compress_kernel,
        "compress",
        [pairs, (w_compress,)],
        [shape_of((pairs.shape[0], width))],
        scratch=[pltpu.VMEM((count, depth // count, width), bf16)],
        copies=count,
        after=after,
        cost_us=3.2,
    )[0]


def score_bias(qdoc, qpos, kdoc_ref, kpos_ref, slot):
    allowed = (kdoc_ref[slot : slot + 1, :] == qdoc) & (kpos_ref[slot : slot + 1, :] <= qpos)
    return jnp.where(allowed, 0.0, masked_score)


def attend_kernel(slots, *refs):
    qdoc_ref, qpos_ref, kdoc_ref, kpos_ref, q_far = refs[:5]
    k_far = refs[5 : 5 + slots]
    v_far = refs[5 + slots : 5 + 2 * slots]
    out_ref, stat_ref, bias_ref, q_ref, k_ref, v_ref, sems = refs[5 + 2 * slots :]
    rows, width = q_ref.shape
    bring = Copies(sems)
    query = bring(q_far, q_ref)
    tiles = [slice(at, at + TILE) for at in range(0, width, TILE)]
    coming = [
        [
            bring(far[slot].at[:, at], near.at[slot, :, at])
            for slot in range(slots)
            for far, near in ((k_far, k_ref), (v_far, v_ref))
        ]
        for at in tiles
    ]
    qdoc, qpos = qdoc_ref[:rows, :], qpos_ref[:rows, :]
    for slot in range(slots):
        bias_ref[slot] = score_bias(qdoc, qpos, kdoc_ref, kpos_ref, slot)
    query.wait()
    lane = lax.broadcasted_iota(jnp.int32, (rows, HD), 1)
    stats = jnp.zeros((rows, HD), f32)
    heads = width // HD
    for head in range(heads):
        if head * HD % TILE == 0:
            for copy in coming[head * HD // TILE]:
                copy.wait()
        at = slice(head * HD, (head + 1) * HD)
        q = q_ref[:, at]
        scores = [
            dot(q, k_ref[slot, :, at], LAST) * SCORE_SCALE + bias_ref[slot]
            for slot in range(slots)
        ]
        top = functools.reduce(jnp.maximum, scores)
        top = jnp.max(top, axis=-1, keepdims=True)
        weights = [jnp.exp2(s - top) for s in scores]
        total = jnp.sum(functools.reduce(jnp.add, weights), axis=-1, keepdims=True)
        out_ref[:, at] = functools.reduce(
            jnp.add,
            [dot(weights[slot].astype(bf16), v_ref[slot, :, at]) for slot in range(slots)],
        )
        stats = jnp.where(lane == head, top, stats)
        stats = jnp.where(lane == heads + head, total, stats)
    stat_ref[...] = stats


def attend(query, keys, values, marks, after):
    slots = len(keys)
    rows, width = query.shape
    key_rows = keys[0].shape[0]
    return call(
        functools.partial(attend_kernel, slots),
        "attend",
        [*marks, (query,)] + [(x,) for x in (*keys, *values)],
        [shape_of((rows, width), f32), shape_of((rows, HD), f32)],
        scratch=[
            pltpu.VMEM((slots, rows, key_rows), f32),
            pltpu.VMEM((rows, width), bf16),
            pltpu.VMEM((slots, key_rows, width), bf16),
            pltpu.VMEM((slots, key_rows, width), bf16),
        ],
        copies=1 + 2 * slots * (width // TILE),
        after=after,
        cost_us=0.1,
    )


def finish_kernel(slot, *refs):
    block_ref, *raw_refs = refs[:4]
    gain_ref, wq_far, wk_far, wv_far = refs[4:8]
    query_far, sum_ref, stat_ref, qdoc_ref, qpos_ref, kdoc_ref, kpos_ref = refs[8:15]
    seg_ref, wo_far, gain_ffn_ref = refs[15:18]
    outs = refs[18:23]
    middle_ref, nf_ref = refs[23:25]
    wq, wk, wv, normed_ref, q_ref, k_ref, v_ref, wo, query_ref, att_ref, raw, sems = refs[25:]
    rows, width = query_ref.shape
    bring = Copies(sems)
    raws = [bring(ref, raw.at[i]) for i, ref in enumerate(raw_refs)]
    coming = [bring_rows(bring, wk_far, wk), bring_rows(bring, wv_far, wv)]
    query = bring(query_far, query_ref)
    output_weight = bring(wo_far, wo)
    own = q_ref.shape[1]
    query_weight = bring(wq_far.at[:, lanes(block_ref[0] * own, own)], wq)
    bias = score_bias(qdoc_ref[:rows, :], qpos_ref[:rows, :], kdoc_ref, kpos_ref, slot)
    wait_all(raws)
    norm_rows(raw, gain_ref, normed_ref)
    leaving = [bring(normed_ref, outs[0])]
    normed = normed_ref[...]
    query.wait()
    heads = width // HD
    for copies, weight, target, out in zip(coming, (wk, wv), (k_ref, v_ref), outs[2:4]):
        wait_all(copies)
        for at in range(0, width, TILE):
            target[:, at : at + TILE] = dot(normed, weight[:, at : at + TILE]).astype(bf16)
        leaving.append(bring(target, out))
    group = 4
    for start in range(0, heads, group):
        some = range(start, start + group)
        at = {h: slice(h * HD, (h + 1) * HD) for h in some}
        scores = {
            h: dot(query_ref[:, at[h]], k_ref[:, at[h]], LAST) * SCORE_SCALE + bias for h in some
        }
        before = {h: stat_ref[:, h : h + 1] for h in some}
        top = {
            h: jnp.maximum(before[h], jnp.max(scores[h], axis=-1, keepdims=True)) for h in some
        }
        weights = {h: jnp.exp2(scores[h] - top[h]) for h in some}
        shrink = {h: jnp.exp2(before[h] - top[h]) for h in some}
        total = {
            h: stat_ref[:, heads + h : heads + h + 1] * shrink[h]
            + jnp.sum(weights[h], axis=-1, keepdims=True)
            for h in some
        }
        out = {
            h: sum_ref[:, at[h]] * shrink[h] + dot(weights[h].astype(bf16), v_ref[:, at[h]])
            for h in some
        }
        for h in some:
            att_ref[:, at[h]] = (out[h] * (1.0 / total[h])).astype(bf16)
    query_weight.wait()
    q_ref[...] = dot(normed[2 * raw.shape[1] :], wq[...]).astype(bf16)
    leaving.append(bring(q_ref, outs[1]))
    leaving.append(bring(att_ref, outs[4]))
    output_weight.wait()
    middle = seg_ref[...].astype(f32) + dot(att_ref[...], wo[...])
    middle_ref[...] = middle
    unit, _ = standardized(middle)
    nf_ref[...] = (unit * gain_ffn_ref[...]).astype(bf16)
    wait_all(leaving)


def finish(
    slot, block, raw_rows, gain, w_query, w_key, w_value, own, query, partial, marks, segment, w_output, gain_ffn, after
):
    rows, width = segment.shape
    shapes = projected_shapes(rows, width, own)
    weights = [(width, own), (width, width), (width, width)]
    return call(
        functools.partial(finish_kernel, slot),
        "finish",
        [block] + [(x,) for x in raw_rows] + [gain, (w_query,), (w_key,), (w_value,), (query,), *partial, *marks]
        + [segment, (w_output,), gain_ffn],
        [(x,) for x in shapes]
        + [(shape_of((rows, width)),), shape_of((rows, width), f32), shape_of((rows, width))],
        scratch=[pltpu.VMEM(x, bf16) for x in weights]
        + [pltpu.VMEM(x.shape, x.dtype) for x in shapes]
        + [
            pltpu.VMEM((width, width), bf16),
            pltpu.VMEM((rows, width), bf16),
            pltpu.VMEM((rows, width), bf16),
            pltpu.VMEM((3, rows, width), bf16),
        ],
        copies=2 * ROW_CUTS + 11,
        after=after,
        cost_us=0.1,
    )


def feed_kernel(chips, place_ref, nf_own, nf_got, cot_own, cot_got, we_far, wr_far, *refs):
    both_far = refs[:chips]
    res_ref, dn_ref, send_ref, nf_ref, cot_ref, both, we, wr, res, dn, sems = refs[chips:]
    rows = nf_own.shape[0]
    tile = wr.shape[1]
    bring = Copies(sems)
    coming = []
    for chip in range(chips):
        at = lanes((place_ref[0] ^ (2 * chip)) * tile, tile)
        coming.append(bring(we_far.at[:, at], we.at[chip]))
        coming.append(bring(wr_far.at[at, :], wr.at[chip]))
    nf_ref[:rows] = nf_own[...]
    nf_ref[rows:] = nf_got[...]
    cot_ref[:rows] = cot_own[...]
    cot_ref[rows:] = cot_got[...]
    res[...] = jnp.zeros_like(res)
    dn[...] = jnp.zeros_like(dn)
    part = tile // 2

    @pl.loop(0, chips)
    def _(chip):
        pltpu.make_async_copy(we.at[chip], we.at[chip], sems.at[2 * chip]).wait()
        pltpu.make_async_copy(wr.at[chip], wr.at[chip], sems.at[2 * chip + 1]).wait()
        for at in range(0, tile, part):
            here = slice(at, at + part)
            hidden = dot(nf_ref[...], we[chip, :, here])
            d_act = dot(cot_ref[...], wr[chip, here, :], LAST)
            cdf = 0.5 + 0.5 * lax.erf(hidden * (0.5**0.5))
            density = jnp.exp2(hidden * hidden * (-0.5 * LOG2E)) * 0.3989422804014327
            both[chip, 0, :, here] = (hidden * cdf).astype(bf16)
            both[chip, 1, :, here] = (d_act * (cdf + hidden * density)).astype(bf16)
        res[...] += dot(both[chip, 0], wr[chip])
        dn[...] += dot(both[chip, 1], we[chip], LAST)

    leaving = [bring(both.at[chip], both_far[chip]) for chip in range(chips)]
    res_ref[...] = res[:rows]
    dn_ref[...] = dn[:rows]
    send_ref[0] = res[rows:].astype(bf16)
    send_ref[1] = dn[rows:].astype(bf16)
    wait_all(leaving)


def feed(place, nf_own, nf_got, cot_own, cot_got, w_expand, w_reduce, after):
    rows, width = nf_own.shape
    chips = PLANE // 2
    tile = w_expand.shape[1] // PLANE
    return call(
        functools.partial(feed_kernel, chips),
        "feed",
        [place, nf_own, nf_got, cot_own, cot_got, (w_expand,), (w_reduce,)],
        [(shape_of((2, 2 * rows, tile)),)] * chips
        + [shape_of((rows, width), f32)] * 2
        + [shape_of((2, rows, width))],
        scratch=[
            pltpu.VMEM((2 * rows, width), bf16),
            pltpu.VMEM((2 * rows, width), bf16),
            pltpu.VMEM((chips, 2, 2 * rows, tile), bf16),
            pltpu.VMEM((chips, width, tile), bf16),
            pltpu.VMEM((chips, tile, width), bf16),
            pltpu.VMEM((2 * rows, width), f32),
            pltpu.VMEM((2 * rows, width), f32),
        ],
        copies=3 * chips,
        grant=28,
        after=after,
        cost_us=0.1,
    )


def leave_kernel(slots, block_ref, *refs):
    res_ref, dn_ref, got_ref, middle_ref, cot_ref, gain_ref, wo_far = refs[:7]
    result_ref, dmid_far, branch_far = refs[7:10]
    datt_refs = refs[10 : 10 + slots]
    wo, dmid_ref, branch_ref, sems = refs[10 + slots :]
    own = wo.shape[1]
    bring = Copies(sems)
    coming = [
        bring(wo_far.at[lanes(lax.rem(block_ref[0] + slot, slots) * own, own), :], wo.at[slot])
        for slot in range(slots)
    ]
    middle = middle_ref[...]
    result_ref[...] = (middle + (res_ref[...] + got_ref[0].astype(f32))).astype(bf16)
    unit, scale = standardized(middle)
    d_normed = dn_ref[...] + got_ref[1].astype(f32)
    d_mid = cot_ref[...].astype(f32) + norm_input_gradient(d_normed, gain_ref[...], unit, scale)
    dmid_ref[...] = d_mid
    branch = d_mid.astype(bf16)
    branch_ref[...] = branch
    leaving = [bring(dmid_ref, dmid_far), bring(branch_ref, branch_far)]
    for slot in range(slots):
        coming[slot].wait()
        datt_refs[slot][...] = dot(branch, wo[slot], LAST).astype(bf16)
    wait_all(leaving)


def leave(block, slots, res, dn, got, middle, cotangent, gain, w_output, after):
    rows, width = middle.shape
    own = width // slots
    return call(
        functools.partial(leave_kernel, slots),
        "leave",
        [block, res, dn, got, middle, cotangent, gain, (w_output,)],
        [shape_of((rows, width)), (shape_of((rows, width), f32),), (shape_of((rows, width)),)]
        + [shape_of((rows, own))] * slots,
        scratch=[
            pltpu.VMEM((slots, own, width), bf16),
            pltpu.VMEM((rows, width), f32),
            pltpu.VMEM((rows, width), bf16),
        ],
        copies=slots + 2,
        after=after,
        cost_us=3.8,
    )


def attend_back_kernel(slots, heads, block_ref, *refs):
    take = iter(refs)
    marks = [next(take) for _ in range(4)]
    g_refs = [next(take) for _ in range(slots)]
    q_far = [next(take) for _ in range(slots)]
    k_far = [next(take) for _ in range(slots)]
    v_far = [next(take) for _ in range(slots)]
    piece_far = [next(take) for _ in range(slots)]
    dk_far, dv_far, q_ref, k_ref, v_ref, piece_refs, dk_ref, dv_ref, sems = take
    qdoc_ref, qpos_ref, kdoc_ref, kpos_ref = marks
    scale = HD ** (-0.5)
    rows = g_refs[0].shape[0]
    own = heads * HD
    bring = Copies(sems)
    owned = lanes(block_ref[0] * own, own)
    coming = []
    for slot in range(slots):
        coming.append(bring(q_far[slot].at[:, owned] if slot == 0 else q_far[slot], q_ref.at[slot]))
        coming.append(bring(k_far[slot].at[:, owned], k_ref.at[slot]))
        coming.append(bring(v_far[slot].at[:, owned], v_ref.at[slot]))
    for copy in coming:
        copy.wait()
    dk = [[None] * slots for _ in range(heads)]
    dv = [[None] * slots for _ in range(heads)]
    for one in range(slots):
        here = slice(one * rows, (one + 1) * rows)
        qdoc, qpos = qdoc_ref[here, :], qpos_ref[here, :]
        bias = [score_bias(qdoc, qpos, kdoc_ref, kpos_ref, slot) for slot in range(slots)]
        for head in range(heads):
            at = slice(head * HD, (head + 1) * HD)
            q = q_ref[one, :, at]
            grad = g_refs[one][:, at]
            scores = [
                dot(q, k_ref[slot, :, at], LAST) * SCORE_SCALE + bias[slot]
                for slot in range(slots)
            ]
            top = jnp.max(functools.reduce(jnp.maximum, scores), axis=-1, keepdims=True)
            weights = [jnp.exp2(s - top) for s in scores]
            total = jnp.sum(functools.reduce(jnp.add, weights), axis=-1, keepdims=True)
            inverse = 1.0 / total
            probs = [w * inverse for w in weights]
            d_probs = [dot(grad, v_ref[slot, :, at], LAST) for slot in range(slots)]
            delta = jnp.sum(
                functools.reduce(jnp.add, [p * d for p, d in zip(probs, d_probs)]),
                axis=-1,
                keepdims=True,
            )
            dq = None
            for slot in range(slots):
                d_score = (probs[slot] * (d_probs[slot] - delta)).astype(bf16)
                part = dot(d_score, k_ref[slot, :, at])
                dq = part if dq is None else dq + part
                dk_part = dot(d_score, q, FIRST)
                dv_part = dot(probs[slot].astype(bf16), grad, FIRST)
                dk[head][slot] = dk_part if one == 0 else dk[head][slot] + dk_part
                dv[head][slot] = dv_part if one == 0 else dv[head][slot] + dv_part
            piece_refs[one, :, at] = (dq * scale).astype(bf16)
    leaving = []
    for slot in range(slots):
        for head in range(heads):
            at = slice(head * HD, (head + 1) * HD)
            d_key = (dk[head][slot] * scale).astype(bf16)
            d_value = dv[head][slot].astype(bf16)
            dk_ref[slot, :, at] = d_key
            dv_ref[slot, :, at] = d_value
            for i, value in enumerate((d_key, d_value)):
                first = (i + 1) * own + head * HD
                piece_refs[slot, :, first : first + HD] = value[2 * rows :]
        leaving.append(bring(piece_refs.at[slot], piece_far[slot]))
    leaving += [bring(dk_ref, dk_far), bring(dv_ref, dv_far)]
    wait_all(leaving)


def attend_back(block, queries, grads, keys, values, marks, after):
    slots = len(keys)
    key_rows = keys[0].shape[0]
    rows, own = grads[0].shape
    heads = own // HD
    return call(
        functools.partial(attend_back_kernel, slots, heads),
        "attend_back",
        [block, *marks, *grads] + [(x,) for x in (*queries, *keys, *values)],
        [(shape_of((rows, 3 * own)),)] * slots + [(shape_of((slots, key_rows, own)),)] * 2,
        scratch=[
            pltpu.VMEM((slots, rows, own), bf16),
            pltpu.VMEM((slots, key_rows, own), bf16),
            pltpu.VMEM((slots, key_rows, own), bf16),
            pltpu.VMEM((slots, rows, 3 * own), bf16),
            pltpu.VMEM((slots, key_rows, own), bf16),
            pltpu.VMEM((slots, key_rows, own), bf16),
        ],
        copies=4 * slots + 2,
        after=after,
        cost_us=4.0,
    )


def heads_kernel(slots, place_ref, *refs):
    piece_far = refs[:slots]
    normed_far = refs[slots : 2 * slots]
    dk_far, dv_far = refs[2 * slots : 2 * slots + 2]
    keep_far, give_ref, out_ref, pieces, normed, dk, dv, sems = refs[2 * slots + 2 :]
    own = dk.shape[2]
    rows = pieces.shape[1]
    cut = out_ref.shape[2]
    core = lax.rem(place_ref[0], 2)
    bring = Copies(sems)
    second = [bring(normed_far[0], normed.at[0]), bring(dv_far, dv)]
    second += [bring(normed_far[slot], normed.at[slot]) for slot in range(1, slots)]
    third = [bring(dk_far, dk)]
    fourth = [bring(piece_far[slot], pieces.at[slot]) for slot in range(slots)]
    leaving = []

    def store(value, at):
        value = value.astype(bf16)
        here = slice(at, at + value.shape[1])
        for j in range(value.shape[0] // cut):
            out_ref[j % 2, j // 2, :, here] = value[j * cut : (j + 1) * cut]
        here = pl.ds(at, value.shape[1])
        give_ref[:, :, here] = out_ref[1 - core, :, :, here]
        leaving.append(bring(out_ref.at[core, :, :, here], keep_far.at[:, :, here]))

    def over_slots(part):
        total = part(0)
        for slot in range(1, slots):
            total = total + part(slot)
        return total

    wait_all(second)
    store(over_slots(lambda slot: dot(normed[slot], dv[slot], FIRST)), 2 * own)
    wait_all(third)
    store(over_slots(lambda slot: dot(normed[slot], dk[slot], FIRST)), own)
    wait_all(fourth)
    store(over_slots(lambda slot: dot(normed[slot, 2 * rows :], pieces[slot, :, :own], FIRST)), 0)
    wait_all(leaving)


def heads_gradient(place, normed, pieces, dk, dv, cut, after):
    slots, key_rows, own = dk.shape
    rows = pieces[0].shape[0]
    width = normed[0].shape[1]
    half = (width // cut // 2, cut, 3 * own)
    return call(
        functools.partial(heads_kernel, slots),
        "heads_gradient",
        [place] + [(x,) for x in (*pieces, *normed, dk, dv)],
        [(shape_of(half),), shape_of(half)],
        scratch=[
            pltpu.VMEM((2, *half), bf16),
            pltpu.VMEM((slots, *pieces[0].shape), bf16),
            pltpu.VMEM((slots, key_rows, width), bf16),
            pltpu.VMEM((slots, key_rows, own), bf16),
            pltpu.VMEM((slots, key_rows, own), bf16),
        ],
        copies=2 * slots + 5,
        after=after,
        grant=36,
        cost_us=0.1,
    )


def other_kernel(slots, place_ref, block_ref, att_far, branch_far, *refs):
    mem_far = refs[:slots]
    comp_far = refs[slots : 2 * slots]
    keep_far, give_ref, out_ref, att, branch, mem, comp, apart, rows_ref, sems = refs[2 * slots :]
    core = lax.rem(place_ref[0], 2)
    _, chips, cut, _ = out_ref.shape
    bring = Copies(sems)
    first = [bring(att_far, att), bring(branch_far, branch)]
    rows, width = att.shape
    pairs = comp.shape[1]
    second = []
    for slot in range(slots):
        second.append(bring(mem_far[slot], mem.at[pl.ds(slot * rows, rows)]))
        second.append(bring(comp_far[slot], comp.at[slot]))
    wait_all(first)
    for i in range(chips):
        at = slice(2 * i * cut, 2 * (i + 1) * cut)
        value = dot(att[:, at], branch[...], FIRST).astype(bf16)
        for j in range(2):
            out_ref[j, i, :, :width] = value[j * cut : (j + 1) * cut]
    wait_all(second)
    row = lax.broadcasted_iota(jnp.int32, (rows, pairs), 0)
    column = lax.broadcasted_iota(jnp.int32, (rows, pairs), 1)
    groups = PLANE // RATE
    step = width // groups
    part = step // slots
    wide = width // 2
    for i in range(RATE):
        chosen = (row == column * RATE + i).astype(f32).astype(bf16)
        for slot in range(slots):
            apart[slot * rows : (slot + 1) * rows] = dot(chosen, comp[slot]).astype(bf16)
        for group in range(groups):
            rows_ref[...] = dot(mem[:, group * step : (group + 1) * step], apart[...], FIRST)
            value = rows_ref[pl.ds(pl.multiple_of(block_ref[0] * part, part), part), :]
            value = value.astype(bf16)
            owner = i * groups + group
            for k in range(cut // part):
                out_ref[owner % 2, owner // 2, k * part : (k + 1) * part, width:] = value[
                    :, k * wide : (k + 1) * wide
                ]
    give_ref[...] = out_ref[1 - core]
    bring(out_ref.at[core], keep_far).wait()


def other_gradients(place, block, attended, branch, memories, comps, cut, after):
    slots = len(memories)
    rows, width = attended.shape
    pairs = comps[0].shape[0]
    half = (width // cut // 2, cut, width + width // 2)
    return call(
        functools.partial(other_kernel, slots),
        "other_gradients",
        [place, block] + [(x,) for x in (attended, branch, *memories, *comps)],
        [(shape_of(half),), shape_of(half)],
        scratch=[
            pltpu.VMEM((2, *half), bf16),
            pltpu.VMEM((rows, width), bf16),
            pltpu.VMEM((rows, width), bf16),
            pltpu.VMEM((slots * rows, width), bf16),
            pltpu.VMEM((slots, pairs, width), bf16),
            pltpu.VMEM((slots * rows, width), bf16),
            pltpu.VMEM((width * RATE // PLANE, width), f32),
        ],
        copies=3 + 2 * slots,
        after=after,
        cost_us=0.1,
    )


def pair_add_kernel(place_ref, *refs):
    keep_far = refs[:2]
    got = refs[2:4]
    outs = refs[4:8]
    near = refs[8:10]
    total, sems = refs[10:]
    bring = Copies(sems)
    chip = place_ref[0] // 2
    order = [1, 2, 3, 0]
    coming = {j: [bring(f.at[chip ^ j], n.at[j]) for f, n in zip(keep_far, near)] for j in order}
    leaving = []
    width = near[0].shape[2]
    for j in order:
        wait_all(coming[j])
        for at, a, b in zip((slice(0, width), slice(width, None)), near, got):
            total[j, :, at] = (a[j].astype(f32) + b[chip ^ j].astype(f32)).astype(bf16)
        leaving.append(bring(total.at[j], outs[j]))
    wait_all(leaving)


def pair_add(place, qkv_keep, qkv_got, output_keep, output_got, after):
    chips, rows, width = qkv_keep.shape
    wide = output_keep.shape[2]
    return call(
        pair_add_kernel,
        "pair_add",
        [place, (qkv_keep,), (output_keep,), qkv_got, output_got],
        [(shape_of((rows, width + wide)),)] * chips,
        scratch=[
            pltpu.VMEM(qkv_keep.shape, bf16),
            pltpu.VMEM(output_keep.shape, bf16),
            pltpu.VMEM((chips, rows, width + wide), bf16),
        ],
        copies=3 * chips,
        after=after,
        cost_us=3.0,
    )


def chip_add_kernel(chips, block_ref, *refs):
    pieces = refs[:chips]
    outs = refs[chips:-2]
    compress_ref, total = refs[-2:]
    total[...] = sum(p[...].astype(f32) for p in pieces)
    blocks = len(outs)
    rows = total.shape[0] // blocks
    width = outs[0].shape[1]
    for k in range(blocks):
        outs[k][...] = total[lanes((block_ref[0] ^ k) * rows, rows), :width].astype(bf16)
    part, wide = compress_ref.shape[0], total.shape[1] - width
    for i in range(total.shape[0] // part):
        compress_ref[:, i * wide : (i + 1) * wide] = total[i * part : (i + 1) * part, width:]


def chip_add(block, blocks, pieces, width, after):
    rows, total = pieces[0].shape
    wide = 2 * (total - width)
    return call(
        functools.partial(chip_add_kernel, len(pieces)),
        "chip_add",
        [block, *pieces],
        [shape_of((rows // blocks, width))] * blocks
        + [shape_of((rows * (total - width) // wide, wide), f32)],
        scratch=[pltpu.VMEM((rows, total), f32)],
        after=after,
        cost_us=0.1,
    )


def as_row(column):
    return jnp.transpose(jnp.broadcast_to(column, (column.shape[0], HD)))[:1]


def last_heads_kernel(blocks, block_ref, *refs):
    parts = refs[:blocks]
    gain_ref = refs[blocks]
    weights_far = refs[blocks + 1 : blocks + 4]
    at_ref = refs[blocks + 4]
    outs = refs[blocks + 5 : blocks + 8]
    output_ref, norm_ref, weights, sems = refs[blocks + 8 :]
    rows, width = output_ref.shape
    own = width // blocks
    bring = Copies(sems)
    here = pl.ds(pl.multiple_of(at_ref[0] * rows, rows), rows)
    coming = [bring(far.at[here, :], weights.at[i]) for i, far in enumerate(weights_far)]
    for k in range(blocks):
        at = lanes((block_ref[0] ^ k) * own, own)
        for i in range(3):
            outs[i][:, at] = parts[k][:, i * own : (i + 1) * own].astype(f32)
    first = 3 * own
    output_ref[...] = sum(p[:, first : first + width].astype(f32) for p in parts)
    wait_all(coming)
    total = sum(weights[i].astype(f32) * outs[i][...] for i in range(3))
    norm_ref[...] = as_row(jnp.sum(total, axis=1, keepdims=True)) / gain_ref[...]


def last_heads(block, index, parts, gain, w_query, w_key, w_value, after):
    blocks = len(parts)
    rows = parts[0].shape[0]
    width = w_query.shape[0]
    return call(
        functools.partial(last_heads_kernel, blocks),
        "last_heads",
        [block, *parts, gain, (w_query,), (w_key,), (w_value,), index],
        [shape_of((rows, width), f32)] * 4 + [shape_of((1, rows), f32)],
        scratch=[pltpu.VMEM((3, rows, width), bf16)],
        copies=3,
        after=after,
        cost_us=1.8,
    )


def segment_kernel(slots, block_ref, *refs):
    pieces_far = refs[:slots]
    seg_ref, gain_ref, dmid_far = refs[slots : slots + 3]
    far = refs[slots + 3 : slots + 6]
    out_ref, weight, pieces, dmid_ref, sems = refs[slots + 6 :]
    own = pieces.shape[2] // 3
    bring = Copies(sems)
    coming = []
    for slot in range(slots):
        at = lanes(lax.rem(block_ref[0] + slot, slots) * own, own)
        bring_piece = bring(pieces_far[slot], pieces.at[slot])
        coming.append([bring(far[i].at[:, at], weight.at[slot, i]) for i in range(3)])
        coming[-1].append(bring_piece)
    middle = bring(dmid_far, dmid_ref)
    total = None
    for slot in range(slots):
        wait_all(coming[slot])
        for i in range(3):
            part = dot(pieces[slot, :, i * own : (i + 1) * own], weight[slot, i], LAST)
            total = part if total is None else total + part
    unit, scale = standardized(seg_ref[...].astype(f32))
    middle.wait()
    out_ref[...] = (
        dmid_ref[...] + norm_input_gradient(total, gain_ref[...], unit, scale)
    ).astype(bf16)


def segment_gradient(block, pieces, w_query, w_key, w_value, segment, gain, d_middle, after):
    slots = len(pieces)
    rows, width = segment.shape
    return call(
        functools.partial(segment_kernel, slots),
        "segment_gradient",
        [block]
        + [(x,) for x in pieces]
        + [segment, gain, (d_middle,), (w_query,), (w_key,), (w_value,)],
        [shape_of((rows, width))],
        scratch=[
            pltpu.VMEM((slots, 3, width, width // slots), bf16),
            pltpu.VMEM((slots, *pieces[0].shape), bf16),
            pltpu.VMEM((rows, width), f32),
        ],
        copies=4 * slots + 1,
        after=after,
        cost_us=0.1,
    )[0]


def plane_kernel(blocks, block_ref, *refs):
    chips = PLANE // 2
    left_far = refs[: 2 * PLANE]
    right_far = refs[2 * PLANE : 2 * PLANE + chips]
    out_far, first_r, first_e, out_ref, left, right, sems = refs[2 * PLANE + chips :]
    rows = left_far[0].shape[0]
    bring = Copies(sems)
    coming = [[], []]
    for i in range(2):
        for chip in range(chips):
            at = pl.ds(2 * chip * rows, 2 * rows)
            coming[i].append(bring(right_far[chip].at[i], right.at[i, at]))
        for j in range(PLANE):
            at = pl.ds(j * rows, rows)
            coming[i].append(bring(left_far[i * PLANE + j], left.at[i, at]))
    cut = out_ref.shape[3]
    width = left.shape[2]
    step = width // 4
    leaving = []
    for i in range(2):
        wait_all(coming[i])
        for at in range(0, width, step):
            value = dot(left[i, :, at : at + step], right[i], FIRST).astype(bf16)
            for part in range(step // cut):
                j = at // cut + part
                out_ref[j % blocks, i, j // blocks] = value[part * cut : (part + 1) * cut]
    leaving.append(bring(out_ref, out_far))
    start = lax.rem(block_ref[0] + blocks - 1, blocks)
    first_r[...] = out_ref[start, 0]
    first_e[...] = out_ref[start, 1]
    wait_all(leaving)


def plane_gradients(block, cots, nfs, both, blocks, cut, after):
    rows, width = cots[0].shape
    _, _, tile = both[0].shape
    out = (blocks, 2, width // (blocks * cut), cut, tile)
    return call(
        functools.partial(plane_kernel, blocks),
        "plane_gradients",
        [block] + [(x,) for x in (*cots, *nfs, *both)],
        [(shape_of(out),), shape_of(out[2:]), shape_of(out[2:])],
        scratch=[
            pltpu.VMEM(out, bf16),
            pltpu.VMEM((2, PLANE * rows, width), bf16),
            pltpu.VMEM((2, PLANE * rows, tile), bf16),
        ],
        copies=2 * PLANE + PLANE + 1,
        after=after,
        cost_us=80.0,
    )


def ring_kernel(which, k, blocks, block_ref, moved_ref, part_far, out_ref, part_ref, sems):
    bring = Copies(sems)
    piece = lax.rem(block_ref[0] + 2 * blocks - k, blocks)
    bring(part_far.at[piece, which], part_ref).wait()
    out_ref[...] = (moved_ref[...].astype(f32) + part_ref[...].astype(f32)).astype(bf16)


def ring_add(block, which, k, moved, part, after):
    blocks = part.shape[0]
    return call(
        functools.partial(ring_kernel, which, k, blocks),
        "ring_add",
        [block, moved, (part,)],
        [shape_of(moved.shape)],
        scratch=[pltpu.VMEM(moved.shape, bf16)],
        copies=1,
        after=after,
        cost_us=0.1,
    )[0]


def spread_kernel(place_ref, block_ref, r_moved, e_moved, part_far, *refs):
    outs = refs[:PLANE]
    part_ref, sems = refs[PLANE:]
    bring = Copies(sems)
    bring(part_far.at[block_ref[0]], part_ref).wait()
    for j in range(PLANE):
        at = place_ref[0] ^ j
        for i, moved in enumerate((r_moved, e_moved)):
            outs[j][i] = (part_ref[i, at].astype(f32) + moved[at].astype(f32)).astype(bf16)


def spread(place, block, moved, part, after):
    count, rows, tile = moved[0].shape
    return call(
        spread_kernel,
        "spread",
        [place, block, *moved, (part,)],
        [shape_of((2, rows, tile))] * count,
        scratch=[pltpu.VMEM((2, count, rows, tile), bf16)],
        copies=1,
        after=after,
        cost_us=1.2,
    )


def last_wide_kernel(place_ref, index_ref, *refs):
    parts = refs[:PLANE]
    gain_ref, weight_far, expand_ref, reduce_ref, gain_out, weight, sems = refs[PLANE:]
    rows = weight.shape[0]
    tile = parts[0].shape[2]
    bring = Copies(sems)
    coming = bring(
        weight_far.at[pl.ds(pl.multiple_of(index_ref[0] * rows, rows), rows), :], weight
    )
    for j in range(PLANE):
        at = lanes((place_ref[0] ^ j) * tile, tile)
        reduce_ref[:, at] = parts[j][0].astype(f32)
        expand_ref[:, at] = parts[j][1].astype(f32)
    coming.wait()
    total = jnp.sum(weight[...].astype(f32) * expand_ref[...], axis=1, keepdims=True)
    gain_out[...] = as_row(total) / gain_ref[...]


def last_wide(place, index, parts, gain, w_expand, after):
    _, rows, tile = parts[0].shape
    hidden = PLANE * tile
    return call(
        last_wide_kernel,
        "last_wide",
        [place, index, *parts, gain, (w_expand,)],
        [shape_of((rows, hidden), f32)] * 2 + [shape_of((1, rows), f32)],
        scratch=[pltpu.VMEM((rows, hidden), bf16)],
        copies=1,
        after=after,
        cost_us=2.0,
    )


def on_plane(
    segment,
    memory,
    compressed,
    document_labels,
    memory_filled_count,
    norm_gain,
    w_query,
    w_key,
    w_value,
    w_output,
    ffn_gain,
    w_expand,
    w_reduce,
    w_compress,
    result_cotangent,
    compressed_cotangent,
):
    _, rows, width = segment.shape
    blocks = lax.axis_size("blk")
    block = lax.axis_index("blk")
    place = lax.axis_index("stream")
    own = width // blocks
    seg_len = rows * blocks
    part_rows = width // (PLANE * blocks)
    chips = PLANE // 2
    segment, memory, compressed = segment[0], memory[0], compressed[0]
    cotangent, comp_cotangent = result_cotangent[0], compressed_cotangent[0]
    labels, filled = document_labels[0], memory_filled_count[0]
    gain = norm_gain.reshape(1, width)
    gain_ffn = ffn_gain.reshape(1, width)
    block_ref = block.astype(jnp.int32).reshape(1)
    place_ref = place.astype(jnp.int32).reshape(1)
    index = place * blocks + block
    index_ref = index.astype(jnp.int32).reshape(1)

    def along_blk(x, shift):
        return lax.ppermute(x, "blk", [(i, (i + shift) % blocks) for i in range(blocks)])

    def along_blk_flip(x, flip):
        return lax.ppermute(x, "blk", [(i, i ^ flip) for i in range(blocks)])

    def in_plane(x, flip):
        return lax.ppermute(x, "stream", [(i, i ^ flip) for i in range(PLANE)])

    owners = lax.rem(block - jnp.arange(blocks, dtype=jnp.int32) + blocks, blocks)
    by_owner = labels.reshape(3, blocks, rows).transpose(1, 0, 2)
    kdoc = by_owner[owners].reshape(blocks, 3 * rows)
    position = owners[:, None] * rows + jnp.arange(rows, dtype=jnp.int32)[None]
    first_filled = 2 * seg_len - filled
    kpos = jnp.concatenate(
        [
            jnp.where(position >= first_filled, -1, hidden_slot),
            jnp.where(position + seg_len >= first_filled, -1, hidden_slot),
            position,
        ],
        axis=1,
    ).astype(jnp.int32)
    qdoc = kdoc[:, 2 * rows :].reshape(blocks * rows, 1)
    qpos = position.reshape(blocks * rows, 1).astype(jnp.int32)
    marks = (qdoc, qpos, kdoc, kpos)

    def hop(arrays, after):
        arrays = [gate([x], after)[0] for x in arrays]
        return arrays, [along_blk(x, 1) for x in arrays]

    weights = (w_query, w_key, w_value)
    raw = [compressed, memory, segment]
    arriving = [along_blk(x, 1) for x in raw]
    pairs = memory.reshape(rows // RATE, RATE * width)
    projected = [project(block_ref, raw, gain, *weights, width, [])]
    query = projected[0][1]
    memories = [memory]
    raw, arriving = hop(arriving, [query])
    memories.append(raw[1])
    projected.append(raw)
    cots = [cotangent, in_plane(cotangent, 1)]
    for j in range(1, chips):
        cots.append(in_plane(cotangent, 2 * j))
        cots.append(in_plane(cots[-1], 1))
    projected[1] = project(block_ref, projected[1], gain, *weights, own, [])
    later = []
    for k in range(2, blocks - 1):
        raw, arriving = hop(arriving, [projected[1][1]])
        memories.append(raw[1])
        later.append(raw)
    memories.append(arriving[1])
    projected += [project(block_ref, rows3, gain, *weights, own, raw) for rows3 in later]
    keys, values = ([p[i] for p in projected] for i in (2, 3))
    partial = attend(query, keys, values, marks, [])
    *last, attended, middle, normed_ffn = finish(
        blocks - 1,
        block_ref,
        arriving,
        gain,
        *weights,
        own,
        query,
        partial,
        marks,
        segment,
        w_output,
        gain_ffn,
        cots[2:],
    )
    projected.append(last)
    normed, queries, keys, values = ([p[i] for p in projected] for i in range(4))

    nfs = [normed_ffn, in_plane(normed_ffn, 1)]
    for j in range(1, chips - 1):
        nfs.append(in_plane(normed_ffn, 2 * j))
        nfs.append(in_plane(nfs[-1], 1))
    *both, res, dn, send = feed(
        place_ref,
        normed_ffn,
        nfs[1],
        cotangent,
        cots[1],
        w_expand,
        w_reduce,
        [],
    )
    sent = in_plane(send, 1)
    both = [both[0], in_plane(both[1], 2), in_plane(both[2], 4), both[3]]
    result, d_middle, d_branch, *d_attended = leave(
        block_ref,
        blocks,
        res,
        dn,
        sent,
        middle,
        cotangent,
        gain_ffn,
        w_output,
        nfs[3:6],
    )
    grads = [d_attended[0]] + [along_blk(d_attended[k], k) for k in range(1, blocks)]
    both[3], diagonal = gate([both[3], normed_ffn], grads[1:])
    both[3] = in_plane(both[3], 6)
    nfs.append(in_plane(diagonal, 6))
    comps = [comp_cotangent] + [along_blk(comp_cotangent, k) for k in range(1, blocks)]
    *pieces, dk, dv = attend_back(
        block_ref, queries, grads, keys, values, marks, both[1:3]
    )
    arrived = [pieces[0]] + [along_blk(pieces[k], -k) for k in range(1, blocks)]
    nfs.append(in_plane(gate([nfs[6]], [pieces[0]])[0], 1))
    qkv_keep, qkv_give = heads_gradient(
        place_ref, normed, pieces, dk, dv, blocks * part_rows, [nfs[6], both[3], *comps[1:]]
    )
    other_keep, other_give = other_gradients(
        place_ref,
        block_ref,
        attended,
        d_branch,
        memories,
        comps,
        blocks * part_rows,
        [qkv_keep],
    )
    qkv_give, other_give = gate([qkv_give, other_give], [other_keep])
    part, *moved = plane_gradients(
        block_ref, cots, nfs, both, blocks, part_rows, [other_keep, *arrived[1:]]
    )
    four = pair_add(
        place_ref, qkv_keep, in_plane(qkv_give, 1), other_keep, in_plane(other_give, 1), moved
    )
    before = four[0]
    for k in range(2, blocks):
        for i in range(2):
            moved[i] = ring_add(block_ref, i, k, along_blk(moved[i], 1), part, [before])
            before = moved[i]
        if k == 2:
            new_compressed = compress(pairs, w_compress, [before])
            before = new_compressed
    four = [four[0]] + [in_plane(four[j], 2 * j) for j in range(1, chips)]
    grad_segment = segment_gradient(
        block_ref, arrived, *weights, segment, gain, d_middle, [before]
    )
    *parts, grad_compress = chip_add(
        block_ref, blocks, four, 3 * own + width, [grad_segment]
    )
    parts = [parts[0]] + [along_blk_flip(parts[k], k) for k in range(1, blocks)]
    wide = spread(
        place_ref, block_ref, [along_blk(x, 1) for x in moved], part, [parts[0]]
    )
    wide = [wide[0]] + [in_plane(wide[j], j) for j in range(1, PLANE)]

    def mine(x):
        return lax.dynamic_slice_in_dim(x, index * part_rows, part_rows, 0).reshape(1, -1)

    grad_query, grad_key, grad_value, grad_output, grad_norm_gain = last_heads(
        block_ref, index_ref, parts, mine(norm_gain), *weights, [grad_segment]
    )
    grad_expand, reduce_turned, grad_ffn_gain = last_wide(
        place_ref, index_ref, wide, mine(ffn_gain), w_expand, [grad_query]
    )
    return (
        result[None],
        new_compressed[None],
        grad_segment[None],
        grad_norm_gain.reshape(-1),
        grad_query,
        grad_key,
        grad_value,
        grad_output,
        grad_ffn_gain.reshape(-1),
        grad_expand,
        reduce_turned.T,
        grad_compress,
    )


def layer_norm(rows_in, gain):
    center = jnp.mean(rows_in, axis=-1, keepdims=True)
    offset = rows_in - center
    spread = jnp.mean(offset * offset, axis=-1, keepdims=True)
    return offset * lax.rsqrt(spread + epsilon) * gain


def exact_gelu(values_in):
    return jax.nn.gelu(values_in, approximate=False)


def on_any(
    segment,
    memory,
    compressed,
    document_labels,
    memory_filled_count,
    norm_gain,
    w_query,
    w_key,
    w_value,
    w_output,
    ffn_gain,
    w_expand,
    w_reduce,
    w_compress,
    result_cotangent,
    compressed_cotangent,
):
    streams, block_rows, model_width = segment.shape
    head_count = model_width // HD
    blocks = lax.axis_size("blk")
    my_block = lax.axis_index("blk")
    seg_len = block_rows * blocks
    key_count = 3 * seg_len
    score_scale = HD ** (-0.5)
    stacked = jnp.concatenate([compressed, memory, segment], axis=1).astype(jnp.float32)
    normed_full, norm_pull = jax.vjp(layer_norm, stacked, norm_gain)
    normed = normed_full.astype(jnp.bfloat16)
    seg_normed = normed[:, 2 * block_rows :]
    queries = jnp.einsum(
        "srd,de->sre", seg_normed, w_query, preferred_element_type=jnp.float32
    ).astype(jnp.bfloat16)
    query_heads = queries.reshape(streams, block_rows, head_count, HD)
    keys = jnp.einsum("srd,de->rse", normed, w_key, preferred_element_type=jnp.float32).astype(
        jnp.bfloat16
    )
    values = jnp.einsum("srd,de->rse", normed, w_value, preferred_element_type=jnp.float32).astype(
        jnp.bfloat16
    )
    all_keys, all_values = (
        lax.all_gather(keys, "blk", axis=0, tiled=True),
        lax.all_gather(values, "blk", axis=0, tiled=True),
    )
    key_index = jnp.arange(key_count, dtype=jnp.int32)
    key_owner = key_index // (3 * block_rows)
    within = key_index % (3 * block_rows)
    key_kind = within // block_rows
    key_pos = key_owner * block_rows + within % block_rows
    key_slot = key_kind * seg_len + key_pos
    key_docs = (
        document_labels.reshape(streams, 3, blocks, block_rows)
        .transpose(0, 2, 1, 3)
        .reshape(streams, key_count)
    )
    query_pos = my_block * block_rows + jnp.arange(block_rows, dtype=jnp.int32)
    query_docs = lax.dynamic_slice_in_dim(
        document_labels[:, 2], my_block * block_rows, block_rows, 1
    )
    in_memory = key_slot[None, :] >= 2 * seg_len - memory_filled_count[:, None]
    causal = key_pos[None, :] <= query_pos[:, None]
    visible = jnp.where((key_kind < 2)[None, None, :], in_memory[:, None, :], causal[None, :, :])
    allowed = visible & (key_docs[:, None, :] == query_docs[:, :, None])

    def scores_of(key_set):
        key_view = key_set.reshape(key_count, streams, head_count, HD)
        raw_scores = (
            jnp.einsum("sqhd,kshd->shqk", query_heads, key_view, preferred_element_type=jnp.float32)
            * score_scale
        )
        return jnp.where(allowed[:, None], raw_scores, masked_score)

    scores = scores_of(all_keys)
    row_top = jnp.max(scores, axis=-1, keepdims=True)
    weights = jnp.exp(scores - row_top)
    row_total = jnp.sum(weights, axis=-1, keepdims=True)
    probs = (weights / row_total).astype(jnp.bfloat16)
    log_total = row_top + jnp.log(row_total)
    value_heads = all_values.reshape(key_count, streams, head_count, HD)
    attended = jnp.einsum("shqk,kshd->sqhd", probs, value_heads, preferred_element_type=jnp.float32)
    attended = attended.reshape(streams, block_rows, model_width).astype(jnp.bfloat16)
    middle = segment.astype(jnp.float32) + jnp.einsum(
        "sre,ed->srd", attended, w_output, preferred_element_type=jnp.float32
    )
    normed_ffn_full, ffn_pull = jax.vjp(layer_norm, middle, ffn_gain)
    normed_ffn = normed_ffn_full.astype(jnp.bfloat16)
    hidden = jnp.einsum("srd,df->srf", normed_ffn, w_expand, preferred_element_type=jnp.float32)
    activated_full, gelu_pull = jax.vjp(exact_gelu, hidden)
    activated = activated_full.astype(jnp.bfloat16)
    result = (
        middle + jnp.einsum("srf,fd->srd", activated, w_reduce, preferred_element_type=jnp.float32)
    ).astype(jnp.bfloat16)
    mem_pairs = memory.reshape(streams, block_rows // RATE, RATE * model_width)
    new_compressed = jnp.einsum(
        "srp,pd->srd", mem_pairs, w_compress, preferred_element_type=jnp.float32
    ).astype(jnp.bfloat16)
    reduce_turned = jnp.einsum(
        "srd,srf->df", result_cotangent, activated, preferred_element_type=jnp.float32
    )
    d_activated = jnp.einsum(
        "srd,fd->srf", result_cotangent, w_reduce, preferred_element_type=jnp.float32
    )
    d_hidden = gelu_pull(d_activated)[0].astype(jnp.bfloat16)
    grad_expand = jnp.einsum(
        "srd,srf->df", normed_ffn, d_hidden, preferred_element_type=jnp.float32
    )
    d_normed_ffn = jnp.einsum("srf,df->srd", d_hidden, w_expand, preferred_element_type=jnp.float32)
    d_middle_norm, grad_ffn_gain = ffn_pull(d_normed_ffn)
    d_middle = result_cotangent.astype(jnp.float32) + d_middle_norm
    d_branch = d_middle.astype(jnp.bfloat16)
    grad_output = jnp.einsum("sre,srd->ed", attended, d_branch, preferred_element_type=jnp.float32)
    d_attended = jnp.einsum(
        "srd,ed->sre", d_branch, w_output, preferred_element_type=jnp.float32
    ).astype(jnp.bfloat16)
    d_attended = d_attended.reshape(streams, block_rows, head_count, HD)
    key_heads = all_keys.reshape(key_count, streams, head_count, HD)
    probs_full = jnp.exp(scores_of(all_keys) - log_total)
    probs_low = probs_full.astype(jnp.bfloat16)
    d_probs = jnp.einsum(
        "sqhd,kshd->shqk", d_attended, value_heads, preferred_element_type=jnp.float32
    )
    row_delta = jnp.sum(probs_full * d_probs, axis=-1, keepdims=True)
    d_scores = (probs_full * (d_probs - row_delta)).astype(jnp.bfloat16)
    d_queries = (
        jnp.einsum("shqk,kshd->sqhd", d_scores, key_heads, preferred_element_type=jnp.float32)
        * score_scale
    )
    d_queries = d_queries.astype(jnp.bfloat16).reshape(streams, block_rows, model_width)
    count = 3 * block_rows * lax.axis_size("blk")
    key_part = (
        jnp.einsum("shqk,sqhd->kshd", d_scores, query_heads, preferred_element_type=jnp.float32)
        * score_scale
    )
    value_part = jnp.einsum(
        "shqk,sqhd->kshd", probs_low, d_attended, preferred_element_type=jnp.float32
    )
    key_grads = lax.psum_scatter(
        jnp.stack(
            [
                key_part.reshape(count, streams, model_width),
                value_part.reshape(count, streams, model_width),
            ],
            axis=1,
        ).astype(jnp.bfloat16),
        "blk",
        scatter_dimension=0,
        tiled=True,
    ).astype(jnp.float32)
    d_keys = key_grads[:, 0].astype(jnp.bfloat16)
    d_values = key_grads[:, 1].astype(jnp.bfloat16)
    grad_query = jnp.einsum(
        "srd,sre->de", seg_normed, d_queries, preferred_element_type=jnp.float32
    )
    grad_key = jnp.einsum("srd,rse->de", normed, d_keys, preferred_element_type=jnp.float32)
    grad_value = jnp.einsum("srd,rse->de", normed, d_values, preferred_element_type=jnp.float32)
    d_normed = jnp.einsum("rse,de->srd", d_keys, w_key, preferred_element_type=jnp.float32)
    d_normed = d_normed + jnp.einsum(
        "rse,de->srd", d_values, w_value, preferred_element_type=jnp.float32
    )
    d_seg_normed = jnp.einsum("sre,de->srd", d_queries, w_query, preferred_element_type=jnp.float32)
    d_normed = d_normed + jnp.pad(d_seg_normed, ((0, 0), (2 * block_rows, 0), (0, 0)))
    d_stacked, grad_norm_gain = norm_pull(d_normed)
    grad_segment = (d_middle + d_stacked[:, 2 * block_rows :]).astype(jnp.bfloat16)
    grad_compress = jnp.einsum(
        "srp,srd->pd", mem_pairs, compressed_cotangent, preferred_element_type=jnp.float32
    )
    weight_grads = (
        grad_norm_gain,
        grad_query,
        grad_key,
        grad_value,
        grad_output,
        grad_ffn_gain,
        grad_expand,
        reduce_turned,
        grad_compress,
    )
    summed = (
        lax.psum_scatter(weight_grads[0], ("stream", "blk"), scatter_dimension=0, tiled=True),
        lax.psum_scatter(weight_grads[1], ("stream", "blk"), scatter_dimension=0, tiled=True),
        lax.psum_scatter(weight_grads[2], ("stream", "blk"), scatter_dimension=0, tiled=True),
        lax.psum_scatter(weight_grads[3], ("stream", "blk"), scatter_dimension=0, tiled=True),
        lax.psum_scatter(weight_grads[4], ("stream", "blk"), scatter_dimension=0, tiled=True),
        lax.psum_scatter(weight_grads[5], ("stream", "blk"), scatter_dimension=0, tiled=True),
        lax.psum_scatter(weight_grads[6], ("stream", "blk"), scatter_dimension=0, tiled=True),
        lax.psum_scatter(weight_grads[7], ("stream", "blk"), scatter_dimension=0, tiled=True),
        lax.psum_scatter(weight_grads[8], ("stream", "blk"), scatter_dimension=0, tiled=True),
    )
    grad_reduce = summed[7].T
    return (
        result,
        new_compressed,
        grad_segment,
        summed[0],
        summed[1],
        summed[2],
        summed[3],
        summed[4],
        summed[5],
        summed[6],
        grad_reduce,
        summed[8],
    )


def solution(mesh):
    tokens = P("stream", "blk", None)
    both = ("stream", "blk")
    in_specs = (
        (tokens,) * 3
        + (P("stream", None, None), P("stream"))
        + (P(),) * 9
        + (tokens,) * 2
    )
    out_specs = (
        (tokens,) * 3
        + (P(both),)
        + (P(both, None),) * 4
        + (P(both), P(both, None), P(None, both), P(both, None))
    )
    one_plane = mesh.shape["stream"] == PLANE
    return jax.shard_map(
        on_plane if one_plane else on_any, mesh=mesh, in_specs=in_specs, out_specs=out_specs, check_vma=False
    )
```

```python
import functools

import jax
import jax.numpy as jnp
from jax import lax
from jax.experimental import pallas as pl
from jax.experimental.pallas import tpu as pltpu
from jax.sharding import PartitionSpec as P

HD = 128
RATE = 2
PLANE = 8

epsilon = 1e-05
masked_score = -1e30
hidden_slot = 1 << 30

f32 = jnp.float32
bf16 = jnp.bfloat16
MIB = 1 << 20
FLOPS_PER_US = 0.5e9
VM = pl.BlockSpec(memory_space=pltpu.VMEM)
SM = pl.BlockSpec(memory_space=pltpu.SMEM)
ANY = pl.BlockSpec(memory_space=pl.ANY)


def dot(left, right, contract=((1,), (0,))):
    return lax.dot_general(left, right, (contract, ((), ())), preferred_element_type=f32)


def standardized(rows):
    offset = rows - jnp.mean(rows, axis=-1, keepdims=True)
    scale = lax.rsqrt(jnp.mean(offset * offset, axis=-1, keepdims=True) + epsilon)
    return offset * scale, scale


def norm_input_gradient(e, gain, unit, scale):
    eg = e * gain
    return scale * (
        eg
        - jnp.mean(eg, axis=-1, keepdims=True)
        - unit * jnp.mean(eg * unit, axis=-1, keepdims=True)
    )


LOG2E = 1.4426950408889634
SCORE_SCALE = HD ** (-0.5) * LOG2E
LAST = ((1,), (1,))
FIRST = ((0,), (0,))
TILE = 256


def in_hbm(x):
    return pltpu.with_memory_space_constraint(x, pltpu.HBM)


def block_of(shape):
    return pl.BlockSpec(shape, lambda i: (0,) * len(shape))


def call(
    kernel, name, ins, outs, scratch=(), copies=0, grant=24, after=(), cost_us=1.0
):
    in_specs, operands = [], []
    inputs = len(ins)

    def body(*refs):
        kernel(*refs[:inputs], *refs[inputs + len(after) :])

    for x in ins:
        far = isinstance(x, tuple)
        x = x[0] if far else x
        operands.append(in_hbm(x) if far else x)
        in_specs.append(ANY if far else SM if x.size == 1 else block_of(x.shape))
    operands += [in_hbm(x[0]) if isinstance(x, tuple) else x for x in after]
    in_specs += [ANY] * len(after)
    scratch = list(scratch)
    if copies:
        scratch.append(pltpu.SemaphoreType.DMA((copies,)))
    return pl.pallas_call(
        body,
        grid=(1,),
        in_specs=in_specs,
        out_specs=[ANY if isinstance(o, tuple) else block_of(o.shape) for o in outs],
        out_shape=[
            pltpu.HBM(o[0].shape, o[0].dtype) if isinstance(o, tuple) else o for o in outs
        ],
        scratch_shapes=scratch,
        compiler_params=pltpu.CompilerParams(vmem_limit_bytes=grant * MIB),
        cost_estimate=pl.CostEstimate(
            flops=int(cost_us * FLOPS_PER_US), bytes_accessed=0, transcendentals=0
        ),
        name=name,
    )(*operands)


def gate(arrays, after):
    count = len(arrays)
    return pl.pallas_call(
        lambda *refs: None,
        in_specs=[ANY] * (count + len(after)),
        out_specs=[ANY] * count,
        out_shape=[pltpu.HBM(x.shape, x.dtype) for x in arrays],
        input_output_aliases={i: i for i in range(count)},
        compiler_params=pltpu.CompilerParams(vmem_limit_bytes=MIB),
        cost_estimate=pl.CostEstimate(flops=0, bytes_accessed=0, transcendentals=0),
        name="gate",
    )(*arrays, *[in_hbm(x[0]) if isinstance(x, tuple) else x for x in after])


class Copies:
    def __init__(self, sems):
        self.sems, self.count = sems, 0

    def __call__(self, source, target):
        copy = pltpu.make_async_copy(source, target, self.sems.at[self.count])
        copy.start()
        self.count += 1
        return copy


def lanes(start, size):
    return pl.ds(pl.multiple_of(start, size), size)


def shape_of(shape, dtype=bf16):
    return jax.ShapeDtypeStruct(shape, dtype)


def norm_rows(raw, gain_ref, normed_ref):
    rows = raw.shape[1]
    for i in range(raw.shape[0]):
        unit, _ = standardized(raw[i].astype(f32))
        normed_ref[i * rows : (i + 1) * rows, :] = (unit * gain_ref[...]).astype(bf16)


ROW_CUTS = 4


def bring_rows(bring, source, target):
    step = source.shape[0] // ROW_CUTS
    return [
        bring(source.at[pl.ds(i * step, step)], target.at[pl.ds(i * step, step)])
        for i in range(ROW_CUTS)
    ]


def wait_all(copies):
    for copy in copies:
        copy.wait()


def project_kernel(all_queries, *refs):
    block_ref, *raw_refs = refs[:4]
    gain_ref, wq_ref, wk_ref, wv_ref = refs[4:8]
    outs = refs[8:12]
    wq, wk, wv, normed_ref, q_ref, k_ref, v_ref, raw, sems = refs[12:]
    bring = Copies(sems)
    width = k_ref.shape[1]
    raws = [bring(ref, raw.at[i]) for i, ref in enumerate(raw_refs)]
    coming = [bring_rows(bring, wk_ref, wk), bring_rows(bring, wv_ref, wv)]
    if all_queries:
        query_weight = bring(wq_ref, wq)
    else:
        own = q_ref.shape[1]
        query_weight = bring(wq_ref.at[:, lanes(block_ref[0] * own, own)], wq)
    wait_all(raws)
    norm_rows(raw, gain_ref, normed_ref)
    leaving = [bring(normed_ref, outs[0])]
    normed = normed_ref[...]
    for copies, weight, target, out in zip(coming, (wk, wv), (k_ref, v_ref), outs[2:]):
        wait_all(copies)
        for at in range(0, width, TILE):
            target[:, at : at + TILE] = dot(normed, weight[:, at : at + TILE]).astype(bf16)
        leaving.append(bring(target, out))
    query_weight.wait()
    q_ref[...] = dot(normed[2 * raw.shape[1] :], wq[...]).astype(bf16)
    leaving.append(bring(q_ref, outs[1]))
    wait_all(leaving)


def projected_shapes(rows, width, own):
    return [
        shape_of((3 * rows, width)),
        shape_of((rows, own)),
        shape_of((3 * rows, width)),
        shape_of((3 * rows, width)),
    ]


def project(block, raw_rows, gain, w_query, w_key, w_value, own, after):
    rows, width = raw_rows[0].shape
    shapes = projected_shapes(rows, width, own)
    weights = [(width, own), (width, width), (width, width)]
    return call(
        functools.partial(project_kernel, own == width),
        "project",
        [block] + [(x,) for x in raw_rows] + [gain, (w_query,), (w_key,), (w_value,)],
        [(x,) for x in shapes],
        scratch=[pltpu.VMEM(x, bf16) for x in weights]
        + [pltpu.VMEM(x.shape, x.dtype) for x in shapes]
        + [pltpu.VMEM((3, rows, width), bf16)],
        copies=2 * ROW_CUTS + 8,
        after=after,
        cost_us=0.1,
    )


def compress_kernel(pairs_ref, w_far, out_ref, w_ref, sems):
    bring = Copies(sems)
    count = w_ref.shape[0]
    coming = [bring(w_far.at[pl.ds(i * w_ref.shape[1], w_ref.shape[1])], w_ref.at[i]) for i in range(count)]
    total = None
    for i in range(count):
        coming[i].wait()
        part = dot(pairs_ref[:, i * w_ref.shape[1] : (i + 1) * w_ref.shape[1]], w_ref[i])
        total = part if total is None else total + part
    out_ref[...] = total.astype(bf16)


def compress(pairs, w_compress, after):
    depth, width = w_compress.shape
    count = 4
    return call(
        compress_kernel,
        "compress",
        [pairs, (w_compress,)],
        [shape_of((pairs.shape[0], width))],
        scratch=[pltpu.VMEM((count, depth // count, width), bf16)],
        copies=count,
        after=after,
        cost_us=3.2,
    )[0]


def score_bias(qdoc, qpos, kdoc_ref, kpos_ref, slot):
    allowed = (kdoc_ref[slot : slot + 1, :] == qdoc) & (kpos_ref[slot : slot + 1, :] <= qpos)
    return jnp.where(allowed, 0.0, masked_score)


def attend_kernel(slots, *refs):
    qdoc_ref, qpos_ref, kdoc_ref, kpos_ref, q_far = refs[:5]
    k_far = refs[5 : 5 + slots]
    v_far = refs[5 + slots : 5 + 2 * slots]
    out_ref, stat_ref, bias_ref, q_ref, k_ref, v_ref, sems = refs[5 + 2 * slots :]
    rows, width = q_ref.shape
    bring = Copies(sems)
    query = bring(q_far, q_ref)
    tiles = [slice(at, at + TILE) for at in range(0, width, TILE)]
    coming = [
        [
            bring(far[slot].at[:, at], near.at[slot, :, at])
            for slot in range(slots)
            for far, near in ((k_far, k_ref), (v_far, v_ref))
        ]
        for at in tiles
    ]
    qdoc, qpos = qdoc_ref[:rows, :], qpos_ref[:rows, :]
    for slot in range(slots):
        bias_ref[slot] = score_bias(qdoc, qpos, kdoc_ref, kpos_ref, slot)
    query.wait()
    lane = lax.broadcasted_iota(jnp.int32, (rows, HD), 1)
    stats = jnp.zeros((rows, HD), f32)
    heads = width // HD
    for head in range(heads):
        if head * HD % TILE == 0:
            for copy in coming[head * HD // TILE]:
                copy.wait()
        at = slice(head * HD, (head + 1) * HD)
        q = q_ref[:, at]
        scores = [
            dot(q, k_ref[slot, :, at], LAST) * SCORE_SCALE + bias_ref[slot]
            for slot in range(slots)
        ]
        top = functools.reduce(jnp.maximum, scores)
        top = jnp.max(top, axis=-1, keepdims=True)
        weights = [jnp.exp2(s - top) for s in scores]
        total = jnp.sum(functools.reduce(jnp.add, weights), axis=-1, keepdims=True)
        out_ref[:, at] = functools.reduce(
            jnp.add,
            [dot(weights[slot].astype(bf16), v_ref[slot, :, at]) for slot in range(slots)],
        )
        stats = jnp.where(lane == head, top, stats)
        stats = jnp.where(lane == heads + head, total, stats)
    stat_ref[...] = stats


def attend(query, keys, values, marks, after):
    slots = len(keys)
    rows, width = query.shape
    key_rows = keys[0].shape[0]
    return call(
        functools.partial(attend_kernel, slots),
        "attend",
        [*marks, (query,)] + [(x,) for x in (*keys, *values)],
        [shape_of((rows, width), f32), shape_of((rows, HD), f32)],
        scratch=[
            pltpu.VMEM((slots, rows, key_rows), f32),
            pltpu.VMEM((rows, width), bf16),
            pltpu.VMEM((slots, key_rows, width), bf16),
            pltpu.VMEM((slots, key_rows, width), bf16),
        ],
        copies=1 + 2 * slots * (width // TILE),
        after=after,
        cost_us=0.1,
    )


def finish_kernel(slot, *refs):
    block_ref, *raw_refs = refs[:4]
    gain_ref, wq_far, wk_far, wv_far = refs[4:8]
    query_far, sum_ref, stat_ref, qdoc_ref, qpos_ref, kdoc_ref, kpos_ref = refs[8:15]
    seg_ref, wo_far, gain_ffn_ref = refs[15:18]
    outs = refs[18:24]
    middle_ref, nf_ref = refs[24:26]
    wq, wk, wv, normed_ref, q_ref, k_ref, v_ref, wo, query_ref, att_ref, raw, nf_copy, sems = refs[26:]
    rows, width = query_ref.shape
    bring = Copies(sems)
    raws = [bring(ref, raw.at[i]) for i, ref in enumerate(raw_refs)]
    coming = [bring_rows(bring, wk_far, wk), bring_rows(bring, wv_far, wv)]
    query = bring(query_far, query_ref)
    output_weight = bring(wo_far, wo)
    own = q_ref.shape[1]
    query_weight = bring(wq_far.at[:, lanes(block_ref[0] * own, own)], wq)
    bias = score_bias(qdoc_ref[:rows, :], qpos_ref[:rows, :], kdoc_ref, kpos_ref, slot)
    wait_all(raws)
    norm_rows(raw, gain_ref, normed_ref)
    leaving = [bring(normed_ref, outs[0])]
    normed = normed_ref[...]
    query.wait()
    heads = width // HD
    for copies, weight, target, out in zip(coming, (wk, wv), (k_ref, v_ref), outs[2:4]):
        wait_all(copies)
        for at in range(0, width, TILE):
            target[:, at : at + TILE] = dot(normed, weight[:, at : at + TILE]).astype(bf16)
        leaving.append(bring(target, out))
    group = 4
    for start in range(0, heads, group):
        some = range(start, start + group)
        at = {h: slice(h * HD, (h + 1) * HD) for h in some}
        scores = {
            h: dot(query_ref[:, at[h]], k_ref[:, at[h]], LAST) * SCORE_SCALE + bias for h in some
        }
        before = {h: stat_ref[:, h : h + 1] for h in some}
        top = {
            h: jnp.maximum(before[h], jnp.max(scores[h], axis=-1, keepdims=True)) for h in some
        }
        weights = {h: jnp.exp2(scores[h] - top[h]) for h in some}
        shrink = {h: jnp.exp2(before[h] - top[h]) for h in some}
        total = {
            h: stat_ref[:, heads + h : heads + h + 1] * shrink[h]
            + jnp.sum(weights[h], axis=-1, keepdims=True)
            for h in some
        }
        out = {
            h: sum_ref[:, at[h]] * shrink[h] + dot(weights[h].astype(bf16), v_ref[:, at[h]])
            for h in some
        }
        for h in some:
            att_ref[:, at[h]] = (out[h] * (1.0 / total[h])).astype(bf16)
    query_weight.wait()
    q_ref[...] = dot(normed[2 * raw.shape[1] :], wq[...]).astype(bf16)
    leaving.append(bring(q_ref, outs[1]))
    leaving.append(bring(att_ref, outs[4]))
    output_weight.wait()
    middle = seg_ref[...].astype(f32) + dot(att_ref[...], wo[...])
    middle_ref[...] = middle
    unit, _ = standardized(middle)
    nf_ref[...] = (unit * gain_ffn_ref[...]).astype(bf16)
    nf_copy[...] = nf_ref[...]
    leaving.append(bring(nf_copy, outs[5]))
    wait_all(leaving)


def finish(
    slot, block, raw_rows, gain, w_query, w_key, w_value, own, query, partial, marks, segment, w_output, gain_ffn, after
):
    rows, width = segment.shape
    shapes = projected_shapes(rows, width, own)
    weights = [(width, own), (width, width), (width, width)]
    return call(
        functools.partial(finish_kernel, slot),
        "finish",
        [block] + [(x,) for x in raw_rows] + [gain, (w_query,), (w_key,), (w_value,), (query,), *partial, *marks]
        + [segment, (w_output,), gain_ffn],
        [(x,) for x in shapes]
        + [(shape_of((rows, width)),)] * 2
        + [shape_of((rows, width), f32), shape_of((rows, width))],
        scratch=[pltpu.VMEM(x, bf16) for x in weights]
        + [pltpu.VMEM(x.shape, x.dtype) for x in shapes]
        + [
            pltpu.VMEM((width, width), bf16),
            pltpu.VMEM((rows, width), bf16),
            pltpu.VMEM((rows, width), bf16),
            pltpu.VMEM((3, rows, width), bf16),
            pltpu.VMEM((rows, width), bf16),
        ],
        copies=2 * ROW_CUTS + 12,
        after=after,
        cost_us=0.1,
    )


def feed_kernel(chips, place_ref, nf_own, nf_got, cot_own, cot_got, we_far, wr_far, *refs):
    both_far = refs[:chips]
    res_ref, dn_ref, send_ref, nf_ref, cot_ref, both, we, wr, res, dn, sems = refs[chips:]
    rows = nf_own.shape[0]
    tile = wr.shape[1]
    bring = Copies(sems)
    coming = []
    for chip in range(chips):
        at = lanes((place_ref[0] ^ (2 * chip)) * tile, tile)
        coming.append(bring(we_far.at[:, at], we.at[chip]))
        coming.append(bring(wr_far.at[at, :], wr.at[chip]))
    nf_ref[:rows] = nf_own[...]
    nf_ref[rows:] = nf_got[...]
    cot_ref[:rows] = cot_own[...]
    cot_ref[rows:] = cot_got[...]
    res[...] = jnp.zeros_like(res)
    dn[...] = jnp.zeros_like(dn)
    part = tile // 2

    @pl.loop(0, chips)
    def _(chip):
        pltpu.make_async_copy(we.at[chip], we.at[chip], sems.at[2 * chip]).wait()
        pltpu.make_async_copy(wr.at[chip], wr.at[chip], sems.at[2 * chip + 1]).wait()
        for at in range(0, tile, part):
            here = slice(at, at + part)
            hidden = dot(nf_ref[...], we[chip, :, here])
            d_act = dot(cot_ref[...], wr[chip, here, :], LAST)
            cdf = 0.5 + 0.5 * lax.erf(hidden * (0.5**0.5))
            density = jnp.exp2(hidden * hidden * (-0.5 * LOG2E)) * 0.3989422804014327
            both[chip, 0, :, here] = (hidden * cdf).astype(bf16)
            both[chip, 1, :, here] = (d_act * (cdf + hidden * density)).astype(bf16)
        res[...] += dot(both[chip, 0], wr[chip])
        dn[...] += dot(both[chip, 1], we[chip], LAST)

    leaving = [bring(both.at[chip], both_far[chip]) for chip in range(chips)]
    res_ref[...] = res[:rows]
    dn_ref[...] = dn[:rows]
    send_ref[0] = res[rows:].astype(bf16)
    send_ref[1] = dn[rows:].astype(bf16)
    wait_all(leaving)


def feed(place, nf_own, nf_got, cot_own, cot_got, w_expand, w_reduce, after):
    rows, width = nf_own.shape
    chips = PLANE // 2
    tile = w_expand.shape[1] // PLANE
    return call(
        functools.partial(feed_kernel, chips),
        "feed",
        [place, nf_own, nf_got, cot_own, cot_got, (w_expand,), (w_reduce,)],
        [(shape_of((2, 2 * rows, tile)),)] * chips
        + [shape_of((rows, width), f32)] * 2
        + [shape_of((2, rows, width))],
        scratch=[
            pltpu.VMEM((2 * rows, width), bf16),
            pltpu.VMEM((2 * rows, width), bf16),
            pltpu.VMEM((chips, 2, 2 * rows, tile), bf16),
            pltpu.VMEM((chips, width, tile), bf16),
            pltpu.VMEM((chips, tile, width), bf16),
            pltpu.VMEM((2 * rows, width), f32),
            pltpu.VMEM((2 * rows, width), f32),
        ],
        copies=3 * chips,
        grant=28,
        after=after,
        cost_us=0.1,
    )


def leave_kernel(slots, block_ref, *refs):
    res_ref, dn_ref, got_ref, middle_ref, cot_ref, gain_ref, wo_far = refs[:7]
    result_ref, dmid_far, branch_far = refs[7:10]
    datt_refs = refs[10 : 10 + slots]
    wo, dmid_ref, branch_ref, sems = refs[10 + slots :]
    own = wo.shape[1]
    bring = Copies(sems)
    coming = [
        bring(wo_far.at[lanes(lax.rem(block_ref[0] + slot, slots) * own, own), :], wo.at[slot])
        for slot in range(slots)
    ]
    middle = middle_ref[...]
    result_ref[...] = (middle + (res_ref[...] + got_ref[0].astype(f32))).astype(bf16)
    unit, scale = standardized(middle)
    d_normed = dn_ref[...] + got_ref[1].astype(f32)
    d_mid = cot_ref[...].astype(f32) + norm_input_gradient(d_normed, gain_ref[...], unit, scale)
    dmid_ref[...] = d_mid
    branch = d_mid.astype(bf16)
    branch_ref[...] = branch
    leaving = [bring(dmid_ref, dmid_far), bring(branch_ref, branch_far)]
    for slot in range(slots):
        coming[slot].wait()
        datt_refs[slot][...] = dot(branch, wo[slot], LAST).astype(bf16)
    wait_all(leaving)


def leave(block, slots, res, dn, got, middle, cotangent, gain, w_output, after):
    rows, width = middle.shape
    own = width // slots
    return call(
        functools.partial(leave_kernel, slots),
        "leave",
        [block, res, dn, got, middle, cotangent, gain, (w_output,)],
        [shape_of((rows, width)), (shape_of((rows, width), f32),), (shape_of((rows, width)),)]
        + [shape_of((rows, own))] * slots,
        scratch=[
            pltpu.VMEM((slots, own, width), bf16),
            pltpu.VMEM((rows, width), f32),
            pltpu.VMEM((rows, width), bf16),
        ],
        copies=slots + 2,
        after=after,
        cost_us=3.8,
    )


def attend_back_kernel(slots, heads, block_ref, *refs):
    take = iter(refs)
    marks = [next(take) for _ in range(4)]
    g_refs = [next(take) for _ in range(slots)]
    q_far = [next(take) for _ in range(slots)]
    k_far = [next(take) for _ in range(slots)]
    v_far = [next(take) for _ in range(slots)]
    piece_far = [next(take) for _ in range(slots)]
    dk_far, dv_far, q_ref, k_ref, v_ref, piece_refs, dk_ref, dv_ref, sems = take
    qdoc_ref, qpos_ref, kdoc_ref, kpos_ref = marks
    scale = HD ** (-0.5)
    rows = g_refs[0].shape[0]
    own = heads * HD
    bring = Copies(sems)
    owned = lanes(block_ref[0] * own, own)
    coming = []
    for slot in range(slots):
        coming.append(bring(q_far[slot].at[:, owned] if slot == 0 else q_far[slot], q_ref.at[slot]))
        coming.append(bring(k_far[slot].at[:, owned], k_ref.at[slot]))
        coming.append(bring(v_far[slot].at[:, owned], v_ref.at[slot]))
    for copy in coming:
        copy.wait()
    dk = [[None] * slots for _ in range(heads)]
    dv = [[None] * slots for _ in range(heads)]
    for one in range(slots):
        here = slice(one * rows, (one + 1) * rows)
        qdoc, qpos = qdoc_ref[here, :], qpos_ref[here, :]
        bias = [score_bias(qdoc, qpos, kdoc_ref, kpos_ref, slot) for slot in range(slots)]
        every = range(heads)
        at = [slice(head * HD, (head + 1) * HD) for head in every]
        q = [q_ref[one, :, at[head]] for head in every]
        grad = [g_refs[one][:, at[head]] for head in every]
        scores = [
            [
                dot(q[head], k_ref[slot, :, at[head]], LAST) * SCORE_SCALE + bias[slot]
                for slot in range(slots)
            ]
            for head in every
        ]
        d_probs = [
            [dot(grad[head], v_ref[slot, :, at[head]], LAST) for slot in range(slots)]
            for head in every
        ]
        top = [
            jnp.max(functools.reduce(jnp.maximum, scores[head]), axis=-1, keepdims=True)
            for head in every
        ]
        weights = [[jnp.exp2(x - top[head]) for x in scores[head]] for head in every]
        inverse = [
            1.0 / jnp.sum(functools.reduce(jnp.add, weights[head]), axis=-1, keepdims=True)
            for head in every
        ]
        probs = [[x * inverse[head] for x in weights[head]] for head in every]
        delta = [
            jnp.sum(
                functools.reduce(jnp.add, [p * d for p, d in zip(probs[head], d_probs[head])]),
                axis=-1,
                keepdims=True,
            )
            for head in every
        ]
        for head in every:
            d_score = [
                (p * (d - delta[head])).astype(bf16) for p, d in zip(probs[head], d_probs[head])
            ]
            dq = None
            for slot in range(slots):
                part = dot(d_score[slot], k_ref[slot, :, at[head]])
                dq = part if dq is None else dq + part
                dk_part = dot(q[head], d_score[slot], FIRST)
                dv_part = dot(grad[head], probs[head][slot].astype(bf16), FIRST)
                dk[head][slot] = dk_part if one == 0 else dk[head][slot] + dk_part
                dv[head][slot] = dv_part if one == 0 else dv[head][slot] + dv_part
            piece_refs[one, :, at[head]] = (dq * scale).astype(bf16)
    leaving = []
    for slot in range(slots):
        for head in range(heads):
            at = slice(head * HD, (head + 1) * HD)
            d_key = jnp.transpose((dk[head][slot] * scale).astype(bf16))
            d_value = jnp.transpose(dv[head][slot].astype(bf16))
            dk_ref[slot, :, at] = d_key
            dv_ref[slot, :, at] = d_value
            for i, value in enumerate((d_key, d_value)):
                first = (i + 1) * own + head * HD
                piece_refs[slot, :, first : first + HD] = value[2 * rows :]
        leaving.append(bring(piece_refs.at[slot], piece_far[slot]))
    leaving += [bring(dk_ref, dk_far), bring(dv_ref, dv_far)]
    wait_all(leaving)


def attend_back(block, queries, grads, keys, values, marks, after):
    slots = len(keys)
    key_rows = keys[0].shape[0]
    rows, own = grads[0].shape
    heads = own // HD
    return call(
        functools.partial(attend_back_kernel, slots, heads),
        "attend_back",
        [block, *marks, *grads] + [(x,) for x in (*queries, *keys, *values)],
        [(shape_of((rows, 3 * own)),)] * slots + [(shape_of((slots, key_rows, own)),)] * 2,
        scratch=[
            pltpu.VMEM((slots, rows, own), bf16),
            pltpu.VMEM((slots, key_rows, own), bf16),
            pltpu.VMEM((slots, key_rows, own), bf16),
            pltpu.VMEM((slots, rows, 3 * own), bf16),
            pltpu.VMEM((slots, key_rows, own), bf16),
            pltpu.VMEM((slots, key_rows, own), bf16),
        ],
        copies=4 * slots + 2,
        after=after,
        cost_us=4.0,
    )


def heads_kernel(slots, place_ref, *refs):
    piece_far = refs[:slots]
    normed_far = refs[slots : 2 * slots]
    dk_far, dv_far = refs[2 * slots : 2 * slots + 2]
    keep_far, give_far, out_ref, pieces, normed, dk, dv, sems = refs[2 * slots + 2 :]
    own = dk.shape[2]
    rows = pieces.shape[1]
    cut = out_ref.shape[2]
    core = lax.rem(place_ref[0], 2)
    bring = Copies(sems)
    second = [bring(normed_far[0], normed.at[0]), bring(dv_far, dv)]
    second += [bring(normed_far[slot], normed.at[slot]) for slot in range(1, slots)]
    third = [bring(dk_far, dk)]
    fourth = [bring(piece_far[slot], pieces.at[slot]) for slot in range(slots)]
    leaving = []

    def store(value, at):
        here = slice(at, at + value.shape[1])
        for j in range(value.shape[0] // cut):
            out_ref[j % 2, j // 2, :, here] = value[j * cut : (j + 1) * cut]
        here = pl.ds(at, value.shape[1])
        leaving.append(bring(out_ref.at[1 - core, :, :, here], give_far.at[:, :, here]))
        leaving.append(bring(out_ref.at[core, :, :, here], keep_far.at[:, :, here]))

    def turned(narrow, wide):
        return jnp.transpose(dot(narrow, wide, FIRST).astype(bf16))

    wait_all(second)
    every = normed[...].reshape(-1, normed.shape[2])
    store(turned(dv[...].reshape(-1, own), every), 2 * own)
    wait_all(third)
    store(turned(dk[...].reshape(-1, own), every), own)
    wait_all(fourth)
    queries = normed[:, 2 * rows :, :].reshape(-1, normed.shape[2])
    store(turned(pieces[:, :, :own].reshape(-1, own), queries), 0)
    wait_all(leaving)


def heads_gradient(place, normed, pieces, dk, dv, cut, after):
    slots, key_rows, own = dk.shape
    rows = pieces[0].shape[0]
    width = normed[0].shape[1]
    half = (width // cut // 2, cut, 3 * own)
    return call(
        functools.partial(heads_kernel, slots),
        "heads_gradient",
        [place] + [(x,) for x in (*pieces, *normed, dk, dv)],
        [(shape_of(half),)] * 2,
        scratch=[
            pltpu.VMEM((2, *half), bf16),
            pltpu.VMEM((slots, *pieces[0].shape), bf16),
            pltpu.VMEM((slots, key_rows, width), bf16),
            pltpu.VMEM((slots, key_rows, own), bf16),
            pltpu.VMEM((slots, key_rows, own), bf16),
        ],
        copies=2 * slots + 8,
        after=after,
        grant=36,
        cost_us=0.1,
    )


def other_kernel(slots, place_ref, block_ref, att_far, branch_far, *refs):
    mem_far = refs[:slots]
    comp_far = refs[slots : 2 * slots]
    keep_far, give_far, out_ref, att, branch, mem, comp, apart, rows_ref, sems = refs[2 * slots :]
    core = lax.rem(place_ref[0], 2)
    _, chips, cut, _ = out_ref.shape
    bring = Copies(sems)
    first = [bring(att_far, att), bring(branch_far, branch)]
    rows, width = att.shape
    pairs = comp.shape[1]
    second = []
    for slot in range(slots):
        second.append(bring(mem_far[slot], mem.at[pl.ds(slot * rows, rows)]))
        second.append(bring(comp_far[slot], comp.at[slot]))
    wait_all(first)
    for i in range(chips):
        at = slice(2 * i * cut, 2 * (i + 1) * cut)
        value = dot(att[:, at], branch[...], FIRST).astype(bf16)
        for j in range(2):
            out_ref[j, i, :, :width] = value[j * cut : (j + 1) * cut]
    wait_all(second)
    row = lax.broadcasted_iota(jnp.int32, (rows, pairs), 0)
    column = lax.broadcasted_iota(jnp.int32, (rows, pairs), 1)
    groups = PLANE // RATE
    step = width // groups
    part = step // slots
    wide = width // 2
    for i in range(RATE):
        chosen = (row == column * RATE + i).astype(f32).astype(bf16)
        for slot in range(slots):
            apart[slot * rows : (slot + 1) * rows, i * width : (i + 1) * width] = dot(
                chosen, comp[slot]
            ).astype(bf16)
    for group in range(groups):
        rows_ref[...] = dot(mem[:, group * step : (group + 1) * step], apart[...], FIRST)
        value = rows_ref[pl.ds(pl.multiple_of(block_ref[0] * part, part), part), :].astype(bf16)
        for i in range(RATE):
            owner = i * groups + group
            for k in range(cut // part):
                first = i * width + k * wide
                out_ref[owner % 2, owner // 2, k * part : (k + 1) * part, width:] = value[
                    :, first : first + wide
                ]
    wait_all([bring(out_ref.at[1 - core], give_far), bring(out_ref.at[core], keep_far)])


def other_gradients(place, block, attended, branch, memories, comps, cut, after):
    slots = len(memories)
    rows, width = attended.shape
    pairs = comps[0].shape[0]
    half = (width // cut // 2, cut, width + width // 2)
    return call(
        functools.partial(other_kernel, slots),
        "other_gradients",
        [place, block] + [(x,) for x in (attended, branch, *memories, *comps)],
        [(shape_of(half),)] * 2,
        scratch=[
            pltpu.VMEM((2, *half), bf16),
            pltpu.VMEM((rows, width), bf16),
            pltpu.VMEM((rows, width), bf16),
            pltpu.VMEM((slots * rows, width), bf16),
            pltpu.VMEM((slots, pairs, width), bf16),
            pltpu.VMEM((slots * rows, RATE * width), bf16),
            pltpu.VMEM((width * RATE // PLANE, RATE * width), f32),
        ],
        copies=4 + 2 * slots,
        after=after,
        cost_us=0.1,
    )


def pair_add_kernel(place_ref, *refs):
    keep_far = refs[:2]
    got = refs[2:4]
    outs = refs[4:8]
    near = refs[8:10]
    total, sems = refs[10:]
    bring = Copies(sems)
    chip = place_ref[0] // 2
    order = [1, 2, 3, 0]
    coming = {j: [bring(f.at[chip ^ j], n.at[j]) for f, n in zip(keep_far, near)] for j in order}
    leaving = []
    width = near[0].shape[2]
    for j in order:
        wait_all(coming[j])
        for at, a, b in zip((slice(0, width), slice(width, None)), near, got):
            total[j, :, at] = (a[j].astype(f32) + b[chip ^ j].astype(f32)).astype(bf16)
        leaving.append(bring(total.at[j], outs[j]))
    wait_all(leaving)


def pair_add(place, qkv_keep, qkv_got, output_keep, output_got, after):
    chips, rows, width = qkv_keep.shape
    wide = output_keep.shape[2]
    return call(
        pair_add_kernel,
        "pair_add",
        [place, (qkv_keep,), (output_keep,), qkv_got, output_got],
        [(shape_of((rows, width + wide)),)] * chips,
        scratch=[
            pltpu.VMEM(qkv_keep.shape, bf16),
            pltpu.VMEM(output_keep.shape, bf16),
            pltpu.VMEM((chips, rows, width + wide), bf16),
        ],
        copies=3 * chips,
        after=after,
        cost_us=3.0,
    )


def chip_add_kernel(chips, block_ref, *refs):
    pieces = refs[:chips]
    outs = refs[chips:-2]
    compress_ref, total = refs[-2:]
    total[...] = sum(p[...].astype(f32) for p in pieces)
    blocks = len(outs)
    rows = total.shape[0] // blocks
    width = outs[0].shape[1]
    for k in range(blocks):
        outs[k][...] = total[lanes((block_ref[0] ^ k) * rows, rows), :width].astype(bf16)
    part, wide = compress_ref.shape[0], total.shape[1] - width
    for i in range(total.shape[0] // part):
        compress_ref[:, i * wide : (i + 1) * wide] = total[i * part : (i + 1) * part, width:]


def chip_add(block, blocks, pieces, width, after):
    rows, total = pieces[0].shape
    wide = 2 * (total - width)
    return call(
        functools.partial(chip_add_kernel, len(pieces)),
        "chip_add",
        [block, *pieces],
        [shape_of((rows // blocks, width))] * blocks
        + [shape_of((rows * (total - width) // wide, wide), f32)],
        scratch=[pltpu.VMEM((rows, total), f32)],
        after=after,
        cost_us=0.1,
    )


def as_row(column):
    return jnp.transpose(jnp.broadcast_to(column, (column.shape[0], HD)))[:1]


def last_heads_kernel(blocks, block_ref, *refs):
    parts = refs[:blocks]
    gain_ref = refs[blocks]
    weights_far = refs[blocks + 1 : blocks + 4]
    at_ref = refs[blocks + 4]
    outs = refs[blocks + 5 : blocks + 8]
    output_ref, norm_ref, weights, sems = refs[blocks + 8 :]
    rows, width = output_ref.shape
    own = width // blocks
    bring = Copies(sems)
    here = pl.ds(pl.multiple_of(at_ref[0] * rows, rows), rows)
    coming = [bring(far.at[here, :], weights.at[i]) for i, far in enumerate(weights_far)]
    for k in range(blocks):
        at = lanes((block_ref[0] ^ k) * own, own)
        for i in range(3):
            outs[i][:, at] = parts[k][:, i * own : (i + 1) * own].astype(f32)
    first = 3 * own
    output_ref[...] = sum(p[:, first : first + width].astype(f32) for p in parts)
    wait_all(coming)
    total = sum(weights[i].astype(f32) * outs[i][...] for i in range(3))
    norm_ref[...] = as_row(jnp.sum(total, axis=1, keepdims=True)) / gain_ref[...]


def last_heads(block, index, parts, gain, w_query, w_key, w_value, after):
    blocks = len(parts)
    rows = parts[0].shape[0]
    width = w_query.shape[0]
    return call(
        functools.partial(last_heads_kernel, blocks),
        "last_heads",
        [block, *parts, gain, (w_query,), (w_key,), (w_value,), index],
        [shape_of((rows, width), f32)] * 4 + [shape_of((1, rows), f32)],
        scratch=[pltpu.VMEM((3, rows, width), bf16)],
        copies=3,
        after=after,
        cost_us=1.8,
    )


def segment_kernel(slots, block_ref, *refs):
    pieces_far = refs[:slots]
    seg_ref, gain_ref, dmid_far = refs[slots : slots + 3]
    far = refs[slots + 3 : slots + 6]
    out_ref, weight, pieces, dmid_ref, sems = refs[slots + 6 :]
    own = pieces.shape[2] // 3
    bring = Copies(sems)
    coming = []
    for slot in range(slots):
        at = lanes(lax.rem(block_ref[0] + slot, slots) * own, own)
        bring_piece = bring(pieces_far[slot], pieces.at[slot])
        coming.append([bring(far[i].at[:, at], weight.at[slot, i]) for i in range(3)])
        coming[-1].append(bring_piece)
    middle = bring(dmid_far, dmid_ref)
    total = None
    for slot in range(slots):
        wait_all(coming[slot])
        for i in range(3):
            part = dot(pieces[slot, :, i * own : (i + 1) * own], weight[slot, i], LAST)
            total = part if total is None else total + part
    unit, scale = standardized(seg_ref[...].astype(f32))
    middle.wait()
    out_ref[...] = (
        dmid_ref[...] + norm_input_gradient(total, gain_ref[...], unit, scale)
    ).astype(bf16)


def segment_gradient(block, pieces, w_query, w_key, w_value, segment, gain, d_middle, after):
    slots = len(pieces)
    rows, width = segment.shape
    return call(
        functools.partial(segment_kernel, slots),
        "segment_gradient",
        [block]
        + [(x,) for x in pieces]
        + [segment, gain, (d_middle,), (w_query,), (w_key,), (w_value,)],
        [shape_of((rows, width))],
        scratch=[
            pltpu.VMEM((slots, 3, width, width // slots), bf16),
            pltpu.VMEM((slots, *pieces[0].shape), bf16),
            pltpu.VMEM((rows, width), f32),
        ],
        copies=4 * slots + 1,
        after=after,
        cost_us=0.1,
    )[0]


def plane_kernel(blocks, block_ref, *refs):
    chips = PLANE // 2
    left_far = refs[: 2 * PLANE]
    right_far = refs[2 * PLANE : 2 * PLANE + chips]
    out_far, first_r, first_e, out_ref, left, right, sems = refs[2 * PLANE + chips :]
    rows = left_far[0].shape[0]
    bring = Copies(sems)
    coming = [[], []]
    for i in range(2):
        for chip in range(chips):
            at = pl.ds(2 * chip * rows, 2 * rows)
            coming[i].append(bring(right_far[chip].at[i], right.at[i, at]))
        for j in range(PLANE):
            at = pl.ds(j * rows, rows)
            coming[i].append(bring(left_far[i * PLANE + j], left.at[i, at]))
    cut = out_ref.shape[3]
    width = left.shape[2]
    step = width // 4
    leaving = []
    for i in range(2):
        wait_all(coming[i])
        for at in range(0, width, step):
            value = dot(left[i, :, at : at + step], right[i], FIRST).astype(bf16)
            for part in range(step // cut):
                j = at // cut + part
                out_ref[j % blocks, i, j // blocks] = value[part * cut : (part + 1) * cut]
    leaving.append(bring(out_ref, out_far))
    start = lax.rem(block_ref[0] + blocks - 1, blocks)
    first_r[...] = out_ref[start, 0]
    first_e[...] = out_ref[start, 1]
    wait_all(leaving)


def plane_gradients(block, cots, nfs, both, blocks, cut, after):
    rows, width = cots[0].shape
    _, _, tile = both[0].shape
    out = (blocks, 2, width // (blocks * cut), cut, tile)
    return call(
        functools.partial(plane_kernel, blocks),
        "plane_gradients",
        [block] + [(x,) for x in (*cots, *nfs[:-1])] + nfs[-1:] + [(x,) for x in both],
        [(shape_of(out),), shape_of(out[2:]), shape_of(out[2:])],
        scratch=[
            pltpu.VMEM(out, bf16),
            pltpu.VMEM((2, PLANE * rows, width), bf16),
            pltpu.VMEM((2, PLANE * rows, tile), bf16),
        ],
        copies=2 * PLANE + PLANE + 1,
        after=after,
        cost_us=80.0,
    )


def ring_kernel(which, k, blocks, block_ref, moved_ref, part_far, out_ref, part_ref, sems):
    bring = Copies(sems)
    piece = lax.rem(block_ref[0] + 2 * blocks - k, blocks)
    bring(part_far.at[piece, which], part_ref).wait()
    out_ref[...] = (moved_ref[...].astype(f32) + part_ref[...].astype(f32)).astype(bf16)


def ring_add(block, which, k, moved, part, after):
    blocks = part.shape[0]
    return call(
        functools.partial(ring_kernel, which, k, blocks),
        "ring_add",
        [block, moved, (part,)],
        [shape_of(moved.shape)],
        scratch=[pltpu.VMEM(moved.shape, bf16)],
        copies=1,
        after=after,
        cost_us=0.1,
    )[0]


def spread_kernel(place_ref, block_ref, r_moved, e_moved, part_far, *refs):
    outs = refs[:2]
    part_ref, sems = refs[2:]
    bring = Copies(sems)
    bring(part_far.at[block_ref[0]], part_ref).wait()
    for j in range(PLANE):
        at = place_ref[0] ^ j
        for i, moved in enumerate((r_moved, e_moved)):
            total = part_ref[i, at].astype(f32) + moved[at].astype(f32)
            outs[j % 2][j // 2, i] = total.astype(bf16)


def spread(place, block, moved, part, after):
    count, rows, tile = moved[0].shape
    return call(
        spread_kernel,
        "spread",
        [place, block, *moved, (part,)],
        [shape_of((count // 2, 2, rows, tile))] * 2,
        scratch=[pltpu.VMEM((2, count, rows, tile), bf16)],
        copies=1,
        after=after,
        cost_us=0.1,
    )


def join_kernel(keep_ref, got_ref, *outs):
    for j, out in enumerate(outs):
        out[0] = keep_ref[j + 1]
        out[1] = got_ref[j + 1]


def join(keep, got):
    chips = keep.shape[0]
    return call(
        join_kernel,
        "join",
        [keep, got],
        [shape_of((2, *keep.shape[1:]))] * (chips - 1),
        cost_us=0.1,
    )


def last_wide_kernel(place_ref, index_ref, *refs):
    chips = PLANE // 2
    keep_ref, got_ref, *moved = refs[: chips + 1]
    gain_ref, weight_far, expand_ref, reduce_ref, gain_out, weight, sems = refs[chips + 1 :]
    rows = weight.shape[0]
    tile = keep_ref.shape[3]
    parts = [keep_ref.at[0], got_ref.at[0]]
    for ref in moved:
        parts += [ref.at[0], ref.at[1]]
    bring = Copies(sems)
    coming = bring(
        weight_far.at[pl.ds(pl.multiple_of(index_ref[0] * rows, rows), rows), :], weight
    )
    for j in range(PLANE):
        at = lanes((place_ref[0] ^ j) * tile, tile)
        reduce_ref[:, at] = parts[j][0].astype(f32)
        expand_ref[:, at] = parts[j][1].astype(f32)
    coming.wait()
    total = jnp.sum(weight[...].astype(f32) * expand_ref[...], axis=1, keepdims=True)
    gain_out[...] = as_row(total) / gain_ref[...]


def last_wide(place, index, parts, gain, w_expand, after):
    _, _, rows, tile = parts[0].shape
    hidden = PLANE * tile
    return call(
        last_wide_kernel,
        "last_wide",
        [place, index, *parts, gain, (w_expand,)],
        [shape_of((rows, hidden), f32)] * 2 + [shape_of((1, rows), f32)],
        scratch=[pltpu.VMEM((rows, hidden), bf16)],
        copies=1,
        after=after,
        cost_us=2.0,
    )


def on_plane(
    segment,
    memory,
    compressed,
    document_labels,
    memory_filled_count,
    norm_gain,
    w_query,
    w_key,
    w_value,
    w_output,
    ffn_gain,
    w_expand,
    w_reduce,
    w_compress,
    result_cotangent,
    compressed_cotangent,
):
    _, rows, width = segment.shape
    blocks = lax.axis_size("blk")
    block = lax.axis_index("blk")
    place = lax.axis_index("stream")
    own = width // blocks
    seg_len = rows * blocks
    part_rows = width // (PLANE * blocks)
    chips = PLANE // 2
    segment, memory, compressed = segment[0], memory[0], compressed[0]
    cotangent, comp_cotangent = result_cotangent[0], compressed_cotangent[0]
    labels, filled = document_labels[0], memory_filled_count[0]
    gain = norm_gain.reshape(1, width)
    gain_ffn = ffn_gain.reshape(1, width)
    block_ref = block.astype(jnp.int32).reshape(1)
    place_ref = place.astype(jnp.int32).reshape(1)
    index = place * blocks + block
    index_ref = index.astype(jnp.int32).reshape(1)

    def along_blk(x, shift):
        return lax.ppermute(x, "blk", [(i, (i + shift) % blocks) for i in range(blocks)])

    def along_blk_flip(x, flip):
        return lax.ppermute(x, "blk", [(i, i ^ flip) for i in range(blocks)])

    def in_plane(x, flip):
        return lax.ppermute(x, "stream", [(i, i ^ flip) for i in range(PLANE)])

    owners = lax.rem(block - jnp.arange(blocks, dtype=jnp.int32) + blocks, blocks)
    by_owner = labels.reshape(3, blocks, rows).transpose(1, 0, 2)
    kdoc = by_owner[owners].reshape(blocks, 3 * rows)
    position = owners[:, None] * rows + jnp.arange(rows, dtype=jnp.int32)[None]
    first_filled = 2 * seg_len - filled
    kpos = jnp.concatenate(
        [
            jnp.where(position >= first_filled, -1, hidden_slot),
            jnp.where(position + seg_len >= first_filled, -1, hidden_slot),
            position,
        ],
        axis=1,
    ).astype(jnp.int32)
    qdoc = kdoc[:, 2 * rows :].reshape(blocks * rows, 1)
    qpos = position.reshape(blocks * rows, 1).astype(jnp.int32)
    marks = (qdoc, qpos, kdoc, kpos)

    def hop(arrays, after):
        arrays = [gate([x], after)[0] for x in arrays]
        return arrays, [along_blk(x, 1) for x in arrays]

    weights = (w_query, w_key, w_value)
    raw = [compressed, memory, segment]
    arriving = [along_blk(x, 1) for x in raw]
    pairs = memory.reshape(rows // RATE, RATE * width)
    projected = [project(block_ref, raw, gain, *weights, width, [])]
    query = projected[0][1]
    memories = [memory]
    raw, arriving = hop(arriving, [query])
    memories.append(raw[1])
    projected.append(raw)
    cots = [cotangent, in_plane(cotangent, 1)]
    for j in range(1, chips):
        cots.append(in_plane(cotangent, 2 * j))
        cots.append(in_plane(cots[-1], 1))
    projected[1] = project(block_ref, projected[1], gain, *weights, own, [])
    later = []
    for k in range(2, blocks - 1):
        raw, arriving = hop(arriving, [projected[1][1]])
        memories.append(raw[1])
        later.append(raw)
    memories.append(arriving[1])
    projected += [project(block_ref, rows3, gain, *weights, own, raw) for rows3 in later]
    keys, values = ([p[i] for p in projected] for i in (2, 3))
    partial = attend(query, keys, values, marks, [])
    *last, attended, normed_ffn_far, middle, normed_ffn = finish(
        blocks - 1,
        block_ref,
        arriving,
        gain,
        *weights,
        own,
        query,
        partial,
        marks,
        segment,
        w_output,
        gain_ffn,
        cots[2:],
    )
    projected.append(last)
    normed, queries, keys, values = ([p[i] for p in projected] for i in range(4))

    nfs = [normed_ffn, in_plane(normed_ffn, 1)]
    for j in range(1, chips - 1):
        nfs.append(in_plane(normed_ffn, 2 * j))
        nfs.append(in_plane(nfs[-1], 1))
    *both, res, dn, send = feed(
        place_ref,
        normed_ffn,
        nfs[1],
        cotangent,
        cots[1],
        w_expand,
        w_reduce,
        [],
    )
    sent = in_plane(send, 1)
    both = [both[0], in_plane(both[1], 2), in_plane(both[2], 4), both[3]]
    result, d_middle, d_branch, *d_attended = leave(
        block_ref,
        blocks,
        res,
        dn,
        sent,
        middle,
        cotangent,
        gain_ffn,
        w_output,
        nfs[3:6],
    )
    grads = [d_attended[0]] + [along_blk(d_attended[k], k) for k in range(1, blocks)]
    both[3], diagonal = gate([both[3], normed_ffn_far], grads[1:])
    both[3] = in_plane(both[3], 6)
    nfs.append(in_plane(diagonal, 6))
    comps = [comp_cotangent] + [along_blk(comp_cotangent, k) for k in range(1, blocks)]
    *pieces, dk, dv = attend_back(
        block_ref, queries, grads, keys, values, marks, both[1:3]
    )
    arrived = [pieces[0]] + [along_blk(pieces[k], -k) for k in range(1, blocks)]
    (nfs[6],) = gate([nfs[6]], [(pieces[0],)])
    nfs.append(in_plane(nfs[6], 1))
    qkv_keep, qkv_give = heads_gradient(
        place_ref, normed, pieces, dk, dv, blocks * part_rows, [(nfs[6],), both[3], *comps[1:]]
    )
    other_keep, other_give = other_gradients(
        place_ref,
        block_ref,
        attended,
        d_branch,
        memories,
        comps,
        blocks * part_rows,
        [(qkv_keep,)],
    )
    qkv_give, other_give = gate([qkv_give, other_give], [(other_keep,)])
    part, *moved = plane_gradients(
        block_ref, cots, nfs, both, blocks, part_rows, [(other_keep,), *arrived[1:]]
    )
    four = pair_add(
        place_ref, qkv_keep, in_plane(qkv_give, 1), other_keep, in_plane(other_give, 1), moved
    )
    before = (four[0],)
    for k in range(2, blocks):
        for i in range(2):
            moved[i] = ring_add(block_ref, i, k, along_blk(moved[i], 1), part, [before])
            before = moved[i]
        if k == 2:
            new_compressed = compress(pairs, w_compress, [before])
            before = (new_compressed,)
    four = [four[0]] + [in_plane(four[j], 2 * j) for j in range(1, chips)]
    moved = [along_blk(x, 1) for x in moved]
    grad_segment = segment_gradient(
        block_ref, arrived, *weights, segment, gain, d_middle, [before]
    )
    *parts, grad_compress = chip_add(
        block_ref, blocks, four, 3 * own + width, [(grad_segment,), moved[0]]
    )
    parts = [parts[0]] + [along_blk_flip(parts[k], k) for k in range(1, blocks)]
    wide_keep, wide_give = spread(place_ref, block_ref, moved, part, [parts[0]])
    wide_got = in_plane(wide_give, 1)
    wide = join(wide_keep, wide_got)
    wide = [in_plane(wide[j - 1], 2 * j) for j in range(1, chips)]

    def mine(x):
        return lax.dynamic_slice_in_dim(x, index * part_rows, part_rows, 0).reshape(1, -1)

    grad_query, grad_key, grad_value, grad_output, grad_norm_gain = last_heads(
        block_ref, index_ref, parts, mine(norm_gain), *weights, [grad_segment]
    )
    grad_expand, reduce_turned, grad_ffn_gain = last_wide(
        place_ref, index_ref, [wide_keep, wide_got, *wide], mine(ffn_gain), w_expand, [(grad_query,)]
    )
    return (
        result[None],
        new_compressed[None],
        grad_segment[None],
        grad_norm_gain.reshape(-1),
        grad_query,
        grad_key,
        grad_value,
        grad_output,
        grad_ffn_gain.reshape(-1),
        grad_expand,
        reduce_turned.T,
        grad_compress,
    )


def layer_norm(rows_in, gain):
    center = jnp.mean(rows_in, axis=-1, keepdims=True)
    offset = rows_in - center
    spread = jnp.mean(offset * offset, axis=-1, keepdims=True)
    return offset * lax.rsqrt(spread + epsilon) * gain


def exact_gelu(values_in):
    return jax.nn.gelu(values_in, approximate=False)


def on_any(
    segment,
    memory,
    compressed,
    document_labels,
    memory_filled_count,
    norm_gain,
    w_query,
    w_key,
    w_value,
    w_output,
    ffn_gain,
    w_expand,
    w_reduce,
    w_compress,
    result_cotangent,
    compressed_cotangent,
):
    streams, block_rows, model_width = segment.shape
    head_count = model_width // HD
    blocks = lax.axis_size("blk")
    my_block = lax.axis_index("blk")
    seg_len = block_rows * blocks
    key_count = 3 * seg_len
    score_scale = HD ** (-0.5)
    stacked = jnp.concatenate([compressed, memory, segment], axis=1).astype(jnp.float32)
    normed_full, norm_pull = jax.vjp(layer_norm, stacked, norm_gain)
    normed = normed_full.astype(jnp.bfloat16)
    seg_normed = normed[:, 2 * block_rows :]
    queries = jnp.einsum(
        "srd,de->sre", seg_normed, w_query, preferred_element_type=jnp.float32
    ).astype(jnp.bfloat16)
    query_heads = queries.reshape(streams, block_rows, head_count, HD)
    keys = jnp.einsum("srd,de->rse", normed, w_key, preferred_element_type=jnp.float32).astype(
        jnp.bfloat16
    )
    values = jnp.einsum("srd,de->rse", normed, w_value, preferred_element_type=jnp.float32).astype(
        jnp.bfloat16
    )
    all_keys, all_values = (
        lax.all_gather(keys, "blk", axis=0, tiled=True),
        lax.all_gather(values, "blk", axis=0, tiled=True),
    )
    key_index = jnp.arange(key_count, dtype=jnp.int32)
    key_owner = key_index // (3 * block_rows)
    within = key_index % (3 * block_rows)
    key_kind = within // block_rows
    key_pos = key_owner * block_rows + within % block_rows
    key_slot = key_kind * seg_len + key_pos
    key_docs = (
        document_labels.reshape(streams, 3, blocks, block_rows)
        .transpose(0, 2, 1, 3)
        .reshape(streams, key_count)
    )
    query_pos = my_block * block_rows + jnp.arange(block_rows, dtype=jnp.int32)
    query_docs = lax.dynamic_slice_in_dim(
        document_labels[:, 2], my_block * block_rows, block_rows, 1
    )
    in_memory = key_slot[None, :] >= 2 * seg_len - memory_filled_count[:, None]
    causal = key_pos[None, :] <= query_pos[:, None]
    visible = jnp.where((key_kind < 2)[None, None, :], in_memory[:, None, :], causal[None, :, :])
    allowed = visible & (key_docs[:, None, :] == query_docs[:, :, None])

    def scores_of(key_set):
        key_view = key_set.reshape(key_count, streams, head_count, HD)
        raw_scores = (
            jnp.einsum("sqhd,kshd->shqk", query_heads, key_view, preferred_element_type=jnp.float32)
            * score_scale
        )
        return jnp.where(allowed[:, None], raw_scores, masked_score)

    scores = scores_of(all_keys)
    row_top = jnp.max(scores, axis=-1, keepdims=True)
    weights = jnp.exp(scores - row_top)
    row_total = jnp.sum(weights, axis=-1, keepdims=True)
    probs = (weights / row_total).astype(jnp.bfloat16)
    log_total = row_top + jnp.log(row_total)
    value_heads = all_values.reshape(key_count, streams, head_count, HD)
    attended = jnp.einsum("shqk,kshd->sqhd", probs, value_heads, preferred_element_type=jnp.float32)
    attended = attended.reshape(streams, block_rows, model_width).astype(jnp.bfloat16)
    middle = segment.astype(jnp.float32) + jnp.einsum(
        "sre,ed->srd", attended, w_output, preferred_element_type=jnp.float32
    )
    normed_ffn_full, ffn_pull = jax.vjp(layer_norm, middle, ffn_gain)
    normed_ffn = normed_ffn_full.astype(jnp.bfloat16)
    hidden = jnp.einsum("srd,df->srf", normed_ffn, w_expand, preferred_element_type=jnp.float32)
    activated_full, gelu_pull = jax.vjp(exact_gelu, hidden)
    activated = activated_full.astype(jnp.bfloat16)
    result = (
        middle + jnp.einsum("srf,fd->srd", activated, w_reduce, preferred_element_type=jnp.float32)
    ).astype(jnp.bfloat16)
    mem_pairs = memory.reshape(streams, block_rows // RATE, RATE * model_width)
    new_compressed = jnp.einsum(
        "srp,pd->srd", mem_pairs, w_compress, preferred_element_type=jnp.float32
    ).astype(jnp.bfloat16)
    reduce_turned = jnp.einsum(
        "srd,srf->df", result_cotangent, activated, preferred_element_type=jnp.float32
    )
    d_activated = jnp.einsum(
        "srd,fd->srf", result_cotangent, w_reduce, preferred_element_type=jnp.float32
    )
    d_hidden = gelu_pull(d_activated)[0].astype(jnp.bfloat16)
    grad_expand = jnp.einsum(
        "srd,srf->df", normed_ffn, d_hidden, preferred_element_type=jnp.float32
    )
    d_normed_ffn = jnp.einsum("srf,df->srd", d_hidden, w_expand, preferred_element_type=jnp.float32)
    d_middle_norm, grad_ffn_gain = ffn_pull(d_normed_ffn)
    d_middle = result_cotangent.astype(jnp.float32) + d_middle_norm
    d_branch = d_middle.astype(jnp.bfloat16)
    grad_output = jnp.einsum("sre,srd->ed", attended, d_branch, preferred_element_type=jnp.float32)
    d_attended = jnp.einsum(
        "srd,ed->sre", d_branch, w_output, preferred_element_type=jnp.float32
    ).astype(jnp.bfloat16)
    d_attended = d_attended.reshape(streams, block_rows, head_count, HD)
    key_heads = all_keys.reshape(key_count, streams, head_count, HD)
    probs_full = jnp.exp(scores_of(all_keys) - log_total)
    probs_low = probs_full.astype(jnp.bfloat16)
    d_probs = jnp.einsum(
        "sqhd,kshd->shqk", d_attended, value_heads, preferred_element_type=jnp.float32
    )
    row_delta = jnp.sum(probs_full * d_probs, axis=-1, keepdims=True)
    d_scores = (probs_full * (d_probs - row_delta)).astype(jnp.bfloat16)
    d_queries = (
        jnp.einsum("shqk,kshd->sqhd", d_scores, key_heads, preferred_element_type=jnp.float32)
        * score_scale
    )
    d_queries = d_queries.astype(jnp.bfloat16).reshape(streams, block_rows, model_width)
    count = 3 * block_rows * lax.axis_size("blk")
    key_part = (
        jnp.einsum("shqk,sqhd->kshd", d_scores, query_heads, preferred_element_type=jnp.float32)
        * score_scale
    )
    value_part = jnp.einsum(
        "shqk,sqhd->kshd", probs_low, d_attended, preferred_element_type=jnp.float32
    )
    key_grads = lax.psum_scatter(
        jnp.stack(
            [
                key_part.reshape(count, streams, model_width),
                value_part.reshape(count, streams, model_width),
            ],
            axis=1,
        ).astype(jnp.bfloat16),
        "blk",
        scatter_dimension=0,
        tiled=True,
    ).astype(jnp.float32)
    d_keys = key_grads[:, 0].astype(jnp.bfloat16)
    d_values = key_grads[:, 1].astype(jnp.bfloat16)
    grad_query = jnp.einsum(
        "srd,sre->de", seg_normed, d_queries, preferred_element_type=jnp.float32
    )
    grad_key = jnp.einsum("srd,rse->de", normed, d_keys, preferred_element_type=jnp.float32)
    grad_value = jnp.einsum("srd,rse->de", normed, d_values, preferred_element_type=jnp.float32)
    d_normed = jnp.einsum("rse,de->srd", d_keys, w_key, preferred_element_type=jnp.float32)
    d_normed = d_normed + jnp.einsum(
        "rse,de->srd", d_values, w_value, preferred_element_type=jnp.float32
    )
    d_seg_normed = jnp.einsum("sre,de->srd", d_queries, w_query, preferred_element_type=jnp.float32)
    d_normed = d_normed + jnp.pad(d_seg_normed, ((0, 0), (2 * block_rows, 0), (0, 0)))
    d_stacked, grad_norm_gain = norm_pull(d_normed)
    grad_segment = (d_middle + d_stacked[:, 2 * block_rows :]).astype(jnp.bfloat16)
    grad_compress = jnp.einsum(
        "srp,srd->pd", mem_pairs, compressed_cotangent, preferred_element_type=jnp.float32
    )
    weight_grads = (
        grad_norm_gain,
        grad_query,
        grad_key,
        grad_value,
        grad_output,
        grad_ffn_gain,
        grad_expand,
        reduce_turned,
        grad_compress,
    )
    summed = (
        lax.psum_scatter(weight_grads[0], ("stream", "blk"), scatter_dimension=0, tiled=True),
        lax.psum_scatter(weight_grads[1], ("stream", "blk"), scatter_dimension=0, tiled=True),
        lax.psum_scatter(weight_grads[2], ("stream", "blk"), scatter_dimension=0, tiled=True),
        lax.psum_scatter(weight_grads[3], ("stream", "blk"), scatter_dimension=0, tiled=True),
        lax.psum_scatter(weight_grads[4], ("stream", "blk"), scatter_dimension=0, tiled=True),
        lax.psum_scatter(weight_grads[5], ("stream", "blk"), scatter_dimension=0, tiled=True),
        lax.psum_scatter(weight_grads[6], ("stream", "blk"), scatter_dimension=0, tiled=True),
        lax.psum_scatter(weight_grads[7], ("stream", "blk"), scatter_dimension=0, tiled=True),
        lax.psum_scatter(weight_grads[8], ("stream", "blk"), scatter_dimension=0, tiled=True),
    )
    grad_reduce = summed[7].T
    return (
        result,
        new_compressed,
        grad_segment,
        summed[0],
        summed[1],
        summed[2],
        summed[3],
        summed[4],
        summed[5],
        summed[6],
        grad_reduce,
        summed[8],
    )


def solution(mesh):
    tokens = P("stream", "blk", None)
    both = ("stream", "blk")
    in_specs = (
        (tokens,) * 3
        + (P("stream", None, None), P("stream"))
        + (P(),) * 9
        + (tokens,) * 2
    )
    out_specs = (
        (tokens,) * 3
        + (P(both),)
        + (P(both, None),) * 4
        + (P(both), P(both, None), P(None, both), P(both, None))
    )
    one_plane = mesh.shape["stream"] == PLANE
    return jax.shard_map(
        on_plane if one_plane else on_any, mesh=mesh, in_specs=in_specs, out_specs=out_specs, check_vma=False
    )
```

```python
import functools

import jax
import jax.numpy as jnp
from jax import lax
from jax.experimental import pallas as pl
from jax.experimental.pallas import tpu as pltpu
from jax.sharding import PartitionSpec as P

HD = 128
RATE = 2
PLANE = 8

epsilon = 1e-05
masked_score = -1e30
hidden_slot = 1 << 30

f32 = jnp.float32
bf16 = jnp.bfloat16
MIB = 1 << 20
FLOPS_PER_US = 0.5e9
VM = pl.BlockSpec(memory_space=pltpu.VMEM)
SM = pl.BlockSpec(memory_space=pltpu.SMEM)
ANY = pl.BlockSpec(memory_space=pl.ANY)


def dot(left, right, contract=((1,), (0,))):
    return lax.dot_general(left, right, (contract, ((), ())), preferred_element_type=f32)


def standardized(rows):
    offset = rows - jnp.mean(rows, axis=-1, keepdims=True)
    scale = lax.rsqrt(jnp.mean(offset * offset, axis=-1, keepdims=True) + epsilon)
    return offset * scale, scale


def norm_input_gradient(e, gain, unit, scale):
    eg = e * gain
    return scale * (
        eg
        - jnp.mean(eg, axis=-1, keepdims=True)
        - unit * jnp.mean(eg * unit, axis=-1, keepdims=True)
    )


LOG2E = 1.4426950408889634
SCORE_SCALE = HD ** (-0.5) * LOG2E
LAST = ((1,), (1,))
FIRST = ((0,), (0,))
TILE = 256


def in_hbm(x):
    return pltpu.with_memory_space_constraint(x, pltpu.HBM)


def block_of(shape):
    return pl.BlockSpec(shape, lambda i: (0,) * len(shape))


def call(
    kernel, name, ins, outs, scratch=(), copies=0, grant=24, after=(), cost_us=1.0
):
    in_specs, operands = [], []
    inputs = len(ins)

    def body(*refs):
        kernel(*refs[:inputs], *refs[inputs + len(after) :])

    for x in ins:
        far = isinstance(x, tuple)
        x = x[0] if far else x
        operands.append(in_hbm(x) if far else x)
        in_specs.append(ANY if far else SM if x.size == 1 else block_of(x.shape))
    operands += [in_hbm(x[0]) if isinstance(x, tuple) else x for x in after]
    in_specs += [ANY] * len(after)
    scratch = list(scratch)
    if copies:
        scratch.append(pltpu.SemaphoreType.DMA((copies,)))
    return pl.pallas_call(
        body,
        grid=(1,),
        in_specs=in_specs,
        out_specs=[ANY if isinstance(o, tuple) else block_of(o.shape) for o in outs],
        out_shape=[
            pltpu.HBM(o[0].shape, o[0].dtype) if isinstance(o, tuple) else o for o in outs
        ],
        scratch_shapes=scratch,
        compiler_params=pltpu.CompilerParams(vmem_limit_bytes=grant * MIB),
        cost_estimate=pl.CostEstimate(
            flops=int(cost_us * FLOPS_PER_US), bytes_accessed=0, transcendentals=0
        ),
        name=name,
    )(*operands)


def gate(arrays, after):
    count = len(arrays)
    return pl.pallas_call(
        lambda *refs: None,
        in_specs=[ANY] * (count + len(after)),
        out_specs=[ANY] * count,
        out_shape=[pltpu.HBM(x.shape, x.dtype) for x in arrays],
        input_output_aliases={i: i for i in range(count)},
        compiler_params=pltpu.CompilerParams(vmem_limit_bytes=MIB),
        cost_estimate=pl.CostEstimate(flops=0, bytes_accessed=0, transcendentals=0),
        name="gate",
    )(*arrays, *[in_hbm(x[0]) if isinstance(x, tuple) else x for x in after])


class Copies:
    def __init__(self, sems):
        self.sems, self.count = sems, 0

    def __call__(self, source, target):
        copy = pltpu.make_async_copy(source, target, self.sems.at[self.count])
        copy.start()
        self.count += 1
        return copy


def lanes(start, size):
    return pl.ds(pl.multiple_of(start, size), size)


def shape_of(shape, dtype=bf16):
    return jax.ShapeDtypeStruct(shape, dtype)


def norm_rows(raw, gain_ref, normed_ref):
    rows = raw.shape[1]
    for i in range(raw.shape[0]):
        unit, _ = standardized(raw[i].astype(f32))
        normed_ref[i * rows : (i + 1) * rows, :] = (unit * gain_ref[...]).astype(bf16)


ROW_CUTS = 4


def bring_rows(bring, source, target):
    step = source.shape[0] // ROW_CUTS
    return [
        bring(source.at[pl.ds(i * step, step)], target.at[pl.ds(i * step, step)])
        for i in range(ROW_CUTS)
    ]


def wait_all(copies):
    for copy in copies:
        copy.wait()


def project_kernel(all_queries, *refs):
    block_ref, *raw_refs = refs[:4]
    gain_ref, wq_ref, wk_ref, wv_ref = refs[4:8]
    outs = refs[8:12]
    wq, wk, wv, normed_ref, q_ref, k_ref, v_ref, raw, sems = refs[12:]
    bring = Copies(sems)
    width = k_ref.shape[1]
    raws = [bring(ref, raw.at[i]) for i, ref in enumerate(raw_refs)]
    coming = [bring_rows(bring, wk_ref, wk), bring_rows(bring, wv_ref, wv)]
    if all_queries:
        query_weight = bring(wq_ref, wq)
    else:
        own = q_ref.shape[1]
        query_weight = bring(wq_ref.at[:, lanes(block_ref[0] * own, own)], wq)
    wait_all(raws)
    norm_rows(raw, gain_ref, normed_ref)
    leaving = [bring(normed_ref, outs[0])]
    normed = normed_ref[...]
    for copies, weight, target, out in zip(coming, (wk, wv), (k_ref, v_ref), outs[2:]):
        wait_all(copies)
        for at in range(0, width, TILE):
            target[:, at : at + TILE] = dot(normed, weight[:, at : at + TILE]).astype(bf16)
        leaving.append(bring(target, out))
    query_weight.wait()
    q_ref[...] = dot(normed[2 * raw.shape[1] :], wq[...]).astype(bf16)
    leaving.append(bring(q_ref, outs[1]))
    wait_all(leaving)


def projected_shapes(rows, width, own):
    return [
        shape_of((3 * rows, width)),
        shape_of((rows, own)),
        shape_of((3 * rows, width)),
        shape_of((3 * rows, width)),
    ]


def project(block, raw_rows, gain, w_query, w_key, w_value, own, after):
    rows, width = raw_rows[0].shape
    shapes = projected_shapes(rows, width, own)
    weights = [(width, own), (width, width), (width, width)]
    return call(
        functools.partial(project_kernel, own == width),
        "project",
        [block] + [(x,) for x in raw_rows] + [gain, (w_query,), (w_key,), (w_value,)],
        [(x,) for x in shapes],
        scratch=[pltpu.VMEM(x, bf16) for x in weights]
        + [pltpu.VMEM(x.shape, x.dtype) for x in shapes]
        + [pltpu.VMEM((3, rows, width), bf16)],
        copies=2 * ROW_CUTS + 8,
        after=after,
        cost_us=0.1,
    )


def compress_kernel(pairs_ref, w_far, out_ref, w_ref, sems):
    bring = Copies(sems)
    count = w_ref.shape[0]
    coming = [bring(w_far.at[pl.ds(i * w_ref.shape[1], w_ref.shape[1])], w_ref.at[i]) for i in range(count)]
    total = None
    for i in range(count):
        coming[i].wait()
        part = dot(pairs_ref[:, i * w_ref.shape[1] : (i + 1) * w_ref.shape[1]], w_ref[i])
        total = part if total is None else total + part
    out_ref[...] = total.astype(bf16)


def compress(pairs, w_compress, after):
    depth, width = w_compress.shape
    count = 4
    return call(
        compress_kernel,
        "compress",
        [pairs, (w_compress,)],
        [shape_of((pairs.shape[0], width))],
        scratch=[pltpu.VMEM((count, depth // count, width), bf16)],
        copies=count,
        after=after,
        cost_us=3.2,
    )[0]


def score_bias(qdoc, qpos, kdoc_ref, kpos_ref, slot):
    allowed = (kdoc_ref[slot : slot + 1, :] == qdoc) & (kpos_ref[slot : slot + 1, :] <= qpos)
    return jnp.where(allowed, 0.0, masked_score)


def attend_kernel(slots, *refs):
    qdoc_ref, qpos_ref, kdoc_ref, kpos_ref, q_far = refs[:5]
    k_far = refs[5 : 5 + slots]
    v_far = refs[5 + slots : 5 + 2 * slots]
    out_ref, stat_ref, bias_ref, q_ref, k_ref, v_ref, sems = refs[5 + 2 * slots :]
    rows, width = q_ref.shape
    bring = Copies(sems)
    query = bring(q_far, q_ref)
    tiles = [slice(at, at + TILE) for at in range(0, width, TILE)]
    coming = [
        [
            bring(far[slot].at[:, at], near.at[slot, :, at])
            for slot in range(slots)
            for far, near in ((k_far, k_ref), (v_far, v_ref))
        ]
        for at in tiles
    ]
    qdoc, qpos = qdoc_ref[:rows, :], qpos_ref[:rows, :]
    for slot in range(slots):
        bias_ref[slot] = score_bias(qdoc, qpos, kdoc_ref, kpos_ref, slot)
    query.wait()
    lane = lax.broadcasted_iota(jnp.int32, (rows, HD), 1)
    stats = jnp.zeros((rows, HD), f32)
    heads = width // HD
    for head in range(heads):
        if head * HD % TILE == 0:
            for copy in coming[head * HD // TILE]:
                copy.wait()
        at = slice(head * HD, (head + 1) * HD)
        q = q_ref[:, at]
        scores = [
            dot(q, k_ref[slot, :, at], LAST) * SCORE_SCALE + bias_ref[slot]
            for slot in range(slots)
        ]
        top = functools.reduce(jnp.maximum, scores)
        top = jnp.max(top, axis=-1, keepdims=True)
        weights = [jnp.exp2(s - top) for s in scores]
        total = jnp.sum(functools.reduce(jnp.add, weights), axis=-1, keepdims=True)
        out_ref[:, at] = functools.reduce(
            jnp.add,
            [dot(weights[slot].astype(bf16), v_ref[slot, :, at]) for slot in range(slots)],
        )
        stats = jnp.where(lane == head, top, stats)
        stats = jnp.where(lane == heads + head, total, stats)
    stat_ref[...] = stats


def attend(query, keys, values, marks, after):
    slots = len(keys)
    rows, width = query.shape
    key_rows = keys[0].shape[0]
    return call(
        functools.partial(attend_kernel, slots),
        "attend",
        [*marks, (query,)] + [(x,) for x in (*keys, *values)],
        [shape_of((rows, width), f32), shape_of((rows, HD), f32)],
        scratch=[
            pltpu.VMEM((slots, rows, key_rows), f32),
            pltpu.VMEM((rows, width), bf16),
            pltpu.VMEM((slots, key_rows, width), bf16),
            pltpu.VMEM((slots, key_rows, width), bf16),
        ],
        copies=1 + 2 * slots * (width // TILE),
        after=after,
        cost_us=0.1,
    )


def finish_kernel(slot, *refs):
    block_ref, *raw_refs = refs[:4]
    gain_ref, wq_far, wk_far, wv_far = refs[4:8]
    query_far, sum_ref, stat_ref, qdoc_ref, qpos_ref, kdoc_ref, kpos_ref = refs[8:15]
    seg_ref, wo_far, gain_ffn_ref = refs[15:18]
    outs = refs[18:24]
    middle_ref, nf_ref = refs[24:26]
    wq, wk, wv, normed_ref, q_ref, k_ref, v_ref, wo, query_ref, att_ref, raw, nf_copy, sems = refs[26:]
    rows, width = query_ref.shape
    bring = Copies(sems)
    raws = [bring(ref, raw.at[i]) for i, ref in enumerate(raw_refs)]
    coming = [bring_rows(bring, wk_far, wk), bring_rows(bring, wv_far, wv)]
    query = bring(query_far, query_ref)
    output_weight = bring(wo_far, wo)
    own = q_ref.shape[1]
    query_weight = bring(wq_far.at[:, lanes(block_ref[0] * own, own)], wq)
    bias = score_bias(qdoc_ref[:rows, :], qpos_ref[:rows, :], kdoc_ref, kpos_ref, slot)
    wait_all(raws)
    norm_rows(raw, gain_ref, normed_ref)
    leaving = [bring(normed_ref, outs[0])]
    normed = normed_ref[...]
    query.wait()
    heads = width // HD
    for copies, weight, target, out in zip(coming, (wk, wv), (k_ref, v_ref), outs[2:4]):
        wait_all(copies)
        for at in range(0, width, TILE):
            target[:, at : at + TILE] = dot(normed, weight[:, at : at + TILE]).astype(bf16)
        leaving.append(bring(target, out))
    group = 4
    for start in range(0, heads, group):
        some = range(start, start + group)
        at = {h: slice(h * HD, (h + 1) * HD) for h in some}
        scores = {
            h: dot(query_ref[:, at[h]], k_ref[:, at[h]], LAST) * SCORE_SCALE + bias for h in some
        }
        before = {h: stat_ref[:, h : h + 1] for h in some}
        top = {
            h: jnp.maximum(before[h], jnp.max(scores[h], axis=-1, keepdims=True)) for h in some
        }
        weights = {h: jnp.exp2(scores[h] - top[h]) for h in some}
        shrink = {h: jnp.exp2(before[h] - top[h]) for h in some}
        total = {
            h: stat_ref[:, heads + h : heads + h + 1] * shrink[h]
            + jnp.sum(weights[h], axis=-1, keepdims=True)
            for h in some
        }
        out = {
            h: sum_ref[:, at[h]] * shrink[h] + dot(weights[h].astype(bf16), v_ref[:, at[h]])
            for h in some
        }
        for h in some:
            att_ref[:, at[h]] = (out[h] * (1.0 / total[h])).astype(bf16)
    query_weight.wait()
    q_ref[...] = dot(normed[2 * raw.shape[1] :], wq[...]).astype(bf16)
    leaving.append(bring(q_ref, outs[1]))
    leaving.append(bring(att_ref, outs[4]))
    output_weight.wait()
    middle = seg_ref[...].astype(f32) + dot(att_ref[...], wo[...])
    middle_ref[...] = middle
    unit, _ = standardized(middle)
    nf_ref[...] = (unit * gain_ffn_ref[...]).astype(bf16)
    nf_copy[...] = nf_ref[...]
    leaving.append(bring(nf_copy, outs[5]))
    wait_all(leaving)


def finish(
    slot, block, raw_rows, gain, w_query, w_key, w_value, own, query, partial, marks, segment, w_output, gain_ffn, after
):
    rows, width = segment.shape
    shapes = projected_shapes(rows, width, own)
    weights = [(width, own), (width, width), (width, width)]
    return call(
        functools.partial(finish_kernel, slot),
        "finish",
        [block] + [(x,) for x in raw_rows] + [gain, (w_query,), (w_key,), (w_value,), (query,), *partial, *marks]
        + [segment, (w_output,), gain_ffn],
        [(x,) for x in shapes]
        + [(shape_of((rows, width)),)] * 2
        + [shape_of((rows, width), f32), shape_of((rows, width))],
        scratch=[pltpu.VMEM(x, bf16) for x in weights]
        + [pltpu.VMEM(x.shape, x.dtype) for x in shapes]
        + [
            pltpu.VMEM((width, width), bf16),
            pltpu.VMEM((rows, width), bf16),
            pltpu.VMEM((rows, width), bf16),
            pltpu.VMEM((3, rows, width), bf16),
            pltpu.VMEM((rows, width), bf16),
        ],
        copies=2 * ROW_CUTS + 12,
        after=after,
        cost_us=0.1,
    )


def feed_kernel(chips, place_ref, nf_own, nf_got, cot_own, cot_got, we_far, wr_far, *refs):
    both_far = refs[:chips]
    res_ref, dn_ref, send_ref, nf_ref, cot_ref, both, we, wr, res, dn, sems = refs[chips:]
    rows = nf_own.shape[0]
    tile = wr.shape[1]
    bring = Copies(sems)
    coming = []
    for chip in range(chips):
        at = lanes((place_ref[0] ^ (2 * chip)) * tile, tile)
        coming.append(bring(we_far.at[:, at], we.at[chip]))
        coming.append(bring(wr_far.at[at, :], wr.at[chip]))
    nf_ref[:rows] = nf_own[...]
    nf_ref[rows:] = nf_got[...]
    cot_ref[:rows] = cot_own[...]
    cot_ref[rows:] = cot_got[...]
    res[...] = jnp.zeros_like(res)
    dn[...] = jnp.zeros_like(dn)
    part = tile // 2

    @pl.loop(0, chips)
    def _(chip):
        pltpu.make_async_copy(we.at[chip], we.at[chip], sems.at[2 * chip]).wait()
        pltpu.make_async_copy(wr.at[chip], wr.at[chip], sems.at[2 * chip + 1]).wait()
        for at in range(0, tile, part):
            here = slice(at, at + part)
            hidden = dot(nf_ref[...], we[chip, :, here])
            d_act = dot(cot_ref[...], wr[chip, here, :], LAST)
            cdf = 0.5 + 0.5 * lax.erf(hidden * (0.5**0.5))
            density = jnp.exp2(hidden * hidden * (-0.5 * LOG2E)) * 0.3989422804014327
            both[chip, 0, :, here] = (hidden * cdf).astype(bf16)
            both[chip, 1, :, here] = (d_act * (cdf + hidden * density)).astype(bf16)
        res[...] += dot(both[chip, 0], wr[chip])
        dn[...] += dot(both[chip, 1], we[chip], LAST)

    leaving = [bring(both.at[chip], both_far[chip]) for chip in range(chips)]
    res_ref[...] = res[:rows]
    dn_ref[...] = dn[:rows]
    send_ref[0] = res[rows:].astype(bf16)
    send_ref[1] = dn[rows:].astype(bf16)
    wait_all(leaving)


def feed(place, nf_own, nf_got, cot_own, cot_got, w_expand, w_reduce, after):
    rows, width = nf_own.shape
    chips = PLANE // 2
    tile = w_expand.shape[1] // PLANE
    return call(
        functools.partial(feed_kernel, chips),
        "feed",
        [place, nf_own, nf_got, cot_own, cot_got, (w_expand,), (w_reduce,)],
        [(shape_of((2, 2 * rows, tile)),)] * chips
        + [shape_of((rows, width), f32)] * 2
        + [shape_of((2, rows, width))],
        scratch=[
            pltpu.VMEM((2 * rows, width), bf16),
            pltpu.VMEM((2 * rows, width), bf16),
            pltpu.VMEM((chips, 2, 2 * rows, tile), bf16),
            pltpu.VMEM((chips, width, tile), bf16),
            pltpu.VMEM((chips, tile, width), bf16),
            pltpu.VMEM((2 * rows, width), f32),
            pltpu.VMEM((2 * rows, width), f32),
        ],
        copies=3 * chips,
        grant=28,
        after=after,
        cost_us=0.1,
    )


def leave_kernel(slots, block_ref, *refs):
    res_ref, dn_ref, got_ref, middle_ref, cot_ref, gain_ref, wo_far = refs[:7]
    result_ref, dmid_far, branch_far = refs[7:10]
    datt_refs = refs[10 : 10 + slots]
    wo, dmid_ref, branch_ref, sems = refs[10 + slots :]
    own = wo.shape[1]
    bring = Copies(sems)
    coming = [
        bring(wo_far.at[lanes(lax.rem(block_ref[0] + slot, slots) * own, own), :], wo.at[slot])
        for slot in range(slots)
    ]
    middle = middle_ref[...]
    result_ref[...] = (middle + (res_ref[...] + got_ref[0].astype(f32))).astype(bf16)
    unit, scale = standardized(middle)
    d_normed = dn_ref[...] + got_ref[1].astype(f32)
    d_mid = cot_ref[...].astype(f32) + norm_input_gradient(d_normed, gain_ref[...], unit, scale)
    dmid_ref[...] = d_mid
    branch = d_mid.astype(bf16)
    branch_ref[...] = branch
    leaving = [bring(dmid_ref, dmid_far), bring(branch_ref, branch_far)]
    for slot in range(slots):
        coming[slot].wait()
        datt_refs[slot][...] = dot(branch, wo[slot], LAST).astype(bf16)
    wait_all(leaving)


def leave(block, slots, res, dn, got, middle, cotangent, gain, w_output, after):
    rows, width = middle.shape
    own = width // slots
    return call(
        functools.partial(leave_kernel, slots),
        "leave",
        [block, res, dn, got, middle, cotangent, gain, (w_output,)],
        [shape_of((rows, width)), (shape_of((rows, width), f32),), (shape_of((rows, width)),)]
        + [shape_of((rows, own))] * slots,
        scratch=[
            pltpu.VMEM((slots, own, width), bf16),
            pltpu.VMEM((rows, width), f32),
            pltpu.VMEM((rows, width), bf16),
        ],
        copies=slots + 2,
        after=after,
        cost_us=3.8,
    )


def attend_back_kernel(slots, heads, block_ref, *refs):
    take = iter(refs)
    marks = [next(take) for _ in range(4)]
    g_refs = [next(take) for _ in range(slots)]
    q_far = [next(take) for _ in range(slots)]
    k_far = [next(take) for _ in range(slots)]
    v_far = [next(take) for _ in range(slots)]
    piece_far = [next(take) for _ in range(slots)]
    dk_far, dv_far, q_ref, k_ref, v_ref, piece_refs, dk_ref, dv_ref, sems = take
    qdoc_ref, qpos_ref, kdoc_ref, kpos_ref = marks
    scale = HD ** (-0.5)
    rows = g_refs[0].shape[0]
    own = heads * HD
    bring = Copies(sems)
    owned = lanes(block_ref[0] * own, own)
    coming = []
    for slot in range(slots):
        coming.append(bring(q_far[slot].at[:, owned] if slot == 0 else q_far[slot], q_ref.at[slot]))
        coming.append(bring(k_far[slot].at[:, owned], k_ref.at[slot]))
        coming.append(bring(v_far[slot].at[:, owned], v_ref.at[slot]))
    for copy in coming:
        copy.wait()
    dk = [[None] * slots for _ in range(heads)]
    dv = [[None] * slots for _ in range(heads)]
    for one in range(slots):
        here = slice(one * rows, (one + 1) * rows)
        qdoc, qpos = qdoc_ref[here, :], qpos_ref[here, :]
        bias = [score_bias(qdoc, qpos, kdoc_ref, kpos_ref, slot) for slot in range(slots)]
        every = range(heads)
        at = [slice(head * HD, (head + 1) * HD) for head in every]
        q = [q_ref[one, :, at[head]] for head in every]
        grad = [g_refs[one][:, at[head]] for head in every]
        scores = [
            [
                dot(q[head], k_ref[slot, :, at[head]], LAST) * SCORE_SCALE + bias[slot]
                for slot in range(slots)
            ]
            for head in every
        ]
        d_probs = [
            [dot(grad[head], v_ref[slot, :, at[head]], LAST) for slot in range(slots)]
            for head in every
        ]
        top = [
            jnp.max(functools.reduce(jnp.maximum, scores[head]), axis=-1, keepdims=True)
            for head in every
        ]
        weights = [[jnp.exp2(x - top[head]) for x in scores[head]] for head in every]
        inverse = [
            1.0 / jnp.sum(functools.reduce(jnp.add, weights[head]), axis=-1, keepdims=True)
            for head in every
        ]
        probs = [[x * inverse[head] for x in weights[head]] for head in every]
        delta = [
            jnp.sum(
                functools.reduce(jnp.add, [p * d for p, d in zip(probs[head], d_probs[head])]),
                axis=-1,
                keepdims=True,
            )
            for head in every
        ]
        for head in every:
            d_score = [
                (p * (d - delta[head])).astype(bf16) for p, d in zip(probs[head], d_probs[head])
            ]
            dq = None
            for slot in range(slots):
                part = dot(d_score[slot], k_ref[slot, :, at[head]])
                dq = part if dq is None else dq + part
                dk_part = dot(q[head], d_score[slot], FIRST)
                dv_part = dot(grad[head], probs[head][slot].astype(bf16), FIRST)
                dk[head][slot] = dk_part if one == 0 else dk[head][slot] + dk_part
                dv[head][slot] = dv_part if one == 0 else dv[head][slot] + dv_part
            piece_refs[one, :, at[head]] = (dq * scale).astype(bf16)
    leaving = []
    for slot in range(slots):
        for head in range(heads):
            at = slice(head * HD, (head + 1) * HD)
            d_key = jnp.transpose((dk[head][slot] * scale).astype(bf16))
            d_value = jnp.transpose(dv[head][slot].astype(bf16))
            dk_ref[slot, :, at] = d_key
            dv_ref[slot, :, at] = d_value
            for i, value in enumerate((d_key, d_value)):
                first = (i + 1) * own + head * HD
                piece_refs[slot, :, first : first + HD] = value[2 * rows :]
        leaving.append(bring(piece_refs.at[slot], piece_far[slot]))
    leaving += [bring(dk_ref, dk_far), bring(dv_ref, dv_far)]
    wait_all(leaving)


def attend_back(block, queries, grads, keys, values, marks, after):
    slots = len(keys)
    key_rows = keys[0].shape[0]
    rows, own = grads[0].shape
    heads = own // HD
    return call(
        functools.partial(attend_back_kernel, slots, heads),
        "attend_back",
        [block, *marks, *grads] + [(x,) for x in (*queries, *keys, *values)],
        [(shape_of((rows, 3 * own)),)] * slots + [(shape_of((slots, key_rows, own)),)] * 2,
        scratch=[
            pltpu.VMEM((slots, rows, own), bf16),
            pltpu.VMEM((slots, key_rows, own), bf16),
            pltpu.VMEM((slots, key_rows, own), bf16),
            pltpu.VMEM((slots, rows, 3 * own), bf16),
            pltpu.VMEM((slots, key_rows, own), bf16),
            pltpu.VMEM((slots, key_rows, own), bf16),
        ],
        copies=4 * slots + 2,
        after=after,
        cost_us=4.0,
    )


def heads_kernel(slots, place_ref, *refs):
    piece_far = refs[:slots]
    normed_far = refs[slots : 2 * slots]
    dk_far, dv_far = refs[2 * slots : 2 * slots + 2]
    keep_far, give_far, out_ref, pieces, normed, dk, dv, sems = refs[2 * slots + 2 :]
    own = dk.shape[2]
    rows = pieces.shape[1]
    cut = out_ref.shape[2]
    core = lax.rem(place_ref[0], 2)
    bring = Copies(sems)
    second = [bring(normed_far[0], normed.at[0]), bring(dv_far, dv)]
    second += [bring(normed_far[slot], normed.at[slot]) for slot in range(1, slots)]
    third = [bring(dk_far, dk)]
    fourth = [bring(piece_far[slot], pieces.at[slot]) for slot in range(slots)]
    leaving = []

    def store(value, at):
        here = slice(at, at + value.shape[1])
        for j in range(value.shape[0] // cut):
            out_ref[j % 2, j // 2, :, here] = value[j * cut : (j + 1) * cut]
        here = pl.ds(at, value.shape[1])
        leaving.append(bring(out_ref.at[1 - core, :, :, here], give_far.at[:, :, here]))
        leaving.append(bring(out_ref.at[core, :, :, here], keep_far.at[:, :, here]))

    def turned(narrow, wide):
        return jnp.transpose(dot(narrow, wide, FIRST).astype(bf16))

    wait_all(second)
    every = normed[...].reshape(-1, normed.shape[2])
    store(turned(dv[...].reshape(-1, own), every), 2 * own)
    wait_all(third)
    store(turned(dk[...].reshape(-1, own), every), own)
    wait_all(fourth)
    queries = normed[:, 2 * rows :, :].reshape(-1, normed.shape[2])
    store(turned(pieces[:, :, :own].reshape(-1, own), queries), 0)
    wait_all(leaving)


def heads_gradient(place, normed, pieces, dk, dv, cut, after):
    slots, key_rows, own = dk.shape
    rows = pieces[0].shape[0]
    width = normed[0].shape[1]
    half = (width // cut // 2, cut, 3 * own)
    return call(
        functools.partial(heads_kernel, slots),
        "heads_gradient",
        [place] + [(x,) for x in (*pieces, *normed, dk, dv)],
        [(shape_of(half),)] * 2,
        scratch=[
            pltpu.VMEM((2, *half), bf16),
            pltpu.VMEM((slots, *pieces[0].shape), bf16),
            pltpu.VMEM((slots, key_rows, width), bf16),
            pltpu.VMEM((slots, key_rows, own), bf16),
            pltpu.VMEM((slots, key_rows, own), bf16),
        ],
        copies=2 * slots + 8,
        after=after,
        grant=36,
        cost_us=0.1,
    )


def other_kernel(slots, place_ref, block_ref, att_far, branch_far, *refs):
    mem_far = refs[:slots]
    comp_far = refs[slots : 2 * slots]
    keep_far, give_far, out_ref, att, branch, mem, comp, apart, rows_ref, sems = refs[2 * slots :]
    core = lax.rem(place_ref[0], 2)
    _, chips, cut, _ = out_ref.shape
    bring = Copies(sems)
    first = [bring(att_far, att), bring(branch_far, branch)]
    rows, width = att.shape
    pairs = comp.shape[1]
    second = []
    for slot in range(slots):
        second.append(bring(mem_far[slot], mem.at[pl.ds(slot * rows, rows)]))
        second.append(bring(comp_far[slot], comp.at[slot]))
    wait_all(first)
    for i in range(chips):
        at = slice(2 * i * cut, 2 * (i + 1) * cut)
        value = dot(att[:, at], branch[...], FIRST).astype(bf16)
        for j in range(2):
            out_ref[j, i, :, :width] = value[j * cut : (j + 1) * cut]
    wait_all(second)
    row = lax.broadcasted_iota(jnp.int32, (rows, pairs), 0)
    column = lax.broadcasted_iota(jnp.int32, (rows, pairs), 1)
    groups = PLANE // RATE
    step = width // groups
    part = step // slots
    wide = width // 2
    for i in range(RATE):
        chosen = (row == column * RATE + i).astype(f32).astype(bf16)
        for slot in range(slots):
            apart[slot * rows : (slot + 1) * rows, i * width : (i + 1) * width] = dot(
                chosen, comp[slot]
            ).astype(bf16)
    for group in range(groups):
        rows_ref[...] = dot(mem[:, group * step : (group + 1) * step], apart[...], FIRST)
        value = rows_ref[pl.ds(pl.multiple_of(block_ref[0] * part, part), part), :].astype(bf16)
        for i in range(RATE):
            owner = i * groups + group
            for k in range(cut // part):
                first = i * width + k * wide
                out_ref[owner % 2, owner // 2, k * part : (k + 1) * part, width:] = value[
                    :, first : first + wide
                ]
    wait_all([bring(out_ref.at[1 - core], give_far), bring(out_ref.at[core], keep_far)])


def other_gradients(place, block, attended, branch, memories, comps, cut, after):
    slots = len(memories)
    rows, width = attended.shape
    pairs = comps[0].shape[0]
    half = (width // cut // 2, cut, width + width // 2)
    return call(
        functools.partial(other_kernel, slots),
        "other_gradients",
        [place, block] + [(x,) for x in (attended, branch, *memories, *comps)],
        [(shape_of(half),)] * 2,
        scratch=[
            pltpu.VMEM((2, *half), bf16),
            pltpu.VMEM((rows, width), bf16),
            pltpu.VMEM((rows, width), bf16),
            pltpu.VMEM((slots * rows, width), bf16),
            pltpu.VMEM((slots, pairs, width), bf16),
            pltpu.VMEM((slots * rows, RATE * width), bf16),
            pltpu.VMEM((width * RATE // PLANE, RATE * width), f32),
        ],
        copies=4 + 2 * slots,
        after=after,
        cost_us=0.1,
    )


def pair_add_kernel(place_ref, *refs):
    keep_far = refs[:2]
    got = refs[2:4]
    outs = refs[4:8]
    near = refs[8:10]
    total, sems = refs[10:]
    bring = Copies(sems)
    chip = place_ref[0] // 2
    order = [1, 2, 3, 0]
    coming = {j: [bring(f.at[chip ^ j], n.at[j]) for f, n in zip(keep_far, near)] for j in order}
    leaving = []
    width = near[0].shape[2]
    for j in order:
        wait_all(coming[j])
        for at, a, b in zip((slice(0, width), slice(width, None)), near, got):
            total[j, :, at] = (a[j].astype(f32) + b[chip ^ j].astype(f32)).astype(bf16)
        leaving.append(bring(total.at[j], outs[j]))
    wait_all(leaving)


def pair_add(place, qkv_keep, qkv_got, output_keep, output_got, after):
    chips, rows, width = qkv_keep.shape
    wide = output_keep.shape[2]
    return call(
        pair_add_kernel,
        "pair_add",
        [place, (qkv_keep,), (output_keep,), qkv_got, output_got],
        [(shape_of((rows, width + wide)),)] * chips,
        scratch=[
            pltpu.VMEM(qkv_keep.shape, bf16),
            pltpu.VMEM(output_keep.shape, bf16),
            pltpu.VMEM((chips, rows, width + wide), bf16),
        ],
        copies=3 * chips,
        after=after,
        cost_us=3.0,
    )


def chip_add_kernel(chips, block_ref, *refs):
    pieces = refs[:chips]
    outs = refs[chips:-2]
    compress_ref, total = refs[-2:]
    total[...] = sum(p[...].astype(f32) for p in pieces)
    blocks = len(outs)
    rows = total.shape[0] // blocks
    width = outs[0].shape[1]
    for k in range(blocks):
        outs[k][...] = total[lanes((block_ref[0] ^ k) * rows, rows), :width].astype(bf16)
    part, wide = compress_ref.shape[0], total.shape[1] - width
    for i in range(total.shape[0] // part):
        compress_ref[:, i * wide : (i + 1) * wide] = total[i * part : (i + 1) * part, width:]


def chip_add(block, blocks, pieces, width, after):
    rows, total = pieces[0].shape
    wide = 2 * (total - width)
    return call(
        functools.partial(chip_add_kernel, len(pieces)),
        "chip_add",
        [block, *pieces],
        [shape_of((rows // blocks, width))] * blocks
        + [shape_of((rows * (total - width) // wide, wide), f32)],
        scratch=[pltpu.VMEM((rows, total), f32)],
        after=after,
        cost_us=0.1,
    )


def as_row(column):
    return jnp.transpose(jnp.broadcast_to(column, (column.shape[0], HD)))[:1]


def last_heads_kernel(blocks, block_ref, *refs):
    parts = refs[:blocks]
    gain_ref = refs[blocks]
    weights_far = refs[blocks + 1 : blocks + 4]
    at_ref = refs[blocks + 4]
    outs = refs[blocks + 5 : blocks + 8]
    output_ref, norm_ref, weights, sems = refs[blocks + 8 :]
    rows, width = output_ref.shape
    own = width // blocks
    bring = Copies(sems)
    here = pl.ds(pl.multiple_of(at_ref[0] * rows, rows), rows)
    coming = [bring(far.at[here, :], weights.at[i]) for i, far in enumerate(weights_far)]
    for k in range(blocks):
        at = lanes((block_ref[0] ^ k) * own, own)
        for i in range(3):
            outs[i][:, at] = parts[k][:, i * own : (i + 1) * own].astype(f32)
    first = 3 * own
    output_ref[...] = sum(p[:, first : first + width].astype(f32) for p in parts)
    wait_all(coming)
    total = sum(weights[i].astype(f32) * outs[i][...] for i in range(3))
    norm_ref[...] = as_row(jnp.sum(total, axis=1, keepdims=True)) / gain_ref[...]


def last_heads(block, index, parts, gain, w_query, w_key, w_value, after):
    blocks = len(parts)
    rows = parts[0].shape[0]
    width = w_query.shape[0]
    return call(
        functools.partial(last_heads_kernel, blocks),
        "last_heads",
        [block, *parts, gain, (w_query,), (w_key,), (w_value,), index],
        [shape_of((rows, width), f32)] * 4 + [shape_of((1, rows), f32)],
        scratch=[pltpu.VMEM((3, rows, width), bf16)],
        copies=3,
        after=after,
        cost_us=1.8,
    )


def segment_kernel(slots, block_ref, *refs):
    pieces_far = refs[:slots]
    seg_ref, gain_ref, dmid_far = refs[slots : slots + 3]
    far = refs[slots + 3 : slots + 6]
    out_ref, weight, pieces, dmid_ref, sems = refs[slots + 6 :]
    own = pieces.shape[2] // 3
    bring = Copies(sems)
    coming = []
    for slot in range(slots):
        at = lanes(lax.rem(block_ref[0] + slot, slots) * own, own)
        bring_piece = bring(pieces_far[slot], pieces.at[slot])
        coming.append([bring(far[i].at[:, at], weight.at[slot, i]) for i in range(3)])
        coming[-1].append(bring_piece)
    middle = bring(dmid_far, dmid_ref)
    total = None
    for slot in range(slots):
        wait_all(coming[slot])
        for i in range(3):
            part = dot(pieces[slot, :, i * own : (i + 1) * own], weight[slot, i], LAST)
            total = part if total is None else total + part
    unit, scale = standardized(seg_ref[...].astype(f32))
    middle.wait()
    out_ref[...] = (
        dmid_ref[...] + norm_input_gradient(total, gain_ref[...], unit, scale)
    ).astype(bf16)


def segment_gradient(block, pieces, w_query, w_key, w_value, segment, gain, d_middle, after):
    slots = len(pieces)
    rows, width = segment.shape
    return call(
        functools.partial(segment_kernel, slots),
        "segment_gradient",
        [block]
        + [(x,) for x in pieces]
        + [segment, gain, (d_middle,), (w_query,), (w_key,), (w_value,)],
        [shape_of((rows, width))],
        scratch=[
            pltpu.VMEM((slots, 3, width, width // slots), bf16),
            pltpu.VMEM((slots, *pieces[0].shape), bf16),
            pltpu.VMEM((rows, width), f32),
        ],
        copies=4 * slots + 1,
        after=after,
        cost_us=0.1,
    )[0]


def plane_kernel(blocks, block_ref, *refs):
    chips = PLANE // 2
    left_far = refs[: 2 * PLANE]
    right_far = refs[2 * PLANE : 2 * PLANE + chips]
    out_far, first_r, first_e, out_ref, left, right, sems = refs[2 * PLANE + chips :]
    rows = left_far[0].shape[0]
    bring = Copies(sems)
    coming = [[], []]
    for i in range(2):
        for chip in range(chips):
            at = pl.ds(2 * chip * rows, 2 * rows)
            coming[i].append(bring(right_far[chip].at[i], right.at[i, at]))
        for j in range(PLANE):
            at = pl.ds(j * rows, rows)
            coming[i].append(bring(left_far[i * PLANE + j], left.at[i, at]))
    cut = out_ref.shape[3]
    width = left.shape[2]
    step = width // 4
    leaving = []
    for i in range(2):
        wait_all(coming[i])
        for at in range(0, width, step):
            value = dot(left[i, :, at : at + step], right[i], FIRST).astype(bf16)
            for part in range(step // cut):
                j = at // cut + part
                out_ref[j % blocks, i, j // blocks] = value[part * cut : (part + 1) * cut]
    leaving.append(bring(out_ref, out_far))
    start = lax.rem(block_ref[0] + blocks - 1, blocks)
    first_r[...] = out_ref[start, 0]
    first_e[...] = out_ref[start, 1]
    wait_all(leaving)


def plane_gradients(block, cots, nfs, both, blocks, cut, after):
    rows, width = cots[0].shape
    _, _, tile = both[0].shape
    out = (blocks, 2, width // (blocks * cut), cut, tile)
    return call(
        functools.partial(plane_kernel, blocks),
        "plane_gradients",
        [block] + [(x,) for x in (*cots, *nfs[:-1])] + nfs[-1:] + [(x,) for x in both],
        [(shape_of(out),), shape_of(out[2:]), shape_of(out[2:])],
        scratch=[
            pltpu.VMEM(out, bf16),
            pltpu.VMEM((2, PLANE * rows, width), bf16),
            pltpu.VMEM((2, PLANE * rows, tile), bf16),
        ],
        copies=2 * PLANE + PLANE + 1,
        after=after,
        cost_us=80.0,
    )


def ring_kernel(which, k, blocks, block_ref, moved_ref, part_far, out_ref, part_ref, sems):
    bring = Copies(sems)
    piece = lax.rem(block_ref[0] + 2 * blocks - k, blocks)
    bring(part_far.at[piece, which], part_ref).wait()
    out_ref[...] = (moved_ref[...].astype(f32) + part_ref[...].astype(f32)).astype(bf16)


def ring_add(block, which, k, moved, part, after):
    blocks = part.shape[0]
    return call(
        functools.partial(ring_kernel, which, k, blocks),
        "ring_add",
        [block, moved, (part,)],
        [shape_of(moved.shape)],
        scratch=[pltpu.VMEM(moved.shape, bf16)],
        copies=1,
        after=after,
        cost_us=0.1,
    )[0]


def spread_kernel(place_ref, block_ref, r_moved, e_moved, part_far, *refs):
    outs = refs[:2]
    part_ref, sems = refs[2:]
    bring = Copies(sems)
    bring(part_far.at[block_ref[0]], part_ref).wait()
    for j in range(PLANE):
        at = place_ref[0] ^ j
        for i, moved in enumerate((r_moved, e_moved)):
            total = part_ref[i, at].astype(f32) + moved[at].astype(f32)
            outs[j % 2][j // 2, i] = total.astype(bf16)


def spread(place, block, moved, part, after):
    count, rows, tile = moved[0].shape
    return call(
        spread_kernel,
        "spread",
        [place, block, *moved, (part,)],
        [shape_of((count // 2, 2, rows, tile))] * 2,
        scratch=[pltpu.VMEM((2, count, rows, tile), bf16)],
        copies=1,
        after=after,
        cost_us=0.1,
    )


def join_kernel(keep_ref, got_ref, *outs):
    for j, out in enumerate(outs):
        out[0] = keep_ref[j + 1]
        out[1] = got_ref[j + 1]


def join(keep, got):
    chips = keep.shape[0]
    return call(
        join_kernel,
        "join",
        [keep, got],
        [shape_of((2, *keep.shape[1:]))] * (chips - 1),
        cost_us=0.1,
    )


def last_wide_kernel(place_ref, index_ref, *refs):
    chips = PLANE // 2
    keep_ref, got_ref, *moved = refs[: chips + 1]
    gain_ref, weight_far, expand_ref, reduce_ref, gain_out, weight, sems = refs[chips + 1 :]
    rows = weight.shape[0]
    tile = keep_ref.shape[3]
    parts = [keep_ref.at[0], got_ref.at[0]]
    for ref in moved:
        parts += [ref.at[0], ref.at[1]]
    bring = Copies(sems)
    coming = bring(
        weight_far.at[pl.ds(pl.multiple_of(index_ref[0] * rows, rows), rows), :], weight
    )
    for j in range(PLANE):
        at = lanes((place_ref[0] ^ j) * tile, tile)
        reduce_ref[:, at] = parts[j][0].astype(f32)
        expand_ref[:, at] = parts[j][1].astype(f32)
    coming.wait()
    total = jnp.sum(weight[...].astype(f32) * expand_ref[...], axis=1, keepdims=True)
    gain_out[...] = as_row(total) / gain_ref[...]


def last_wide(place, index, parts, gain, w_expand, after):
    _, _, rows, tile = parts[0].shape
    hidden = PLANE * tile
    return call(
        last_wide_kernel,
        "last_wide",
        [place, index, *parts, gain, (w_expand,)],
        [shape_of((rows, hidden), f32)] * 2 + [shape_of((1, rows), f32)],
        scratch=[pltpu.VMEM((rows, hidden), bf16)],
        copies=1,
        after=after,
        cost_us=2.0,
    )


def on_plane(
    segment,
    memory,
    compressed,
    document_labels,
    memory_filled_count,
    norm_gain,
    w_query,
    w_key,
    w_value,
    w_output,
    ffn_gain,
    w_expand,
    w_reduce,
    w_compress,
    result_cotangent,
    compressed_cotangent,
):
    _, rows, width = segment.shape
    blocks = lax.axis_size("blk")
    block = lax.axis_index("blk")
    place = lax.axis_index("stream")
    own = width // blocks
    seg_len = rows * blocks
    part_rows = width // (PLANE * blocks)
    chips = PLANE // 2
    segment, memory, compressed = segment[0], memory[0], compressed[0]
    cotangent, comp_cotangent = result_cotangent[0], compressed_cotangent[0]
    labels, filled = document_labels[0], memory_filled_count[0]
    gain = norm_gain.reshape(1, width)
    gain_ffn = ffn_gain.reshape(1, width)
    block_ref = block.astype(jnp.int32).reshape(1)
    place_ref = place.astype(jnp.int32).reshape(1)
    index = place * blocks + block
    index_ref = index.astype(jnp.int32).reshape(1)

    def along_blk(x, shift):
        return lax.ppermute(x, "blk", [(i, (i + shift) % blocks) for i in range(blocks)])

    def along_blk_flip(x, flip):
        return lax.ppermute(x, "blk", [(i, i ^ flip) for i in range(blocks)])

    def in_plane(x, flip):
        return lax.ppermute(x, "stream", [(i, i ^ flip) for i in range(PLANE)])

    owners = lax.rem(block - jnp.arange(blocks, dtype=jnp.int32) + blocks, blocks)
    by_owner = labels.reshape(3, blocks, rows).transpose(1, 0, 2)
    kdoc = by_owner[owners].reshape(blocks, 3 * rows)
    position = owners[:, None] * rows + jnp.arange(rows, dtype=jnp.int32)[None]
    first_filled = 2 * seg_len - filled
    kpos = jnp.concatenate(
        [
            jnp.where(position >= first_filled, -1, hidden_slot),
            jnp.where(position + seg_len >= first_filled, -1, hidden_slot),
            position,
        ],
        axis=1,
    ).astype(jnp.int32)
    qdoc = kdoc[:, 2 * rows :].reshape(blocks * rows, 1)
    qpos = position.reshape(blocks * rows, 1).astype(jnp.int32)
    marks = (qdoc, qpos, kdoc, kpos)

    def hop(arrays, after):
        arrays = [gate([x], after)[0] for x in arrays]
        return arrays, [along_blk(x, 1) for x in arrays]

    weights = (w_query, w_key, w_value)
    raw = [compressed, memory, segment]
    arriving = [along_blk(x, 1) for x in raw]
    pairs = memory.reshape(rows // RATE, RATE * width)
    projected = [project(block_ref, raw, gain, *weights, width, [])]
    query = projected[0][1]
    memories = [memory]
    raw, arriving = hop(arriving, [query])
    memories.append(raw[1])
    projected.append(raw)
    cots = [cotangent, in_plane(cotangent, 1)]
    for j in range(1, chips):
        cots.append(in_plane(cotangent, 2 * j))
        cots.append(in_plane(cots[-1], 1))
    projected[1] = project(block_ref, projected[1], gain, *weights, own, [])
    later = []
    for k in range(2, blocks - 1):
        raw, arriving = hop(arriving, [projected[1][1]])
        memories.append(raw[1])
        later.append(raw)
    memories.append(arriving[1])
    projected += [project(block_ref, rows3, gain, *weights, own, raw) for rows3 in later]
    keys, values = ([p[i] for p in projected] for i in (2, 3))
    partial = attend(query, keys, values, marks, [])
    *last, attended, normed_ffn_far, middle, normed_ffn = finish(
        blocks - 1,
        block_ref,
        arriving,
        gain,
        *weights,
        own,
        query,
        partial,
        marks,
        segment,
        w_output,
        gain_ffn,
        cots[2:],
    )
    projected.append(last)
    normed, queries, keys, values = ([p[i] for p in projected] for i in range(4))

    nfs = [normed_ffn, in_plane(normed_ffn, 1)]
    for j in range(1, chips - 1):
        nfs.append(in_plane(normed_ffn, 2 * j))
        nfs.append(in_plane(nfs[-1], 1))
    *both, res, dn, send = feed(
        place_ref,
        normed_ffn,
        nfs[1],
        cotangent,
        cots[1],
        w_expand,
        w_reduce,
        [],
    )
    sent = in_plane(send, 1)
    both = [both[0], in_plane(both[1], 2), in_plane(both[2], 4), both[3]]
    result, d_middle, d_branch, *d_attended = leave(
        block_ref,
        blocks,
        res,
        dn,
        sent,
        middle,
        cotangent,
        gain_ffn,
        w_output,
        nfs[3:6],
    )
    grads = [d_attended[0]] + [along_blk(d_attended[k], k) for k in range(1, blocks)]
    (diagonal,) = gate([normed_ffn_far], grads[1:])
    nfs.append(in_plane(diagonal, 6))
    comps = [comp_cotangent] + [along_blk(comp_cotangent, k) for k in range(1, blocks)]
    *pieces, dk, dv = attend_back(
        block_ref, queries, grads, keys, values, marks, both[1:3]
    )
    arrived = [pieces[0]] + [along_blk(pieces[k], -k) for k in range(1, blocks)]
    nfs[6], both[3] = gate([nfs[6], both[3]], [(pieces[0],)])
    both[3] = in_plane(both[3], 6)
    nfs.append(in_plane(nfs[6], 1))
    qkv_keep, qkv_give = heads_gradient(
        place_ref, normed, pieces, dk, dv, blocks * part_rows, [(nfs[6],), *comps[1:]]
    )
    other_keep, other_give = other_gradients(
        place_ref,
        block_ref,
        attended,
        d_branch,
        memories,
        comps,
        blocks * part_rows,
        [(qkv_keep,)],
    )
    qkv_give, other_give = gate([qkv_give, other_give], [(other_keep,)])
    part, *moved = plane_gradients(
        block_ref, cots, nfs, both, blocks, part_rows, [(other_keep,), *arrived[1:]]
    )
    four = pair_add(
        place_ref, qkv_keep, in_plane(qkv_give, 1), other_keep, in_plane(other_give, 1), moved
    )
    before = (four[0],)
    for k in range(2, blocks):
        for i in range(2):
            moved[i] = ring_add(block_ref, i, k, along_blk(moved[i], 1), part, [before])
            before = moved[i]
        if k == 2:
            new_compressed = compress(pairs, w_compress, [before])
            before = (new_compressed,)
    four = [four[0]] + [in_plane(four[j], 2 * j) for j in range(1, chips)]
    moved = [along_blk(x, 1) for x in moved]
    grad_segment = segment_gradient(
        block_ref, arrived, *weights, segment, gain, d_middle, [before]
    )
    *parts, grad_compress = chip_add(
        block_ref, blocks, four, 3 * own + width, [(grad_segment,), moved[0]]
    )
    parts = [parts[0]] + [along_blk_flip(parts[k], k) for k in range(1, blocks)]
    wide_keep, wide_give = spread(place_ref, block_ref, moved, part, [parts[0]])
    wide_got = in_plane(wide_give, 1)
    wide = join(wide_keep, wide_got)
    wide = [in_plane(wide[j - 1], 2 * j) for j in range(1, chips)]

    def mine(x):
        return lax.dynamic_slice_in_dim(x, index * part_rows, part_rows, 0).reshape(1, -1)

    grad_query, grad_key, grad_value, grad_output, grad_norm_gain = last_heads(
        block_ref, index_ref, parts, mine(norm_gain), *weights, [grad_segment]
    )
    grad_expand, reduce_turned, grad_ffn_gain = last_wide(
        place_ref, index_ref, [wide_keep, wide_got, *wide], mine(ffn_gain), w_expand, [(grad_query,)]
    )
    return (
        result[None],
        new_compressed[None],
        grad_segment[None],
        grad_norm_gain.reshape(-1),
        grad_query,
        grad_key,
        grad_value,
        grad_output,
        grad_ffn_gain.reshape(-1),
        grad_expand,
        reduce_turned.T,
        grad_compress,
    )


def layer_norm(rows_in, gain):
    center = jnp.mean(rows_in, axis=-1, keepdims=True)
    offset = rows_in - center
    spread = jnp.mean(offset * offset, axis=-1, keepdims=True)
    return offset * lax.rsqrt(spread + epsilon) * gain


def exact_gelu(values_in):
    return jax.nn.gelu(values_in, approximate=False)


def on_any(
    segment,
    memory,
    compressed,
    document_labels,
    memory_filled_count,
    norm_gain,
    w_query,
    w_key,
    w_value,
    w_output,
    ffn_gain,
    w_expand,
    w_reduce,
    w_compress,
    result_cotangent,
    compressed_cotangent,
):
    streams, block_rows, model_width = segment.shape
    head_count = model_width // HD
    blocks = lax.axis_size("blk")
    my_block = lax.axis_index("blk")
    seg_len = block_rows * blocks
    key_count = 3 * seg_len
    score_scale = HD ** (-0.5)
    stacked = jnp.concatenate([compressed, memory, segment], axis=1).astype(jnp.float32)
    normed_full, norm_pull = jax.vjp(layer_norm, stacked, norm_gain)
    normed = normed_full.astype(jnp.bfloat16)
    seg_normed = normed[:, 2 * block_rows :]
    queries = jnp.einsum(
        "srd,de->sre", seg_normed, w_query, preferred_element_type=jnp.float32
    ).astype(jnp.bfloat16)
    query_heads = queries.reshape(streams, block_rows, head_count, HD)
    keys = jnp.einsum("srd,de->rse", normed, w_key, preferred_element_type=jnp.float32).astype(
        jnp.bfloat16
    )
    values = jnp.einsum("srd,de->rse", normed, w_value, preferred_element_type=jnp.float32).astype(
        jnp.bfloat16
    )
    all_keys, all_values = (
        lax.all_gather(keys, "blk", axis=0, tiled=True),
        lax.all_gather(values, "blk", axis=0, tiled=True),
    )
    key_index = jnp.arange(key_count, dtype=jnp.int32)
    key_owner = key_index // (3 * block_rows)
    within = key_index % (3 * block_rows)
    key_kind = within // block_rows
    key_pos = key_owner * block_rows + within % block_rows
    key_slot = key_kind * seg_len + key_pos
    key_docs = (
        document_labels.reshape(streams, 3, blocks, block_rows)
        .transpose(0, 2, 1, 3)
        .reshape(streams, key_count)
    )
    query_pos = my_block * block_rows + jnp.arange(block_rows, dtype=jnp.int32)
    query_docs = lax.dynamic_slice_in_dim(
        document_labels[:, 2], my_block * block_rows, block_rows, 1
    )
    in_memory = key_slot[None, :] >= 2 * seg_len - memory_filled_count[:, None]
    causal = key_pos[None, :] <= query_pos[:, None]
    visible = jnp.where((key_kind < 2)[None, None, :], in_memory[:, None, :], causal[None, :, :])
    allowed = visible & (key_docs[:, None, :] == query_docs[:, :, None])

    def scores_of(key_set):
        key_view = key_set.reshape(key_count, streams, head_count, HD)
        raw_scores = (
            jnp.einsum("sqhd,kshd->shqk", query_heads, key_view, preferred_element_type=jnp.float32)
            * score_scale
        )
        return jnp.where(allowed[:, None], raw_scores, masked_score)

    scores = scores_of(all_keys)
    row_top = jnp.max(scores, axis=-1, keepdims=True)
    weights = jnp.exp(scores - row_top)
    row_total = jnp.sum(weights, axis=-1, keepdims=True)
    probs = (weights / row_total).astype(jnp.bfloat16)
    log_total = row_top + jnp.log(row_total)
    value_heads = all_values.reshape(key_count, streams, head_count, HD)
    attended = jnp.einsum("shqk,kshd->sqhd", probs, value_heads, preferred_element_type=jnp.float32)
    attended = attended.reshape(streams, block_rows, model_width).astype(jnp.bfloat16)
    middle = segment.astype(jnp.float32) + jnp.einsum(
        "sre,ed->srd", attended, w_output, preferred_element_type=jnp.float32
    )
    normed_ffn_full, ffn_pull = jax.vjp(layer_norm, middle, ffn_gain)
    normed_ffn = normed_ffn_full.astype(jnp.bfloat16)
    hidden = jnp.einsum("srd,df->srf", normed_ffn, w_expand, preferred_element_type=jnp.float32)
    activated_full, gelu_pull = jax.vjp(exact_gelu, hidden)
    activated = activated_full.astype(jnp.bfloat16)
    result = (
        middle + jnp.einsum("srf,fd->srd", activated, w_reduce, preferred_element_type=jnp.float32)
    ).astype(jnp.bfloat16)
    mem_pairs = memory.reshape(streams, block_rows // RATE, RATE * model_width)
    new_compressed = jnp.einsum(
        "srp,pd->srd", mem_pairs, w_compress, preferred_element_type=jnp.float32
    ).astype(jnp.bfloat16)
    reduce_turned = jnp.einsum(
        "srd,srf->df", result_cotangent, activated, preferred_element_type=jnp.float32
    )
    d_activated = jnp.einsum(
        "srd,fd->srf", result_cotangent, w_reduce, preferred_element_type=jnp.float32
    )
    d_hidden = gelu_pull(d_activated)[0].astype(jnp.bfloat16)
    grad_expand = jnp.einsum(
        "srd,srf->df", normed_ffn, d_hidden, preferred_element_type=jnp.float32
    )
    d_normed_ffn = jnp.einsum("srf,df->srd", d_hidden, w_expand, preferred_element_type=jnp.float32)
    d_middle_norm, grad_ffn_gain = ffn_pull(d_normed_ffn)
    d_middle = result_cotangent.astype(jnp.float32) + d_middle_norm
    d_branch = d_middle.astype(jnp.bfloat16)
    grad_output = jnp.einsum("sre,srd->ed", attended, d_branch, preferred_element_type=jnp.float32)
    d_attended = jnp.einsum(
        "srd,ed->sre", d_branch, w_output, preferred_element_type=jnp.float32
    ).astype(jnp.bfloat16)
    d_attended = d_attended.reshape(streams, block_rows, head_count, HD)
    key_heads = all_keys.reshape(key_count, streams, head_count, HD)
    probs_full = jnp.exp(scores_of(all_keys) - log_total)
    probs_low = probs_full.astype(jnp.bfloat16)
    d_probs = jnp.einsum(
        "sqhd,kshd->shqk", d_attended, value_heads, preferred_element_type=jnp.float32
    )
    row_delta = jnp.sum(probs_full * d_probs, axis=-1, keepdims=True)
    d_scores = (probs_full * (d_probs - row_delta)).astype(jnp.bfloat16)
    d_queries = (
        jnp.einsum("shqk,kshd->sqhd", d_scores, key_heads, preferred_element_type=jnp.float32)
        * score_scale
    )
    d_queries = d_queries.astype(jnp.bfloat16).reshape(streams, block_rows, model_width)
    count = 3 * block_rows * lax.axis_size("blk")
    key_part = (
        jnp.einsum("shqk,sqhd->kshd", d_scores, query_heads, preferred_element_type=jnp.float32)
        * score_scale
    )
    value_part = jnp.einsum(
        "shqk,sqhd->kshd", probs_low, d_attended, preferred_element_type=jnp.float32
    )
    key_grads = lax.psum_scatter(
        jnp.stack(
            [
                key_part.reshape(count, streams, model_width),
                value_part.reshape(count, streams, model_width),
            ],
            axis=1,
        ).astype(jnp.bfloat16),
        "blk",
        scatter_dimension=0,
        tiled=True,
    ).astype(jnp.float32)
    d_keys = key_grads[:, 0].astype(jnp.bfloat16)
    d_values = key_grads[:, 1].astype(jnp.bfloat16)
    grad_query = jnp.einsum(
        "srd,sre->de", seg_normed, d_queries, preferred_element_type=jnp.float32
    )
    grad_key = jnp.einsum("srd,rse->de", normed, d_keys, preferred_element_type=jnp.float32)
    grad_value = jnp.einsum("srd,rse->de", normed, d_values, preferred_element_type=jnp.float32)
    d_normed = jnp.einsum("rse,de->srd", d_keys, w_key, preferred_element_type=jnp.float32)
    d_normed = d_normed + jnp.einsum(
        "rse,de->srd", d_values, w_value, preferred_element_type=jnp.float32
    )
    d_seg_normed = jnp.einsum("sre,de->srd", d_queries, w_query, preferred_element_type=jnp.float32)
    d_normed = d_normed + jnp.pad(d_seg_normed, ((0, 0), (2 * block_rows, 0), (0, 0)))
    d_stacked, grad_norm_gain = norm_pull(d_normed)
    grad_segment = (d_middle + d_stacked[:, 2 * block_rows :]).astype(jnp.bfloat16)
    grad_compress = jnp.einsum(
        "srp,srd->pd", mem_pairs, compressed_cotangent, preferred_element_type=jnp.float32
    )
    weight_grads = (
        grad_norm_gain,
        grad_query,
        grad_key,
        grad_value,
        grad_output,
        grad_ffn_gain,
        grad_expand,
        reduce_turned,
        grad_compress,
    )
    summed = (
        lax.psum_scatter(weight_grads[0], ("stream", "blk"), scatter_dimension=0, tiled=True),
        lax.psum_scatter(weight_grads[1], ("stream", "blk"), scatter_dimension=0, tiled=True),
        lax.psum_scatter(weight_grads[2], ("stream", "blk"), scatter_dimension=0, tiled=True),
        lax.psum_scatter(weight_grads[3], ("stream", "blk"), scatter_dimension=0, tiled=True),
        lax.psum_scatter(weight_grads[4], ("stream", "blk"), scatter_dimension=0, tiled=True),
        lax.psum_scatter(weight_grads[5], ("stream", "blk"), scatter_dimension=0, tiled=True),
        lax.psum_scatter(weight_grads[6], ("stream", "blk"), scatter_dimension=0, tiled=True),
        lax.psum_scatter(weight_grads[7], ("stream", "blk"), scatter_dimension=0, tiled=True),
        lax.psum_scatter(weight_grads[8], ("stream", "blk"), scatter_dimension=0, tiled=True),
    )
    grad_reduce = summed[7].T
    return (
        result,
        new_compressed,
        grad_segment,
        summed[0],
        summed[1],
        summed[2],
        summed[3],
        summed[4],
        summed[5],
        summed[6],
        grad_reduce,
        summed[8],
    )


def solution(mesh):
    tokens = P("stream", "blk", None)
    both = ("stream", "blk")
    in_specs = (
        (tokens,) * 3
        + (P("stream", None, None), P("stream"))
        + (P(),) * 9
        + (tokens,) * 2
    )
    out_specs = (
        (tokens,) * 3
        + (P(both),)
        + (P(both, None),) * 4
        + (P(both), P(both, None), P(None, both), P(both, None))
    )
    one_plane = mesh.shape["stream"] == PLANE
    return jax.shard_map(
        on_plane if one_plane else on_any, mesh=mesh, in_specs=in_specs, out_specs=out_specs, check_vma=False
    )
```
